32 devices in a mesh: grp: 4 (over y, core), dev: 8 (over z, x).
Axes of the slice: x: 2, y: 2, z: 4, core: 2. Of those that a mesh axis runs over, the one named last changes fastest.
Arguments:
- velocity: float32 [3, 512, 8192], P(None, None, ('grp', 'dev'))
- density: float32 [512, 8192], P(None, ('grp', 'dev')), may hold values from 0.1 to 3
- inverse_density: float32 [512, 8192], P(None, ('grp', 'dev')), may hold values from 0.25 to 4
- neighbours: int32 [6, 8192], P(None, ('grp', 'dev')), may hold values from -1 to 8191, as said below
- leaf_layer: int32 [8192], P(('grp', 'dev')), may hold values from 0 to 31, as said below
- leaf_tile: int32 [8192, 1], P(('grp', 'dev')), may hold values from 0 to 7; in each aligned block of 256 rows (0 to 255, 256 to 511, ...) at most 64 rows name the same one
- leaf_block: int32 [8192], P(('grp', 'dev')), may hold values from 0 to 255
- samples: int32 [8], replicated, may hold values from 1 to 32
Outputs:
- projected_velocity: float32 [3, 512, 8192], P(None, None, ('grp', 'dev'))
- rendered: float32 [8, 16384], P('dev', 'grp')
The draws below stay inside these ranges and needn't reach their ends.
Inputs may be any that keep to these rules, and one draw needn't show every extreme that they name: `neighbours`: A neighbour in direction -x or +x lies on the same device or on the device with dev index one lower or higher in the same group; one in -y or +y on the same device or on the device with the same dev index in the group one lower or higher; one in -z or +z on the same device. The relation is symmetric: leaf m is beside l in direction f exactly when l is beside m in the opposite direction. A device's leaves are distinct places of a brick of 8 x 8 x 8 leaf places. `leaf_layer`: the layer of a leaf of group g lies in g * 8 to g * 8 + 7. `leaf_tile`: among the 256 leaves of one device, no tile is named by more than 64, a bound that some block reaches.
All inputs are finite; a program needn't handle non-finite values.
Results may differ from the reference program's by a relative error of at most 0.0001.
Values sent between devices are 32-bit elements; how exact they have to be, the bound alone decides.
No kernel may reach another device: no remote copies, remote signals or barrier semaphores. Data moves between devices by JAX's collectives and lax.ppermute only.
A program may use at most 64 MiB of HBM per device.

```python
import math
import jax
import jax.numpy as jnp
import numpy as np

LEAF_DEV = 256
BX = 8
BY = 8
BZ = 8
LEAF_VOX = 512
ITERS = 3
BLOCKS = 256
TILES = 8
CAP = 64
LEAVES = 8192
NLAYERS = 32
N_GRP = 4
N_DEV = 8


def leaf_geometry(key):
    device_count = N_GRP * N_DEV
    places = BX * BY * BZ
    key_list = jax.random.split(key, device_count)
    shuffled = jax.vmap(lambda sub_key: jax.random.permutation(sub_key, places))(key_list)
    chosen = jnp.sort(shuffled[:, :LEAF_DEV], axis=1).astype(jnp.int32)
    device_ids = jnp.broadcast_to(jnp.arange(device_count, dtype=jnp.int32)[:, None], chosen.shape)
    slot_ids = jnp.broadcast_to(jnp.arange(LEAF_DEV, dtype=jnp.int32)[None, :], chosen.shape)
    slot_map = jnp.full((device_count, places), -1, jnp.int32).at[device_ids, chosen].set(slot_ids)
    leaf_x = chosen // (BY * BZ)
    leaf_y = chosen // BZ % BY
    leaf_z = chosen % BZ
    group_of = device_ids // N_DEV
    member_of = device_ids % N_DEV
    neighbour_rows = []
    for axis_id, offset in ((0, -1), (0, 1), (1, -1), (1, 1), (2, -1), (2, 1)):
        next_x = leaf_x + offset * int(axis_id == 0)
        next_y = leaf_y + offset * int(axis_id == 1)
        next_z = leaf_z + offset * int(axis_id == 2)
        member_next = member_of + jnp.where(next_x < 0, -1, 0) + jnp.where(next_x >= BX, 1, 0)
        group_next = group_of + jnp.where(next_y < 0, -1, 0) + jnp.where(next_y >= BY, 1, 0)
        inside = (member_next >= 0) & (member_next < N_DEV) & (group_next >= 0) & (group_next < N_GRP)
        inside = inside & (next_z >= 0) & (next_z < BZ)
        target = jnp.clip(group_next, 0, N_GRP - 1) * N_DEV + jnp.clip(member_next, 0, N_DEV - 1)
        place = next_x % BX * (BY * BZ) + next_y % BY * BZ + jnp.clip(next_z, 0, BZ - 1)
        found = slot_map[target, place]
        linked = inside & (found >= 0)
        neighbour_rows.append(jnp.where(linked, target * LEAF_DEV + found, -1).reshape(-1).astype(jnp.int32))
    layers = (group_of * BY + leaf_y).reshape(-1).astype(jnp.int32)
    return (jnp.stack(neighbour_rows), layers)


def draw_neighbours(key, part):
    neighbour_table, layer_list = leaf_geometry(key)
    return neighbour_table


def draw_leaf_layer(key, part):
    neighbour_table, layer_list = leaf_geometry(key)
    return layer_list


def draw_velocity(key, part):
    key = jax.random.fold_in(key, 7)
    column_count = LEAF_DEV * N_GRP * N_DEV
    device_rank = (jnp.arange(column_count) // LEAF_DEV).astype(jnp.float32)
    ramp_share = device_rank / max(N_GRP * N_DEV - 1, 1)
    leaf_scale = 10.0 ** jax.random.uniform(jax.random.fold_in(key, 1), (column_count,), jnp.float32)
    noise_part = jax.random.normal(jax.random.fold_in(key, 2), (3, LEAF_VOX, column_count), jnp.float32)
    return noise_part * 0.15 * leaf_scale * 3.0 ** ramp_share


def set_ends(result, stream_key, least, largest):
    shape = result.shape
    spot = [jax.random.randint(jax.random.fold_in(stream_key, axis), (), 0, shape[axis]) for axis in range(len(shape))]
    result = result.at[tuple(spot)].set(least)
    longest = shape.index(max(shape))
    spot[longest] = (spot[longest] + 1) % shape[longest]
    return result.at[tuple(spot)].set(largest)


def levels(stream_key, shape, pieces, least, largest):
    level, own = 1.0, jax.random.fold_in(stream_key, 6)
    for position, shards_of in pieces:
        steps = jnp.exp(jax.random.uniform(jax.random.fold_in(own, position), (shards_of,), jnp.float32, least / len(pieces), largest / len(pieces)))
        level = level * jnp.repeat(steps, shape[position] // shards_of).reshape([-1 if axis == position else 1 for axis in range(len(shape))])
    return level


def assign_block(key, own, number, rows, number_of, top, bound, skew):
    sequence = jax.random.permutation(key, number_of)
    crowded, ordinary = shares(number_of, rows * top, bound, skew, True), shares(number_of, rows * top, bound, skew, False)
    places = jnp.arange(number_of)

    def named(sizes, rotation):
        used = int((sizes > 0).sum())
        fixed = max(1, used // 4)
        passed = fixed + (places - fixed + rotation * (used - fixed)) % max(1, number_of - fixed)
        return jnp.zeros((number_of,), jnp.int32).at[sequence[jnp.where(places < fixed, places, passed)]].set(jnp.asarray(sizes, jnp.int32))

    sizes = jnp.where(number % 4 == 0, named(crowded, number // 4), named(ordinary, number - number // 4 - 1))
    mixed = jax.random.permutation(jax.random.fold_in(own, 3), number_of)
    source_of, taker = mixed[0:number_of // 2 * 2:2], mixed[1:number_of // 2 * 2:2]
    slack = jnp.minimum(sizes[source_of] - 1, bound - sizes[taker]) // 2
    slack = jnp.where((source_of == sequence[0]) | (taker == sequence[0]) | (sizes[taker] == 0), 0, jnp.maximum(slack, 0))
    passed = jax.random.randint(jax.random.fold_in(own, 4), (number_of // 2,), 0, 1 << 20) % (slack + 1)
    sizes = sizes.at[source_of].add(-passed).at[taker].add(passed)
    members = jnp.searchsorted(jnp.cumsum(sizes), jnp.arange(rows * top), side="right").astype(jnp.int32)
    table = members.reshape(top, rows).T
    table = table[jax.random.permutation(jax.random.fold_in(own, 1), rows)]
    rotation = jax.random.randint(jax.random.fold_in(own, 2), (rows, 1), 0, top)
    return jnp.take_along_axis(table, (jnp.arange(top)[None, :] + rotation) % top, axis=1)


def shares(count, total, bound, skew, full):
    loads = [(1 << 20) // math.isqrt(grade ** skew) + 1 for grade in range(1, count + 1)]
    largest = bound if full else min(bound, max(-(-total // count), total * loads[0] // sum(loads)))
    least = 1 if total - largest >= count - 1 else 0
    given, rest = [largest] + [least] * (count - 1), total - largest - least * (count - 1)
    while rest > 0:
        movable = [i for i in range(1, count) if given[i] < largest] or [i for i in range(1, count) if given[i] < bound]
        pool, left = sum([loads[i] for i in movable]), rest
        for i in movable:
            extra = min(bound - given[i], max(1, left * loads[i] // pool), rest)
            given[i] = given[i] + extra
            rest = rest - extra
    return np.array(given)


def setup_inputs(seed: int = 0) -> dict:
    streams_of = jax.random.split(jax.random.key(seed), 9)
    velocity = draw_velocity(jax.random.fold_in(streams_of[8], 71), 0)
    density = jnp.clip(jnp.exp(math.log(3.0) - 3.4011974 * jax.random.uniform(streams_of[1], (LEAF_VOX, LEAVES), jnp.float32) ** levels(streams_of[1], (LEAF_VOX, LEAVES), ((1, 32),), -0.2, 0.2)), 0.1, 3.0)
    inverse_density = jnp.clip(jnp.exp(math.log(4.0) - 2.7725887 * jax.random.uniform(streams_of[2], (LEAF_VOX, LEAVES), jnp.float32) ** levels(streams_of[2], (LEAF_VOX, LEAVES), ((1, 32),), -0.2, 0.2)), 0.25, 4.0)
    neighbours = draw_neighbours(jax.random.fold_in(streams_of[8], 71), 0)
    leaf_layer = draw_leaf_layer(jax.random.fold_in(streams_of[8], 71), 0)
    leaf_tile_keys = jax.random.split(jax.random.fold_in(streams_of[5], 1), LEAVES // LEAF_DEV)
    leaf_tile_turns = jax.random.permutation(jax.random.fold_in(streams_of[5], 3), LEAVES // LEAF_DEV)
    leaf_tile = jax.vmap(lambda own, number: assign_block(jax.random.fold_in(streams_of[5], 2), own, number, LEAF_DEV, TILES, 1, CAP, 2))(leaf_tile_keys, leaf_tile_turns).reshape((LEAVES, 1))
    leaf_block = set_ends(jax.random.randint(streams_of[6], (LEAVES,), 0, BLOCKS), jax.random.fold_in(streams_of[6], 1), 0, BLOCKS - 1).astype(jnp.int32)
    samples = set_ends(jax.random.randint(streams_of[7], (TILES,), 1, NLAYERS + 1), jax.random.fold_in(streams_of[7], 1), 1, NLAYERS).astype(jnp.int32)
    return dict(velocity=velocity, density=density, inverse_density=inverse_density, neighbours=neighbours, leaf_layer=leaf_layer, leaf_tile=leaf_tile, leaf_block=leaf_block, samples=samples)


advect_step = 0.2
ray_step = 0.03


def neighbour_faces(first, second, third, neighbours):
    leaf_count = first.shape[-1]
    safe_index = jnp.maximum(neighbours, 0)
    present = neighbours >= 0
    tables = [first[7].reshape(64, leaf_count), first[0].reshape(64, leaf_count),
              second[:, 7].reshape(64, leaf_count), second[:, 0].reshape(64, leaf_count),
              third[:, :, 7].reshape(64, leaf_count), third[:, :, 0].reshape(64, leaf_count)]
    return [jnp.where(present[face_id][None, :], jnp.take(tables[face_id], safe_index[face_id], axis=1), 0.0)
            for face_id in range(6)]


def shifted(first, second, third, face_list):
    leaf_count = first.shape[-1]
    minus_x = jnp.concatenate([face_list[0].reshape(1, 8, 8, leaf_count), first[:-1]], axis=0)
    plus_x = jnp.concatenate([first[1:], face_list[1].reshape(1, 8, 8, leaf_count)], axis=0)
    minus_y = jnp.concatenate([face_list[2].reshape(8, 1, 8, leaf_count), second[:, :-1]], axis=1)
    plus_y = jnp.concatenate([second[:, 1:], face_list[3].reshape(8, 1, 8, leaf_count)], axis=1)
    minus_z = jnp.concatenate([face_list[4].reshape(8, 8, 1, leaf_count), third[:, :, :-1]], axis=2)
    plus_z = jnp.concatenate([third[:, :, 1:], face_list[5].reshape(8, 8, 1, leaf_count)], axis=2)
    return [minus_x, plus_x, minus_y, plus_y, minus_z, plus_z]


def beside_all(first, second, third, neighbours):
    return shifted(first, second, third, neighbour_faces(first, second, third, neighbours))


def reference(velocity, density, inverse_density, neighbours, leaf_layer, leaf_tile, leaf_block, samples):
    grid_shape = (8, 8, 8, LEAVES)
    inverse = inverse_density.reshape(grid_shape)
    dens_grid = density.reshape(grid_shape)
    velocity_grid = velocity.reshape((3,) + grid_shape)
    present = neighbours >= 0
    ones_grid = jnp.ones(grid_shape, jnp.float32)
    presence_faces = [jnp.broadcast_to(present[face_id][None, :].astype(jnp.float32), (64, LEAVES)) for face_id in range(6)]
    presence = shifted(ones_grid, ones_grid, ones_grid, presence_faces)
    inverse_near = beside_all(inverse, inverse, inverse, neighbours)
    coupling = [0.5 * (inverse + inverse_near[face_id]) + 0.5 * inverse * (1.0 - presence[face_id]) for face_id in range(6)]
    diagonal = coupling[0] + coupling[1] + coupling[2] + coupling[3] + coupling[4] + coupling[5]

    def operate(values):
        near_list = beside_all(values, values, values, neighbours)
        total = diagonal * values
        for face_id in range(6):
            total = total - coupling[face_id] * near_list[face_id]
        return total

    vel_near = beside_all(velocity_grid[0], velocity_grid[1], velocity_grid[2], neighbours)
    source = -0.5 * ((vel_near[1] - vel_near[0]) + (vel_near[3] - vel_near[2]) + (vel_near[5] - vel_near[4]))
    pressure = jnp.zeros(grid_shape, jnp.float32)
    residual = source
    precond = residual / diagonal
    energy = jnp.sum(residual * precond)
    direction = precond
    for iteration in range(ITERS):
        image_dir = operate(direction)
        step_size = energy / jnp.sum(direction * image_dir)
        pressure = pressure + step_size * direction
        residual = residual - step_size * image_dir
        if iteration + 1 < ITERS:
            precond = residual / diagonal
            fresh = jnp.sum(residual * precond)
            direction = precond + (fresh / energy) * direction
            energy = fresh
    press_near = beside_all(pressure, pressure, pressure, neighbours)
    gradient = jnp.stack([press_near[1] - press_near[0], press_near[3] - press_near[2], press_near[5] - press_near[4]]) * 0.5
    new_velocity = velocity_grid - inverse[None] * gradient
    flux = dens_grid[None] * new_velocity
    flux_near = beside_all(flux[0], flux[1], flux[2], neighbours)
    change = 0.5 * ((flux_near[1] - flux_near[0]) + (flux_near[3] - flux_near[2]) + (flux_near[5] - flux_near[4]))
    advected = dens_grid - advect_step * change
    column = ray_step * jnp.sum(advected, axis=1).reshape(64, LEAVES)
    tile_ids = leaf_tile[:, 0]
    marched = (leaf_layer < jnp.take(samples, tile_ids)).astype(jnp.float32)
    column = column * marched[None, :]
    segment_ids = tile_ids * BLOCKS + leaf_block
    summed = jax.ops.segment_sum(column.T, segment_ids, num_segments=TILES * BLOCKS)
    optical = summed.reshape(TILES, BLOCKS, 64).transpose(0, 2, 1).reshape(TILES, 64 * BLOCKS)
    rendered = 1.0 - jnp.exp(-optical)
    return new_velocity.reshape(3, LEAF_VOX, LEAVES), rendered
```

```python
import functools

import jax
import jax.numpy as jnp
from jax import lax
from jax.experimental import pallas as pl
from jax.experimental.pallas import tpu as pltpu
from jax.sharding import PartitionSpec as P

BLOCKS = 256
HALF = 128
SLOTS = 64
ADVECT = 0.2
RAY = 0.03

f32 = jnp.float32
bf16 = jnp.bfloat16
i32 = jnp.int32


def iota(shape, axis):
    return lax.broadcasted_iota(i32, shape, axis)


def take(table, lane):
    index = jnp.broadcast_to(lane, table.shape)
    return jnp.take_along_axis(table, index, axis=1, mode="promise_in_bounds")


def pick(low, high, lane, code, other):
    near = jnp.where(code == 1, take(low, lane), take(high, lane))
    return jnp.where((code == 1) | (code == 2), near, other)


def pick_remote(packed, lane, second):
    return take(packed, lane + second * SLOTS)


def packed_pair(first, second, lane, code):
    ga = jnp.where(code == 2, take(first[1], lane), take(first[0], lane))
    gb = jnp.where(code == 2, take(second[1], lane), take(second[0], lane))
    left = iota((1, HALF), 1) < SLOTS
    return jnp.where(left, ga, gb)


def ends(slab, low, high):
    down = jnp.concatenate([low, slab[:-8]], axis=0)
    up = jnp.concatenate([slab[8:], high], axis=0)
    return down, up


def turns(slab, low, high):
    n = slab.shape[0]
    row = iota((1, 8, 1), 1)
    down = jnp.where(row == 0, low.reshape(n, 1, HALF), pltpu.roll(slab, 1, 1))
    up = jnp.where(row == 7, high.reshape(n, 1, HALF), pltpu.roll(slab, 7, 1))
    return down, up


def zturns(slab, low, high):
    down, up = turns(slab.reshape(8, 8, HALF), low, high)
    return down.reshape(64, HALF), up.reshape(64, HALF)


def face_y(read, j):
    return jnp.concatenate([read(64 * i + 8 * j, 8) for i in range(8)], axis=0)


def odd_on(axis):
    return lax.axis_index(axis) & 1


def slot_of(n, odd):
    return (n + 1 + odd) & 1


def both_sides(first_ref, second_ref, odd):
    first, second = first_ref[...], second_ref[...]
    is_odd = jnp.broadcast_to(odd, first.shape) == 1
    return jnp.where(is_odd, first, second), jnp.where(is_odd, second, first)


def lanes(h):
    return slice(h * HALF, (h + 1) * HALF)


def link_lists(nb, dirs, dev_size):
    count = nb.shape[1]
    me = lax.axis_index("grp") * dev_size + lax.axis_index("dev")
    base = nb - me * count
    present = nb >= 0
    local = present & (base >= 0) & (base < count)
    remote = present & jnp.logical_not(local)
    slot = nb & (count - 1)
    code = jnp.where(local, jnp.where(slot < HALF, 1, 2), jnp.where(remote, 3, 0))
    rem = remote[0:4].astype(f32)
    key = jnp.where(remote[0:4], slot[0:4], 2 * count).astype(f32)
    cols = jnp.concatenate([rem, key], axis=0).T
    tri = (iota((count, count), 1) <= iota((count, count), 0)).astype(bf16)
    upto = jnp.dot(tri, cols.astype(bf16), preferred_element_type=f32)
    target = (iota((1, HALF), 1) & (SLOTS - 1)).astype(f32)
    lists = []
    for f in dirs:
        listed = (upto[:, f : f + 1] <= target).astype(f32)
        lists.append(jnp.sum(listed, axis=0, keepdims=True).astype(i32))
    listing = jnp.concatenate(lists, axis=0)
    clane = listing & (HALF - 1)
    ccode = jnp.where(listing < HALF, 1, jnp.where(listing < count, 2, 0))
    return code, slot, remote, key, cols, clane, ccode


def load_kernel(
    dev_size, v_any, w_any, nb_any, vy_ref, w_ref, nb_ref, send_ref, sems,
):
    copies = [
        pltpu.make_async_copy(nb_any, nb_ref, sems.at[0]),
        pltpu.make_async_copy(v_any.at[1], vy_ref, sems.at[1]),
        pltpu.make_async_copy(w_any, w_ref, sems.at[2]),
    ]
    for c in copies:
        c.start()
    copies[0].wait()
    clane, ccode = link_lists(nb_ref[...], (2, 3), dev_size)[-2:]
    copies[1].wait()
    copies[2].wait()
    for n, j in ((0, 0), (1, 7)):
        send_ref[slot_of(n, odd_on("grp"))] = packed_pair(
            [face_y(lambda r, m: vy_ref[r : r + m, lanes(h)], j) for h in range(2)],
            [face_y(lambda r, m: w_ref[r : r + m, lanes(h)], j) for h in range(2)],
            clane[n : n + 1], ccode[n : n + 1])


def index_kernel(
    dev_size, v_any, dens_any, layer_any, tile_any, block_any, samples_any, nb_ref,
    vxz_ref, dens_ref, idx_ref, cidx_ref, small_ref, samples_ref, sems,
):
    copies = [
        pltpu.make_async_copy(layer_any, small_ref.at[0:1], sems.at[3]),
        pltpu.make_async_copy(tile_any, small_ref.at[1:2], sems.at[4]),
        pltpu.make_async_copy(block_any, small_ref.at[2:3], sems.at[5]),
        pltpu.make_async_copy(samples_any, samples_ref, sems.at[6]),
        pltpu.make_async_copy(v_any.at[0], vxz_ref.at[0], sems.at[0]),
        pltpu.make_async_copy(v_any.at[2], vxz_ref.at[1], sems.at[1]),
        pltpu.make_async_copy(dens_any, dens_ref, sems.at[2]),
    ]
    for c in copies:
        c.start()
    count = nb_ref.shape[1]
    code, slot, remote, key, cols, clane, ccode = link_lists(nb_ref[...], range(4), dev_size)
    lane = slot & (HALF - 1)
    ranks = []
    for f in range(4):
        below = (cols[:, 4 + f : 5 + f] < key[f : f + 1, :]).astype(f32)
        ranks.append(jnp.sum(below, axis=0, keepdims=True).astype(i32))
    rank = jnp.concatenate(ranks, axis=0)
    lane4 = jnp.where(remote[0:4], rank & (SLOTS - 1), lane[0:4])
    zero2 = jnp.zeros((2, count), i32)
    idx_ref[0:8, :] = jnp.concatenate([lane4, lane[4:6], zero2], axis=0)
    idx_ref[8:16, :] = jnp.concatenate([code, zero2], axis=0)
    cidx_ref[...] = jnp.concatenate([clane, ccode], axis=0)
    for c in copies:
        c.wait()


def tile_kernel(cap, reps, small, samples_ref, after_ref, tidx_ref, ids_ref):
    count = small.shape[1]
    tiles = samples_ref.shape[1]
    rows = jnp.concatenate([small[0:1], small[1:2], small[2:3], jnp.zeros((5, count), i32)], axis=0)
    rows = rows.astype(f32)
    cols = rows.T
    tile = cols[:, 1:2]
    hot = tile == iota((count, tiles), 1).astype(f32)
    limit = jnp.sum(jnp.where(hot, samples_ref[...].astype(f32), 0.0), axis=1, keepdims=True)
    marched = cols[:, 0:1] < limit
    hot = hot & marched
    tri = (iota((count, count), 1) <= iota((count, count), 0)).astype(bf16)
    upto = jnp.dot(tri, hot.astype(bf16), preferred_element_type=f32)
    rank = jnp.sum(jnp.where(hot, upto, 0.0), axis=1, keepdims=True) - 1.0
    place = jnp.where(marched, tile * cap + rank, -1.0)
    place = jnp.broadcast_to(place, (count, HALF))
    lane_id = iota((1, HALF), 1)
    used = lane_id < cap * reps
    slot = (lane_id & (cap - 1)).astype(f32)
    listed = jnp.concatenate(
        [(place == jnp.where(used, slot + float(t * cap), -2.0)).astype(bf16)
         for t in range(tiles)], axis=1)
    leaf = iota((1, count), 1).astype(f32)
    table = jnp.concatenate([leaf, rows[2:3], jnp.ones((1, count), f32),
                             jnp.zeros((13, count), f32)], axis=0).astype(bf16)
    found = jnp.dot(table, listed, preferred_element_type=f32)
    for t in range(tiles):
        at = slice(t * HALF, (t + 1) * HALF)
        there = found[2:3, at] > 0.5
        listing = found[0:1, at].astype(i32)
        tidx_ref[t : t + 1, :] = listing & (HALF - 1)
        tidx_ref[tiles + t : tiles + t + 1, :] = jnp.where(
            there, jnp.where(listing < HALF, 1, 2), 0)
        ids_ref[t : t + 1, :] = jnp.where(there, found[1:2, at], -1.0)


def tables(idx_ref):
    lane = [[idx_ref[f : f + 1, lanes(h)] for h in range(2)] for f in range(6)]
    code = [[idx_ref[8 + f : 9 + f, lanes(h)] for h in range(2)] for f in range(6)]
    return lane, code


def edge_kernel(
    vxz_ref, vy_ref, w_ref, first_ref, second_ref, idx_ref, cidx_ref,
    src_ref, dia_ref, send_ref, zs,
):
    lane, code = tables(idx_ref)
    sides = both_sides(first_ref, second_ref, odd_on("grp"))
    for h in range(2):
        for n, start in ((0, 0), (1, 448)):
            rows = slice(start, start + 64)
            zs[0, h, 64 * n : 64 * n + 64] = vxz_ref[1, rows, lanes(h)]
            zs[1, h, 64 * n : 64 * n + 64] = w_ref[rows, lanes(h)]
    for n, start, inner, far_side in ((0, 0, 64, 448), (1, 448, 384, 0)):
        rows = slice(start, start + 64)
        small = slice(start // 8, start // 8 + 8)

        def tabs(read):
            return [read(h) for h in range(2)]

        for h in range(2):
            def face(f, v_tab, w_tab, w_own):
                ln, cd = lane[f][h], code[f][h]
                v_far, w_far = 0.0, jnp.where(cd == 3, 0.0, w_own)
                if f in (2, 3):
                    got = sides[f - 2][small]
                    v_far = jnp.where(cd == 3, pick_remote(got, ln, 0), 0.0)
                    w_far = jnp.where(cd == 3, pick_remote(got, ln, 1), w_own)
                return (pick(v_tab[0], v_tab[1], ln, cd, v_far),
                        pick(w_tab[0], w_tab[1], ln, cd, w_far))

            w = w_ref[rows, lanes(h)]
            far = slice(far_side, far_side + 64)
            next_rows = slice(inner, inner + 64)
            vx, wx = face(n, tabs(lambda g: vxz_ref[0, far, lanes(g)]),
                          tabs(lambda g: w_ref[far, lanes(g)]), w)
            sign = 1.0 if n == 0 else -1.0
            src = sign * (vxz_ref[0, next_rows, lanes(h)] - vx)
            dia = wx + w_ref[next_rows, lanes(h)]
            faces = []
            for f, j in ((2, 7), (3, 0)):
                at = slice(start + 8 * j, start + 8 * j + 8)
                mine = start + 56 - 8 * j
                faces.append(face(f, tabs(lambda g: vy_ref[ at, lanes(g)]),
                                  tabs(lambda g: w_ref[at, lanes(g)]),
                                  w_ref[mine : mine + 8, lanes(h)]))
            v_dn, v_up = ends(vy_ref[ rows, lanes(h)], faces[0][0], faces[1][0])
            w_dn, w_up = ends(w, faces[0][1], faces[1][1])
            src = src + (v_up - v_dn)
            dia = dia + (w_up + w_dn)
            faces = []
            for f, k in ((4, 7), (5, 0)):
                faces.append(face(f, tabs(lambda g: zs[0, g, pl.ds(64 * n + k, 8, stride=8), :]),
                                  tabs(lambda g: zs[1, g, pl.ds(64 * n + k, 8, stride=8), :]),
                                  zs[1, h, pl.ds(64 * n + 7 - k, 8, stride=8), :]))
            v_dn, v_up = zturns(vxz_ref[1, rows, lanes(h)], faces[0][0], faces[1][0])
            w_dn, w_up = zturns(w, faces[0][1], faces[1][1])
            src_ref[n, h] = -0.5 * (src + (v_up - v_dn))
            dia_ref[n, h] = 3.0 * w + 0.5 * (dia + (w_up + w_dn))
        cl, cc = cidx_ref[n : n + 1, :], cidx_ref[4 + n : 5 + n, :]
        slot = slot_of(n, odd_on("dev"))
        send_ref[slot, 0] = packed_pair(
            [vxz_ref[0, rows, lanes(h)] for h in range(2)],
            [w_ref[rows, lanes(h)] for h in range(2)], cl, cc)
        send_ref[slot, 1] = packed_pair(
            [src_ref[n, h] for h in range(2)], [dia_ref[n, h] for h in range(2)], cl, cc)


def inner_kernel(
    vxz_ref, vy_ref, w_ref, dens_ref, first_ref, second_ref, idx_ref, cidx_ref,
    psrc_ref, pdia_ref, aux_ref, xface_ref, zs, vface, face,
):
    lane, code = tables(idx_ref)
    sides = both_sides(first_ref, second_ref, odd_on("grp"))
    for h in range(2):
        zs[0, h] = vxz_ref[1, :, lanes(h)]
        zs[1, h] = w_ref[:, lanes(h)]
    v_tab, w_tab, w_own = {}, {}, {}
    for h in range(2):
        for f, start in ((0, 448), (1, 0)):
            w_tab[f, h] = w_ref[start : start + 64, lanes(h)]
            w_own[1 - f, h] = w_tab[f, h]
        for f, j in ((2, 7), (3, 0)):
            v_tab[f, h] = face_y(lambda r, n: vy_ref[ r : r + n, lanes(h)], j)
            w_tab[f, h] = face_y(lambda r, n: w_ref[r : r + n, lanes(h)], j)
            w_own[5 - f, h] = w_tab[f, h]
        for f, k in ((4, 7), (5, 0)):
            v_tab[f, h] = zs[0, h, pl.ds(k, 64, stride=8), :]
            w_tab[f, h] = zs[1, h, pl.ds(k, 64, stride=8), :]
            w_own[9 - f, h] = w_tab[f, h]
    for f in range(6):
        for h in range(2):
            ln, cd = lane[f][h], code[f][h]
            w_far = jnp.where(cd == 3, 0.0, w_own[f, h])
            v_far = 0.0
            if f in (2, 3):
                got = sides[f - 2]
                v_far = jnp.where(cd == 3, pick_remote(got, ln, 0), 0.0)
                w_far = jnp.where(cd == 3, pick_remote(got, ln, 1), w_own[f, h])
            w_face = pick(w_tab[f, 0], w_tab[f, 1], ln, cd, w_far)
            if f < 2:
                xface_ref[f, h] = w_face
            else:
                face[f - 2, h] = w_face
                vface[f - 2, h] = pick(v_tab[f, 0], v_tab[f, 1], ln, cd, v_far)
    for h in range(2):
        for i in range(8):
            rows = slice(64 * i, 64 * i + 64)
            small = slice(8 * i, 8 * i + 8)
            w = w_ref[rows, lanes(h)]
            wy_dn, wy_up = ends(w, face[0, h, small], face[1, h, small])
            wz_dn, wz_up = zturns(w, face[2, h, small], face[3, h, small])
            aux_ref[1, h, rows] = w + wy_dn
            aux_ref[2, h, rows] = w + wy_up
            aux_ref[3, h, rows] = w + wz_dn
            aux_ref[4, h, rows] = w + wz_up
            aux_ref[5, h, rows] = 0.5 * dens_ref[rows, lanes(h)] * w
            if i < 7:
                aux_ref[0, h, rows] = w + w_ref[64 * i + 64 : 64 * i + 128, lanes(h)]
            if i in (0, 7):
                continue
            below, above = slice(64 * i - 64, 64 * i), slice(64 * i + 64, 64 * i + 128)
            vy_dn, vy_up = ends(vy_ref[ rows, lanes(h)], vface[0, h, small], vface[1, h, small])
            vz_dn, vz_up = zturns(vxz_ref[1, rows, lanes(h)], vface[2, h, small], vface[3, h, small])
            vx = vxz_ref[0, above, lanes(h)] - vxz_ref[0, below, lanes(h)]
            psrc_ref[h, rows] = -0.5 * (vx + (vy_up - vy_dn) + (vz_up - vz_dn))
            wx = w_ref[above, lanes(h)] + w_ref[below, lanes(h)]
            pdia_ref[h, rows] = 3.0 * w + 0.5 * (wx + (wy_up + wy_dn) + (wz_up + wz_dn))


def z_faces(q_ref, lane, code, zface, layers=()):
    for i in layers:
        for f, k in ((4, 7), (5, 0)):
            tabs = [q_ref[h, pl.ds(64 * i + k, 8, stride=8), :] for h in range(2)]
            for h in range(2):
                zface[f - 4, h, 8 * i : 8 * i + 8] = pick(
                    tabs[0], tabs[1], lane[f][h], code[f][h], 0.0)
    if layers:
        return
    for f, k in ((4, 7), (5, 0)):
        tabs = [q_ref[h, pl.ds(k, 64, stride=8), :] for h in range(2)]
        for h in range(2):
            zface[f - 4, h] = pick(tabs[0], tabs[1], lane[f][h], code[f][h], 0.0)


def x_terms(q_ref, aux_ref, xsum_ref, xface, h, i):
    if i == 0:
        dn, c_dn = xface[0, h], xsum_ref[0, h]
    else:
        below = slice(64 * i - 64, 64 * i)
        dn, c_dn = q_ref[h, below], aux_ref[0, h, below]
    if i == 7:
        up, c_up = xface[1, h], xsum_ref[1, h]
    else:
        up, c_up = q_ref[h, 64 * i + 64 : 64 * i + 128], aux_ref[0, h, 64 * i : 64 * i + 64]
    return dn, up, c_dn * dn + c_up * up


def products(q_ref, aux_ref, xsum_ref, rdia_ref, xface, yface, zface, out_ref, layers=range(8)):
    for h in range(2):
        for i in layers:
            rows = slice(64 * i, 64 * i + 64)
            small = slice(8 * i, 8 * i + 8)
            q = q_ref[h, rows]
            total = x_terms(q_ref, aux_ref, xsum_ref, xface, h, i)[2]
            dn, up = ends(q, yface[0, h, small], yface[1, h, small])
            total = total + (aux_ref[1, h, rows] * dn + aux_ref[2, h, rows] * up)
            dn, up = zturns(q, zface[0, h, small], zface[1, h, small])
            total = total + (aux_ref[3, h, rows] * dn + aux_ref[4, h, rows] * up)
            out_ref[h, rows] = (0.5 * rdia_ref[h, rows]) * total


def first_kernel(
    vxz_ref, w_ref, psrc_ref, pdia_ref, esrc_ref, edia_ref, aux_ref, xface_ref,
    first_ref, second_ref, idx_ref, cidx_ref, after_ref,
    dia_ref, z0_ref, rdia_ref, xsum_ref, xq_ref, xhr_ref, send_ref,
):
    lane, code = tables(idx_ref)
    sides = both_sides(first_ref, second_ref, odd_on("dev"))
    for h in range(2):
        for i in range(1, 7):
            rows = slice(64 * i, 64 * i + 64)
            rdia = 1.0 / dia_ref[h, rows]
            rdia_ref[h, rows] = rdia
            z0_ref[h, rows] = psrc_ref[h, rows] * rdia
        for f, start, sign in ((0, 0, 0.5), (1, 448, -0.5)):
            rows = slice(start, start + 64)
            got = sides[f]
            ln, cd = lane[f][h], code[f][h]
            far = cd == 3
            v_m = jnp.where(far, pick_remote(got[0], ln, 0), 0.0)
            w_m = jnp.where(far, pick_remote(got[0], ln, 1), 0.0)
            src_m = jnp.where(far, pick_remote(got[1], ln, 0), 0.0)
            dia_m = jnp.where(far, pick_remote(got[1], ln, 1), 1.0)
            w = w_ref[rows, lanes(h)]
            dia = edia_ref[f, h] + 0.5 * w_m
            rdia = 1.0 / dia
            dia_ref[h, rows] = dia
            rdia_ref[h, rows] = rdia
            z0_ref[h, rows] = (esrc_ref[f, h] + sign * v_m) * rdia
            rdia_m = 1.0 / (dia_m + 0.5 * w)
            z0_m = (src_m - sign * vxz_ref[0, rows, lanes(h)]) * rdia_m
            xhr_ref[f, h] = rdia_m
            xq_ref[f, h] = jnp.where(far, z0_m, 0.0)
            xsum_ref[f, h] = w + jnp.where(far, w_m, xface_ref[f, h])
    for f, start in ((0, 448), (1, 0)):
        tabs = [z0_ref[h, start : start + 64] for h in range(2)]
        for h in range(2):
            xq_ref[f, h] = pick(tabs[0], tabs[1], lane[f][h], code[f][h], xq_ref[f, h])
    z1f = {}
    for n, f, j, there, inner in ((0, 2, 0, 7, 1), (1, 3, 7, 0, 6)):
        tabs = [face_y(lambda r, m: z0_ref[h, r : r + m], there) for h in range(2)]
        at = slice(8 * j, 8 * j + 8)
        for h in range(2):
            q = face_y(lambda r, m: z0_ref[h, r : r + m], j)
            c = face_y(lambda r, m: aux_ref[0, h, r : r + m], j)[:56]
            c_dn = jnp.concatenate([xsum_ref[0, h, at], c], axis=0)
            c_up = jnp.concatenate([c, xsum_ref[1, h, at]], axis=0)
            dn, up = ends(q, xq_ref[0, h, at], xq_ref[1, h, at])
            total = c_dn * dn + c_up * up
            near = pick(tabs[0], tabs[1], lane[f][h], code[f][h], 0.0)
            next_q = face_y(lambda r, m: z0_ref[h, r : r + m], inner)
            c_near = face_y(lambda r, m: aux_ref[1 + n, h, r : r + m], j)
            c_next = face_y(lambda r, m: aux_ref[2 - n, h, r : r + m], j)
            total = total + (c_near * near + c_next * next_q)
            zf = []
            for g, k in ((4, 7), (5, 0)):
                rows = [z0_ref[e, pl.ds(8 * j + k, 8, stride=64), :] for e in range(2)]
                zf.append(pick(rows[0], rows[1], lane[g][h], code[g][h], 0.0))
            dn, up = zturns(q, zf[0], zf[1])
            c_dn = face_y(lambda r, m: aux_ref[3, h, r : r + m], j)
            c_up = face_y(lambda r, m: aux_ref[4, h, r : r + m], j)
            total = total + (c_dn * dn + c_up * up)
            z1f[n, h] = (0.5 * face_y(lambda r, m: rdia_ref[h, r : r + m], j)) * total
    for n, j in ((0, 0), (1, 7)):
        cl, cc = cidx_ref[2 + n : 3 + n, :], cidx_ref[6 + n : 7 + n, :]
        z0f = [face_y(lambda r, m: z0_ref[h, r : r + m], j) for h in range(2)]
        rdf = [face_y(lambda r, m: rdia_ref[h, r : r + m], j) for h in range(2)]
        slot = slot_of(n, odd_on("grp"))
        send_ref[slot, 0] = packed_pair(z0f, [z1f[n, 0], z1f[n, 1]], cl, cc)
        send_ref[slot, 1] = jnp.where(cc == 2, take(rdf[1], cl), take(rdf[0], cl))


def first_rest_kernel(
    z0_ref, aux_ref, xsum_ref, rdia_ref, xq_ref, idx_ref, pz1_ref, yface, zface,
):
    lane, code = tables(idx_ref)
    for f, j in ((2, 7), (3, 0)):
        tabs = [face_y(lambda r, n: z0_ref[h, r : r + n], j) for h in range(2)]
        for h in range(2):
            yface[f - 2, h] = pick(tabs[0], tabs[1], lane[f][h], code[f][h], 0.0)
    z_faces(z0_ref, lane, code, zface)
    products(z0_ref, aux_ref, xsum_ref, rdia_ref, xq_ref, yface, zface, pz1_ref)


def second_kernel(
    vxz_ref, dens_ref, z0_ref, pz1_ref, rdia_ref, aux_ref, xsum_ref,
    first_ref, second_ref, idx_ref, cidx_ref,
    z1_ref, yq0_ref, yq1_ref, send_ref, pz2_ref, xface, zface,
):
    lane, code = tables(idx_ref)
    sides = both_sides(first_ref, second_ref, odd_on("grp"))
    for h in range(2):
        for f, j in ((2, 0), (3, 7)):
            got = sides[f - 2]
            ln, cd = lane[f][h], code[f][h]
            far = cd == 3
            z0_m = jnp.where(far, pick_remote(got[0], ln, 0), 0.0)
            z1_m = pick_remote(got[0], ln, 1)
            rd_m = pick_remote(got[1], ln, 0)
            yq0_ref[f - 2, h] = z0_m
            w_sum = 0.5 * face_y(lambda r, n: aux_ref[f - 1, h, r : r + n], j)
            z0_l = face_y(lambda r, n: z0_ref[h, r : r + n], j)
            rd_l = face_y(lambda r, n: rdia_ref[h, r : r + n], j)
            yq1_ref[f - 2, h] = jnp.where(far, z1_m + rd_m * w_sum * z0_l, 0.0)
            extra = rd_l * w_sum * z0_m
            for i in range(8):
                rows = slice(64 * i + 8 * j, 64 * i + 8 * j + 8)
                z1_ref[h, rows] = z1_ref[h, rows] + extra[8 * i : 8 * i + 8]
    for f, start in ((0, 448), (1, 0)):
        tabs = [z1_ref[h, start : start + 64] for h in range(2)]
        for h in range(2):
            xface[f, h] = pick(tabs[0], tabs[1], lane[f][h], code[f][h], 0.0)
    for f, j in ((2, 7), (3, 0)):
        for q_ref, out in ((z0_ref, yq0_ref), (z1_ref, yq1_ref)):
            tabs = [face_y(lambda r, n: q_ref[h, r : r + n], j) for h in range(2)]
            for h in range(2):
                out[f - 2, h] = pick(tabs[0], tabs[1], lane[f][h], code[f][h], out[f - 2, h])
    layers = (0, 1, 6, 7)
    z_faces(z1_ref, lane, code, zface, layers)
    products(z1_ref, aux_ref, xsum_ref, rdia_ref, xface, yq1_ref, zface, pz2_ref, layers)
    for n, start, inner in ((0, 0, 64), (1, 448, 384)):
        cl, cc = cidx_ref[n : n + 1, :], cidx_ref[4 + n : 5 + n, :]
        rows, next_rows = slice(start, start + 64), slice(inner, inner + 64)
        z1f = [z1_ref[h, rows] for h in range(2)]
        z2f = [pz2_ref[h, rows] for h in range(2)]
        kf, sums = [], []
        for h in range(2):
            k = aux_ref[5, h, rows]
            parts = [k * q[h, next_rows] for q in (z0_ref, z1_ref, pz2_ref)]
            parts.append(dens_ref[rows, lanes(h)] * vxz_ref[0, rows, lanes(h)])
            summed = [over_j(p) for p in parts]
            kf.append(k)
            sums.append(jnp.concatenate(summed + [jnp.zeros((32, HALF), f32)], axis=0))
        slot = slot_of(n, odd_on("dev"))
        send_ref[slot, 0] = packed_pair(z1f, z2f, cl, cc)
        send_ref[slot, 1] = packed_pair(kf, sums, cl, cc)


def second_rest_kernel(
    z1_ref, aux_ref, xsum_ref, rdia_ref, yq1_ref, idx_ref, pz2_ref, xface, zface,
):
    lane, code = tables(idx_ref)
    for f, start in ((0, 448), (1, 0)):
        tabs = [z1_ref[h, start : start + 64] for h in range(2)]
        for h in range(2):
            xface[f, h] = pick(tabs[0], tabs[1], lane[f][h], code[f][h], 0.0)
    z_faces(z1_ref, lane, code, zface)
    products(z1_ref, aux_ref, xsum_ref, rdia_ref, xface, yq1_ref, zface, pz2_ref)


def third_kernel(
    vy_ref, dens_ref, z0_ref, z1_ref, pz2_ref, rdia_ref, aux_ref, xsum_ref, xhr_ref,
    first_ref, second_ref, idx_ref, cidx_ref, after_ref,
    z2_ref, xq1_ref, xq2_ref, xcol_ref, send_ref,
):
    lane, code = tables(idx_ref)
    sides = both_sides(first_ref, second_ref, odd_on("dev"))
    for h in range(2):
        for f, start in ((0, 0), (1, 448)):
            rows = slice(start, start + 64)
            got = sides[f]
            ln, cd = lane[f][h], code[f][h]
            far = cd == 3
            z1_m = jnp.where(far, pick_remote(got[0], ln, 0), 0.0)
            z2_m = pick_remote(got[0], ln, 1)
            k_m = pick_remote(got[1], ln, 0)
            sums = pick_remote(got[1, 0:32], ln, 1)
            w_sum = 0.5 * xsum_ref[f, h]
            xq1_ref[f, h] = z1_m
            xq2_ref[f, h] = jnp.where(far, z2_m + xhr_ref[f, h] * w_sum * z1_ref[h, rows], 0.0)
            z2_l = z2_ref[h, rows] + rdia_ref[h, rows] * w_sum * z1_m
            z2_ref[h, rows] = z2_l
            sign = 1.0 if f == 0 else -1.0
            for c, q in enumerate((z0_ref[h, rows], z1_ref[h, rows], z2_l)):
                mine = over_j(k_m * q)
                xcol_ref[f, h, 8 * c + 8 : 8 * c + 16] = sign * (sums[8 * c : 8 * c + 8] - mine)
            xcol_ref[f, h, 0:8] = sums[24:32]
    for f, start in ((0, 448), (1, 0)):
        for q_ref, out in ((z1_ref, xq1_ref), (z2_ref, xq2_ref)):
            tabs = [q_ref[h, start : start + 64] for h in range(2)]
            for h in range(2):
                out[f, h] = pick(tabs[0], tabs[1], lane[f][h], code[f][h], out[f, h])
    for n, j, inner in ((0, 0, 1), (1, 7, 6)):
        cl, cc = cidx_ref[2 + n : 3 + n, :], cidx_ref[6 + n : 7 + n, :]
        kf, vf = [], []
        for h in range(2):
            dens = face_y(lambda r, m: dens_ref[r : r + m, lanes(h)], j)
            kf.append(face_y(lambda r, m: aux_ref[5, h, r : r + m], j))
            vf.append(dens * face_y(lambda r, m: vy_ref[ r : r + m, lanes(h)], j))
        z2f = [face_y(lambda r, m: z2_ref[h, r : r + m], j) for h in range(2)]
        inners = [
            [kf[h] * face_y(lambda r, m: q[h, r : r + m], inner) for h in range(2)]
            for q in (z0_ref, z1_ref, z2_ref)
        ]
        slot = slot_of(n, odd_on("grp"))
        send_ref[slot, 0] = packed_pair(z2f, kf, cl, cc)
        send_ref[slot, 1] = packed_pair(inners[0], inners[1], cl, cc)
        send_ref[slot, 2] = packed_pair(inners[2], vf, cl, cc)


def over_j(a):
    return jnp.sum(a.reshape(8, 8, HALF), axis=0)


def column_first_kernel(
    vxz_ref, vy_ref, dens_ref, z0_ref, z1_ref, dia_ref, aux_ref, xq0_ref, yq0_ref, yq1_ref, idx_ref,
    col_ref, xs_ref, mom_ref,
    zface, zsum, fy,
):
    lane, code = tables(idx_ref)
    basis = (z0_ref, z1_ref)
    for c in range(2):
        z_faces(basis[c], lane, code, zface.at[c])
    for h in range(2):
        mu = [jnp.zeros((8, HALF), f32) for _ in range(3)]
        for i in range(8):
            rows = slice(64 * i, 64 * i + 64)
            small = slice(8 * i, 8 * i + 8)
            dens = dens_ref[rows, lanes(h)]
            kk = aux_ref[5, h, rows]
            xs_ref[0, h, small] = over_j(dens * vxz_ref[0, rows, lanes(h)])
            zsum[0, h, small] = over_j(dens * vxz_ref[1, rows, lanes(h)])
            col_ref[0, h, small] = over_j(dens)
            q = [basis[c][h, rows] for c in range(2)]
            dn = xq0_ref[0, h] if i == 0 else z0_ref[h, 64 * i - 64 : 64 * i]
            up = xq0_ref[1, h] if i == 7 else z0_ref[h, 64 * i + 64 : 64 * i + 128]
            xs_ref[1, h, small] = over_j(kk * (dn - up))
            for c in range(2):
                zdn, zup = zturns(q[c], zface[c, 0, h, small], zface[c, 1, h, small])
                zsum[c + 1, h, small] = over_j(kk * (zdn - zup))
            dia = dia_ref[h, rows]
            d0, d1 = dia * q[0], dia * q[1]
            mu[0] = mu[0] + over_j(d0 * q[0])
            mu[1] = mu[1] + over_j(d0 * q[1])
            mu[2] = mu[2] + over_j(d1 * q[1])
        for n in range(3):
            mom_ref[h, n] = mu[n]
    scale = RAY * 0.5 * ADVECT
    yq = (yq0_ref, yq1_ref)
    for h in range(2):
        for n, j, inner in ((0, 0, 1), (1, 7, 6)):
            dens = face_y(lambda r, m: dens_ref[r : r + m, lanes(h)], j)
            kk = face_y(lambda r, m: aux_ref[5, h, r : r + m], j)
            fy[n, 0, h] = dens * face_y(lambda r, m: vy_ref[r : r + m, lanes(h)], j)
            for c in range(2):
                near = face_y(lambda r, m: basis[c][h, r : r + m], inner)
                out = yq[c][n, h]
                fy[n, c + 1, h] = kk * ((out - near) if n == 0 else (near - out))
    for c in range(3):
        for h in range(2):
            change = z_change(zsum, c, h, lane, code) + (fy[1, c, h] - fy[0, c, h])
            for n in range(2):
                value = pick(fy[1 - n, c, 0], fy[1 - n, c, 1], lane[2 + n][h], code[2 + n][h], 0.0)
                change = change + value if n == 1 else change - value
            if c == 0:
                col_ref[c, h] = RAY * col_ref[c, h] - scale * change
            else:
                col_ref[c, h] = -scale * change


def z_change(zsum, c, h, lane, code):
    zf = []
    for f, k in ((4, 7), (5, 0)):
        tabs = [zsum[c, g, pl.ds(k, 8, stride=8), :] for g in range(2)]
        zf.append(pick(tabs[0], tabs[1], lane[f][h], code[f][h], 0.0))
    down, up = turns(zsum[c, h].reshape(8, 8, HALF), zf[0], zf[1])
    return (up - down).reshape(64, HALF)


def column_kernel(
    z1_ref, z2_ref, dia_ref, aux_ref, xsum_ref, xq1_ref, xq2_ref, xcol_ref, part_ref, xs_ref, idx_ref,
    col_ref, mom_ref, ynear_ref,
    zface, zsum, xsum,
):
    lane, code = tables(idx_ref)
    for f, j in ((2, 7), (3, 0)):
        tabs = [face_y(lambda r, n: z2_ref[h, r : r + n], j) for h in range(2)]
        for h in range(2):
            ynear_ref[f - 2, h] = pick(tabs[0], tabs[1], lane[f][h], code[f][h], 0.0)
    z_faces(z2_ref, lane, code, zface)
    for h in range(2):
        mu = [jnp.zeros((8, HALF), f32) for _ in range(3)]
        for i in range(8):
            rows = slice(64 * i, 64 * i + 64)
            small = slice(8 * i, 8 * i + 8)
            kk = aux_ref[5, h, rows]
            dn = xq1_ref[0, h] if i == 0 else z1_ref[h, 64 * i - 64 : 64 * i]
            up = xq1_ref[1, h] if i == 7 else z1_ref[h, 64 * i + 64 : 64 * i + 128]
            xsum[0, h, small] = over_j(kk * (dn - up))
            q = z2_ref[h, rows]
            dn, up, total = x_terms(z2_ref, aux_ref, xsum_ref, xq2_ref, h, i)
            xsum[1, h, small] = over_j(kk * (dn - up))
            dn, up = zturns(q, zface[0, h, small], zface[1, h, small])
            zsum[0, h, small] = over_j(kk * (dn - up))
            total = total + (aux_ref[3, h, rows] * dn + aux_ref[4, h, rows] * up)
            dn, up = ends(q, ynear_ref[0, h, small], ynear_ref[1, h, small])
            total = total + (aux_ref[1, h, rows] * dn + aux_ref[2, h, rows] * up)
            d2 = dia_ref[h, rows] * q
            mu[0] = mu[0] + over_j(d2 * z1_ref[h, rows])
            mu[1] = mu[1] + over_j(d2 * q)
            mu[2] = mu[2] + over_j(0.5 * total * q)
        for n in range(3):
            mom_ref[h, n] = mu[n]
    scale = RAY * 0.5 * ADVECT
    for c in range(4):
        for h in range(2):
            sums = [xs_ref[c, g] if c < 2 else xsum[c - 2, g] for g in range(2)]
            faces = []
            for f, start in ((0, 56), (1, 0)):
                far = jnp.where(code[f][h] == 3, xcol_ref[f, h, 8 * c : 8 * c + 8], 0.0)
                faces.append(pick(sums[0][start : start + 8], sums[1][start : start + 8],
                                  lane[f][h], code[f][h], far))
            down, up = ends(sums[h], faces[0], faces[1])
            if c < 3:
                col_ref[c, h] = part_ref[c, h] - scale * (up - down)
            else:
                col_ref[c, h] = -scale * ((up - down) + z_change(zsum, 0, h, lane, code))


def y_kernel(
    tiles, z0_ref, z1_ref, z2_ref, aux_ref,
    col_ref, mom1_ref, mom_ref, ynear_ref, first_ref, second_ref, idx_ref, ids_ref,
    yq2_ref, send_ref, out_ref, fy,
):
    lane, code = tables(idx_ref)
    basis = (z0_ref, z1_ref, z2_ref)
    sides = both_sides(first_ref, second_ref, odd_on("grp"))
    extra = jnp.zeros((64, HALF), f32)
    for h in range(2):
        for n, j, inner in ((0, 0, 1), (1, 7, 6)):
            ln, cd = lane[2 + n][h], code[2 + n][h]
            far = jnp.where(cd == 3, pick_remote(sides[n][0], ln, 0), 0.0)
            out = ynear_ref[n, h] + far
            yq2_ref[n, h] = out
            z2 = face_y(lambda r, m: z2_ref[h, r : r + m], j)
            w_sum = 0.5 * face_y(lambda r, m: aux_ref[1 + n, h, r : r + m], j)
            extra = extra + w_sum * (far * z2)
            kk = face_y(lambda r, m: aux_ref[5, h, r : r + m], j)
            near = face_y(lambda r, m: z2_ref[h, r : r + m], inner)
            fy[n, h] = kk * ((out - near) if n == 0 else (near - out))
    scale = RAY * 0.5 * ADVECT
    for h in range(2):
        change = [None, None, None, fy[1, h] - fy[0, h]]
        for n, j in ((0, 0), (1, 7)):
            got = sides[n]
            ln, cd = lane[2 + n][h], code[2 + n][h]
            far = cd == 3
            k_m = pick_remote(got[0], ln, 1)
            for c in range(4):
                if c == 0:
                    other = pick_remote(got[2], ln, 1)
                else:
                    inner = pick_remote(got[1 + (c - 1) // 2], ln, (c - 1) % 2)
                    mine = k_m * face_y(lambda r, m: basis[c - 1][h, r : r + m], j)
                    other = (mine - inner) if n == 1 else (inner - mine)
                value = jnp.where(far, other, 0.0)
                if c == 3:
                    value = pick(fy[1 - n, 0], fy[1 - n, 1], ln, cd, value)
                value = value if n == 1 else -value
                change[c] = value if change[c] is None else change[c] + value
        for c in range(4):
            out_ref[c, h] = col_ref[c, h] - scale * change[c]
    parts = [m[0, n] + m[1, n] for m in (mom1_ref, mom_ref) for n in range(3)]
    parts[5] = parts[5] + over_j(extra)
    which = iota((1, HALF), 1)
    row = jnp.zeros((1, HALF), f32)
    for n, m in enumerate(parts):
        total = jnp.sum(jnp.sum(m, axis=0, keepdims=True), axis=1, keepdims=True)
        row = jnp.where(which == n, total, row)
    for t in range(tiles):
        names = pltpu.roll(ids_ref[t : t + 1, :], SLOTS, 1)
        line = jnp.where(which < SLOTS, row, names)
        for g in range(send_ref.shape[0] // tiles):
            send_ref[g * tiles + t] = line


def coefficients(mu):
    def dot(a, b):
        total = None
        for i, x in enumerate(a):
            for j, y in enumerate(b):
                if x is None or y is None:
                    continue
                term = x * y * mu[i + j]
                total = term if total is None else total + term
        return total

    one = jnp.ones_like(mu[0])
    residual = [one]
    direction = [one]
    energy = mu[0]
    pressure = [None, None, None]
    for iteration in range(3):
        image = [direction[0]]
        for n in range(1, len(direction)):
            image.append(direction[n] - direction[n - 1])
        image.append(-direction[-1])
        step = energy / dot(direction, image)
        for n, d in enumerate(direction):
            pressure[n] = step * d if pressure[n] is None else pressure[n] + step * d
        if iteration < 2:
            old = residual + [None]
            residual = []
            for n, im in enumerate(image):
                residual.append(-step * im if old[n] is None else old[n] - step * im)
            fresh = dot(residual, residual)
            beta = fresh / energy
            energy = fresh
            longer = direction + [None]
            direction = [
                r if d is None else r + beta * d for r, d in zip(residual, longer)
            ]
    return pressure


def pack_kernel(tiles, cap, fold, got_ref, col_ref, tidx_ref, send_ref, coef_ref):
    sources = got_ref.shape[0]
    total = got_ref[0]
    for s in range(1, sources):
        total = total + got_ref[s]
    coef = coefficients([jnp.broadcast_to(total[:, n : n + 1], (1, HALF)) for n in range(6)])
    coef_ref[...] = jnp.concatenate(coef + [jnp.zeros((5, HALF), f32)], axis=0)
    full = []
    for h in range(2):
        value = col_ref[0, h]
        for n in range(3):
            value = value + coef[n] * col_ref[n + 1, h]
        full.append(value)
    g_count = sources // tiles
    height = 64 // g_count
    left = iota((1, HALF), 1) < cap
    for t in range(tiles):
        ln = tidx_ref[t : t + 1, :]
        cd = tidx_ref[tiles + t : tiles + t + 1, :]
        value = pick(full[0], full[1], ln, cd, 0.0)
        for g in range(g_count):
            part = value[g * height : g * height + height]
            if fold == 2:
                part = jnp.where(left, part[0:8], part[8:16])
            send_ref[g * tiles + t] = part


def final_kernel(
    fold, got_ref, names_ref, coef_ref, vxz_ref, vy_ref, w_ref, z0_ref, z1_ref, z2_ref,
    xq0_ref, xq1_ref, xq2_ref, yq0_ref, yq1_ref, yq2_ref, idx_ref,
    vout_any, image_ref, vout, p, hot, contrib, sems,
):
    coef = [coef_ref[n : n + 1, :] for n in range(3)]
    lane, code = tables(idx_ref)
    for h in range(2):
        for i in range(8):
            rows = slice(64 * i, 64 * i + 64)
            p[h, rows] = (
                coef[0] * z0_ref[h, rows] + coef[1] * z1_ref[h, rows] + coef[2] * z2_ref[h, rows])
    zf = {}
    for f, k in ((4, 7), (5, 0)):
        tabs = [p[h, pl.ds(k, 64, stride=8), :] for h in range(2)]
        for h in range(2):
            zf[f - 4, h] = pick(tabs[0], tabs[1], lane[f][h], code[f][h], 0.0)

    def blend(a_ref, b_ref, c_ref, n, h):
        return coef[0] * a_ref[n, h] + coef[1] * b_ref[n, h] + coef[2] * c_ref[n, h]

    copies = []
    xf = [[blend(xq0_ref, xq1_ref, xq2_ref, n, h) for n in range(2)] for h in range(2)]
    yf = [[blend(yq0_ref, yq1_ref, yq2_ref, n, h) for n in range(2)] for h in range(2)]
    for i in range(8):
        rows = slice(64 * i, 64 * i + 64)
        small = slice(8 * i, 8 * i + 8)
        for h in range(2):
            w = 0.5 * w_ref[rows, lanes(h)]
            mine = p[h, rows]
            dn = xf[h][0] if i == 0 else p[h, 64 * i - 64 : 64 * i]
            up = xf[h][1] if i == 7 else p[h, 64 * i + 64 : 64 * i + 128]
            vout[0, rows, lanes(h)] = vxz_ref[0, rows, lanes(h)] - w * (up - dn)
            dn, up = ends(mine, yf[h][0][small], yf[h][1][small])
            vout[1, rows, lanes(h)] = vy_ref[rows, lanes(h)] - w * (up - dn)
            dn, up = zturns(mine, zf[0, h][small], zf[1, h][small])
            vout[2, rows, lanes(h)] = vxz_ref[1, rows, lanes(h)] - w * (up - dn)
        if i % 2:
            piece = slice(64 * i - 64, 64 * i + 64)
            copies.append(pltpu.make_async_copy(
                vout.at[:, piece], vout_any.at[:, piece], sems.at[i // 2]))
            copies[-1].start()

    sources, height = got_ref.shape[0], 8 * fold
    left = iota((1, HALF), 1) < HALF // 2
    rows_id = iota((BLOCKS, HALF), 0).astype(f32)
    for s in range(0, sources, fold):
        value = got_ref[s]
        after_ids = names_ref[s + 1] if fold == 2 else -1.0
        ids = jnp.where(left, pltpu.roll(names_ref[s], HALF // 2, 1), after_ids)
        if fold == 2:
            after = got_ref[s + 1]
            value = jnp.concatenate(
                [jnp.where(left, value, pltpu.roll(after, HALF // 2, 1)),
                 jnp.where(left, pltpu.roll(value, HALF // 2, 1), after)], axis=0)
        high = value.astype(bf16)
        rest = value - high.astype(f32)
        middle = rest.astype(bf16)
        low = (rest - middle.astype(f32)).astype(bf16)
        cols = slice(s // fold * HALF, (s // fold + 1) * HALF)
        for n, piece in enumerate((high, middle, low)):
            contrib[16 * n : 16 * n + height, cols] = piece
        hot[:, cols] = (rows_id == ids).astype(bf16)
    if height < 16:
        for n in range(3):
            contrib[16 * n + height : 16 * n + 16, :] = jnp.zeros(
                (16 - height, contrib.shape[1]), bf16)
    product = lax.dot_general(
        hot[...], contrib[...], (((1,), (1,)), ((), ())), preferred_element_type=f32).T
    optical = product[0:16] + (product[16:32] + product[32:48])
    shade = 1.0 - jnp.exp(-optical)
    for m in range(height):
        image_ref[0:1, m * BLOCKS : (m + 1) * BLOCKS] = shade[m : m + 1, :]
    for c in copies:
        c.wait()


def call(kernel, outs, scratch, args, any_args=0, limit=10, final=False, alias=None):
    spaces = [pltpu.HBM if n < any_args else pltpu.VMEM for n in range(len(args))]
    out_specs = [pl.BlockSpec(memory_space=pltpu.VMEM) for _ in outs]
    if final:
        out_specs[0] = pl.BlockSpec(memory_space=pltpu.HBM)
    return pl.pallas_call(
        kernel,
        out_shape=[jax.ShapeDtypeStruct(s, d) if final else pltpu.VMEM(s, d) for s, d in outs],
        in_specs=[pl.BlockSpec(memory_space=space) for space in spaces],
        out_specs=out_specs,
        scratch_shapes=scratch,
        input_output_aliases=alias or {},
        compiler_params=pltpu.CompilerParams(vmem_limit_bytes=limit * 1024 * 1024),
    )(*[pltpu.with_memory_space_constraint(a, space) for a, space in zip(args, spaces)])


def swap(packed, axis):
    count = lax.axis_size(axis)
    results = []
    for start in range(2):
        pairs = [(i, i + 1) for i in range(start, count - 1, 2)]
        results.append(lax.ppermute(packed[start], axis, pairs + [(b, a) for a, b in pairs]))
    return results


def shards(
    velocity, density, inverse_density, neighbours, leaf_layer, leaf_tile, leaf_block, samples
):
    count = density.shape[1]
    tiles = samples.shape[0]
    grp_size, dev_size = lax.axis_size("grp"), lax.axis_size("dev")
    cap = 2 * count // tiles
    height = 64 // grp_size
    fold = min(height // 8, HALF // cap)
    sources = grp_size * dev_size
    everyone = ("grp", "dev")

    field = ((2, 512, HALF), f32)
    sides = ((2, 2, 64, HALF), f32)

    def vm(*shape):
        return pltpu.VMEM(shape, f32)

    vy, inv, nb, send = call(
        functools.partial(load_kernel, dev_size),
        [((512, count), f32), ((512, count), f32), ((6, count), i32), ((2, 64, HALF), f32)],
        [pltpu.SemaphoreType.DMA((3,))],
        (velocity, inverse_density, neighbours),
        any_args=3,
    )
    first, second = swap(send, "grp")
    vxz, dens, idx, cidx, small, limits = call(
        functools.partial(index_kernel, dev_size),
        [((2, 512, count), f32), ((512, count), f32), ((16, count), i32), ((8, HALF), i32),
         ((8, count), i32), ((1, tiles), i32)],
        [pltpu.SemaphoreType.DMA((7,))],
        (velocity, density, leaf_layer.reshape(1, count), leaf_tile.reshape(1, count),
         leaf_block.reshape(1, count), samples.reshape(1, tiles), nb),
        any_args=6,
    )
    esrc, edia, send = call(
        edge_kernel,
        [sides, sides, ((2, 2, 64, HALF), f32)],
        [vm(2, 2, HALF, HALF)],
        (vxz, vy, inv, first, second, idx, cidx),
    )
    got_first, got_second = swap(send, "dev")
    psrc, pdia, aux, xface = call(
        inner_kernel,
        [field, field, ((6, 2, 512, HALF), f32), sides],
        [vm(2, 2, 512, HALF), vm(4, 2, 64, HALF), vm(4, 2, 64, HALF)],
        (vxz, vy, inv, dens, first, second, idx, cidx),
    )
    tidx, ids = call(
        functools.partial(tile_kernel, cap, fold),
        [((2 * tiles, HALF), i32), ((tiles, HALF), f32)],
        [],
        (small, limits, esrc),
    )
    dia, z0, rdia, xsum, xq0, xhr, send = call(
        first_kernel,
        [field, field, field, sides, sides, sides, ((2, 2, 64, HALF), f32)],
        [],
        (vxz, inv, psrc, pdia, esrc, edia, aux, xface, got_first, got_second, idx, cidx, ids),
        alias={3: 0},
    )
    first, second = swap(send, "grp")
    (pz1,) = call(
        first_rest_kernel,
        [field],
        [vm(2, 2, 64, HALF), vm(2, 2, 64, HALF)],
        (z0, aux, xsum, rdia, xq0, idx),
    )
    z1, yq0, yq1, send = call(
        second_kernel,
        [field, sides, sides, ((2, 2, 64, HALF), f32)],
        [vm(2, 512, HALF), vm(2, 2, 64, HALF), vm(2, 2, 64, HALF)],
        (vxz, dens, z0, pz1, rdia, aux, xsum, first, second, idx, cidx),
        alias={3: 0},
    )
    first, second = swap(send, "dev")
    (pz2,) = call(
        second_rest_kernel,
        [field],
        [vm(2, 2, 64, HALF), vm(2, 2, 64, HALF)],
        (z1, aux, xsum, rdia, yq1, idx),
    )
    col1, xs, mom1 = call(
        column_first_kernel,
        [((3, 2, 64, HALF), f32), ((2, 2, 64, HALF), f32), ((2, 3, 8, HALF), f32)],
        [vm(2, 2, 2, 64, HALF), vm(3, 2, 64, HALF), vm(2, 3, 2, 64, HALF)],
        (vxz, vy, dens, z0, z1, dia, aux, xq0, yq0, yq1, idx),
    )
    z2, xq1, xq2, xcol, send = call(
        third_kernel,
        [field, sides, sides, ((2, 2, 32, HALF), f32), ((2, 3, 64, HALF), f32)],
        [],
        (vy, dens, z0, z1, pz2, rdia, aux, xsum, xhr, first, second, idx, cidx, mom1),
        alias={4: 0},
    )
    first, second = swap(send, "grp")
    col, mom, ynear = call(
        column_kernel,
        [((4, 2, 64, HALF), f32), ((2, 3, 8, HALF), f32), sides],
        [vm(2, 2, 64, HALF), vm(1, 2, 64, HALF), vm(2, 2, 64, HALF)],
        (z1, z2, dia, aux, xsum, xq1, xq2, xcol, col1, xs, idx),
    )
    yq2, send, col = call(
        functools.partial(y_kernel, tiles),
        [sides, ((sources, 1, HALF), f32), ((4, 2, 64, HALF), f32)],
        [vm(2, 2, 64, HALF)],
        (z0, z1, z2, aux, col, mom1, mom, ynear, first, second, idx, ids),
    )
    moments = lax.all_to_all(send, everyone, 0, 0, tiled=True)
    send, coef = call(
        functools.partial(pack_kernel, tiles, cap, fold),
        [((sources, 8, HALF), f32), ((8, HALF), f32)],
        [],
        (moments, col, tidx),
    )
    got = lax.all_to_all(send, everyone, 0, 0, tiled=True)
    width = sources // fold * HALF
    vout, image = call(
        functools.partial(final_kernel, fold),
        [((3, 512, count), f32), ((1, height * BLOCKS), f32)],
        [vm(3, 512, count), vm(2, 512, HALF), pltpu.VMEM((BLOCKS, width), bf16),
         pltpu.VMEM((48, width), bf16), pltpu.SemaphoreType.DMA((4,))],
        (got, moments, coef, vxz, vy, inv, z0, z1, z2, xq0, xq1, xq2, yq0, yq1, yq2, idx),
        limit=10 + width // 1024,
        final=True,
    )
    return vout, image


def solution(mesh):
    return jax.shard_map(
        shards,
        mesh=mesh,
        in_specs=(
            P(None, None, ("grp", "dev")),
            P(None, ("grp", "dev")),
            P(None, ("grp", "dev")),
            P(None, ("grp", "dev")),
            P(("grp", "dev")),
            P(("grp", "dev"), None),
            P(("grp", "dev")),
            P(),
        ),
        out_specs=(P(None, None, ("grp", "dev")), P("dev", "grp")),
        check_vma=False,
    )
```

```python
import functools

import jax
import jax.numpy as jnp
from jax import lax
from jax.experimental import pallas as pl
from jax.experimental.pallas import tpu as pltpu
from jax.sharding import PartitionSpec as P

BLOCKS = 256
HALF = 128
SLOTS = 64
ADVECT = 0.2
RAY = 0.03

f32 = jnp.float32
bf16 = jnp.bfloat16
i32 = jnp.int32


def iota(shape, axis):
    return lax.broadcasted_iota(i32, shape, axis)


def take(table, lane):
    index = jnp.broadcast_to(lane, table.shape)
    return jnp.take_along_axis(table, index, axis=1, mode="promise_in_bounds")


def pick(low, high, lane, code, other):
    near = jnp.where(code == 1, take(low, lane), take(high, lane))
    return jnp.where((code == 1) | (code == 2), near, other)


def pick_remote(packed, lane, second):
    return take(packed, lane + second * SLOTS)


def packed_pair(first, second, lane, code):
    ga = jnp.where(code == 2, take(first[1], lane), take(first[0], lane))
    gb = jnp.where(code == 2, take(second[1], lane), take(second[0], lane))
    left = iota((1, HALF), 1) < SLOTS
    return jnp.where(left, ga, gb)


def packed_fold(parts, lane, code):
    half = parts[0].shape[0] // 2
    return packed_pair([p[:half] for p in parts], [p[half:] for p in parts], lane, code)


def pick_fold(packed, lane):
    return jnp.concatenate([take(packed, lane), take(packed, lane + SLOTS)], axis=0)


def ends(slab, low, high):
    down = jnp.concatenate([low, slab[:-8]], axis=0)
    up = jnp.concatenate([slab[8:], high], axis=0)
    return down, up


def turns(slab, low, high):
    n = slab.shape[0]
    row = iota((1, 8, 1), 1)
    down = jnp.where(row == 0, low.reshape(n, 1, HALF), pltpu.roll(slab, 1, 1))
    up = jnp.where(row == 7, high.reshape(n, 1, HALF), pltpu.roll(slab, 7, 1))
    return down, up


def zturns(slab, low, high):
    down, up = turns(slab.reshape(8, 8, HALF), low, high)
    return down.reshape(64, HALF), up.reshape(64, HALF)


def face_y(read, j):
    return jnp.concatenate([read(64 * i + 8 * j, 8) for i in range(8)], axis=0)


def odd_on(axis):
    return lax.axis_index(axis) & 1


def slot_of(n, odd):
    return (n + 1 + odd) & 1


def both_sides(first_ref, second_ref, odd):
    first, second = first_ref[...], second_ref[...]
    is_odd = jnp.broadcast_to(odd, first.shape) == 1
    return jnp.where(is_odd, first, second), jnp.where(is_odd, second, first)


def lanes(h):
    return slice(h * HALF, (h + 1) * HALF)


def link_lists(nb, dirs, dev_size):
    count = nb.shape[1]
    me = lax.axis_index("grp") * dev_size + lax.axis_index("dev")
    base = nb - me * count
    present = nb >= 0
    local = present & (base >= 0) & (base < count)
    remote = present & jnp.logical_not(local)
    slot = nb & (count - 1)
    code = jnp.where(local, jnp.where(slot < HALF, 1, 2), jnp.where(remote, 3, 0))
    rem = remote[0:4].astype(f32)
    key = jnp.where(remote[0:4], slot[0:4], 2 * count).astype(f32)
    cols = jnp.concatenate([rem, key], axis=0).T
    tri = (iota((count, count), 1) <= iota((count, count), 0)).astype(bf16)
    upto = jnp.dot(tri, cols.astype(bf16), preferred_element_type=f32)
    target = (iota((1, HALF), 1) & (SLOTS - 1)).astype(f32)
    lists = []
    for f in dirs:
        listed = (upto[:, f : f + 1] <= target).astype(f32)
        lists.append(jnp.sum(listed, axis=0, keepdims=True).astype(i32))
    listing = jnp.concatenate(lists, axis=0)
    clane = listing & (HALF - 1)
    ccode = jnp.where(listing < HALF, 1, jnp.where(listing < count, 2, 0))
    return code, slot, remote, key, cols, clane, ccode


def load_kernel(
    dev_size, v_any, w_any, nb_any, vy_ref, w_ref, nb_ref, send_ref, sems,
):
    copies = [
        pltpu.make_async_copy(nb_any, nb_ref, sems.at[0]),
        pltpu.make_async_copy(v_any.at[1], vy_ref, sems.at[1]),
        pltpu.make_async_copy(w_any, w_ref, sems.at[2]),
    ]
    for c in copies:
        c.start()
    copies[0].wait()
    clane, ccode = link_lists(nb_ref[...], (2, 3), dev_size)[-2:]
    copies[1].wait()
    copies[2].wait()
    for n, j in ((0, 0), (1, 7)):
        send_ref[slot_of(n, odd_on("grp"))] = packed_pair(
            [face_y(lambda r, m: vy_ref[r : r + m, lanes(h)], j) for h in range(2)],
            [face_y(lambda r, m: w_ref[r : r + m, lanes(h)], j) for h in range(2)],
            clane[n : n + 1], ccode[n : n + 1])


def index_kernel(
    dev_size, v_any, dens_any, layer_any, tile_any, block_any, samples_any, nb_ref,
    vxz_ref, dens_ref, idx_ref, cidx_ref, small_ref, samples_ref, sems,
):
    copies = [
        pltpu.make_async_copy(layer_any, small_ref.at[0:1], sems.at[3]),
        pltpu.make_async_copy(tile_any, small_ref.at[1:2], sems.at[4]),
        pltpu.make_async_copy(block_any, small_ref.at[2:3], sems.at[5]),
        pltpu.make_async_copy(samples_any, samples_ref, sems.at[6]),
        pltpu.make_async_copy(v_any.at[0], vxz_ref.at[0], sems.at[0]),
        pltpu.make_async_copy(v_any.at[2], vxz_ref.at[1], sems.at[1]),
        pltpu.make_async_copy(dens_any, dens_ref, sems.at[2]),
    ]
    for c in copies:
        c.start()
    count = nb_ref.shape[1]
    code, slot, remote, key, cols, clane, ccode = link_lists(nb_ref[...], range(4), dev_size)
    lane = slot & (HALF - 1)
    ranks = []
    for f in range(4):
        below = (cols[:, 4 + f : 5 + f] < key[f : f + 1, :]).astype(f32)
        ranks.append(jnp.sum(below, axis=0, keepdims=True).astype(i32))
    rank = jnp.concatenate(ranks, axis=0)
    lane4 = jnp.where(remote[0:4], rank & (SLOTS - 1), lane[0:4])
    zero2 = jnp.zeros((2, count), i32)
    idx_ref[0:8, :] = jnp.concatenate([lane4, lane[4:6], zero2], axis=0)
    idx_ref[8:16, :] = jnp.concatenate([code, zero2], axis=0)
    cidx_ref[...] = jnp.concatenate([clane, ccode], axis=0)
    for c in copies:
        c.wait()


def tile_kernel(cap, reps, small, samples_ref, after_ref, tidx_ref, ids_ref):
    count = small.shape[1]
    tiles = samples_ref.shape[1]
    rows = jnp.concatenate([small[0:1], small[1:2], small[2:3], jnp.zeros((5, count), i32)], axis=0)
    rows = rows.astype(f32)
    cols = rows.T
    tile = cols[:, 1:2]
    hot = tile == iota((count, tiles), 1).astype(f32)
    limit = jnp.sum(jnp.where(hot, samples_ref[...].astype(f32), 0.0), axis=1, keepdims=True)
    marched = cols[:, 0:1] < limit
    hot = hot & marched
    tri = (iota((count, count), 1) <= iota((count, count), 0)).astype(bf16)
    upto = jnp.dot(tri, hot.astype(bf16), preferred_element_type=f32)
    rank = jnp.sum(jnp.where(hot, upto, 0.0), axis=1, keepdims=True) - 1.0
    place = jnp.where(marched, tile * cap + rank, -1.0)
    place = jnp.broadcast_to(place, (count, HALF))
    lane_id = iota((1, HALF), 1)
    used = lane_id < cap * reps
    slot = (lane_id & (cap - 1)).astype(f32)
    listed = jnp.concatenate(
        [(place == jnp.where(used, slot + float(t * cap), -2.0)).astype(bf16)
         for t in range(tiles)], axis=1)
    leaf = iota((1, count), 1).astype(f32)
    table = jnp.concatenate([leaf, rows[2:3], jnp.ones((1, count), f32),
                             jnp.zeros((13, count), f32)], axis=0).astype(bf16)
    found = jnp.dot(table, listed, preferred_element_type=f32)
    for t in range(tiles):
        at = slice(t * HALF, (t + 1) * HALF)
        there = found[2:3, at] > 0.5
        listing = found[0:1, at].astype(i32)
        tidx_ref[t : t + 1, :] = listing & (HALF - 1)
        tidx_ref[tiles + t : tiles + t + 1, :] = jnp.where(
            there, jnp.where(listing < HALF, 1, 2), 0)
        ids_ref[t : t + 1, :] = jnp.where(there, found[1:2, at], -1.0)


def tables(idx_ref):
    lane = [[idx_ref[f : f + 1, lanes(h)] for h in range(2)] for f in range(6)]
    code = [[idx_ref[8 + f : 9 + f, lanes(h)] for h in range(2)] for f in range(6)]
    return lane, code


def edge_kernel(
    vxz_ref, vy_ref, w_ref, first_ref, second_ref, idx_ref, cidx_ref,
    src_ref, dia_ref, send_ref, zs,
):
    lane, code = tables(idx_ref)
    sides = both_sides(first_ref, second_ref, odd_on("grp"))
    for h in range(2):
        for n, start in ((0, 0), (1, 448)):
            rows = slice(start, start + 64)
            zs[0, h, 64 * n : 64 * n + 64] = vxz_ref[1, rows, lanes(h)]
            zs[1, h, 64 * n : 64 * n + 64] = w_ref[rows, lanes(h)]
    for n, start, inner, far_side in ((0, 0, 64, 448), (1, 448, 384, 0)):
        rows = slice(start, start + 64)
        small = slice(start // 8, start // 8 + 8)

        def tabs(read):
            return [read(h) for h in range(2)]

        for h in range(2):
            def face(f, v_tab, w_tab, w_own):
                ln, cd = lane[f][h], code[f][h]
                v_far, w_far = 0.0, jnp.where(cd == 3, 0.0, w_own)
                if f in (2, 3):
                    got = sides[f - 2][small]
                    v_far = jnp.where(cd == 3, pick_remote(got, ln, 0), 0.0)
                    w_far = jnp.where(cd == 3, pick_remote(got, ln, 1), w_own)
                return (pick(v_tab[0], v_tab[1], ln, cd, v_far),
                        pick(w_tab[0], w_tab[1], ln, cd, w_far))

            w = w_ref[rows, lanes(h)]
            far = slice(far_side, far_side + 64)
            next_rows = slice(inner, inner + 64)
            vx, wx = face(n, tabs(lambda g: vxz_ref[0, far, lanes(g)]),
                          tabs(lambda g: w_ref[far, lanes(g)]), w)
            sign = 1.0 if n == 0 else -1.0
            src = sign * (vxz_ref[0, next_rows, lanes(h)] - vx)
            dia = wx + w_ref[next_rows, lanes(h)]
            faces = []
            for f, j in ((2, 7), (3, 0)):
                at = slice(start + 8 * j, start + 8 * j + 8)
                mine = start + 56 - 8 * j
                faces.append(face(f, tabs(lambda g: vy_ref[ at, lanes(g)]),
                                  tabs(lambda g: w_ref[at, lanes(g)]),
                                  w_ref[mine : mine + 8, lanes(h)]))
            v_dn, v_up = ends(vy_ref[ rows, lanes(h)], faces[0][0], faces[1][0])
            w_dn, w_up = ends(w, faces[0][1], faces[1][1])
            src = src + (v_up - v_dn)
            dia = dia + (w_up + w_dn)
            faces = []
            for f, k in ((4, 7), (5, 0)):
                faces.append(face(f, tabs(lambda g: zs[0, g, pl.ds(64 * n + k, 8, stride=8), :]),
                                  tabs(lambda g: zs[1, g, pl.ds(64 * n + k, 8, stride=8), :]),
                                  zs[1, h, pl.ds(64 * n + 7 - k, 8, stride=8), :]))
            v_dn, v_up = zturns(vxz_ref[1, rows, lanes(h)], faces[0][0], faces[1][0])
            w_dn, w_up = zturns(w, faces[0][1], faces[1][1])
            src_ref[n, h] = -0.5 * (src + (v_up - v_dn))
            dia_ref[n, h] = 3.0 * w + 0.5 * (dia + (w_up + w_dn))
        cl, cc = cidx_ref[n : n + 1, :], cidx_ref[4 + n : 5 + n, :]
        slot = slot_of(n, odd_on("dev"))
        send_ref[slot, 0] = packed_pair(
            [vxz_ref[0, rows, lanes(h)] for h in range(2)],
            [w_ref[rows, lanes(h)] for h in range(2)], cl, cc)
        send_ref[slot, 1] = packed_pair(
            [src_ref[n, h] for h in range(2)], [dia_ref[n, h] for h in range(2)], cl, cc)


def inner_kernel(
    vxz_ref, vy_ref, w_ref, dens_ref, first_ref, second_ref, idx_ref, cidx_ref,
    psrc_ref, pdia_ref, aux_ref, xface_ref, zs, vface, face,
):
    lane, code = tables(idx_ref)
    sides = both_sides(first_ref, second_ref, odd_on("grp"))
    for h in range(2):
        zs[0, h] = vxz_ref[1, :, lanes(h)]
        zs[1, h] = w_ref[:, lanes(h)]
    v_tab, w_tab, w_own = {}, {}, {}
    for h in range(2):
        for f, start in ((0, 448), (1, 0)):
            w_tab[f, h] = w_ref[start : start + 64, lanes(h)]
            w_own[1 - f, h] = w_tab[f, h]
        for f, j in ((2, 7), (3, 0)):
            v_tab[f, h] = face_y(lambda r, n: vy_ref[ r : r + n, lanes(h)], j)
            w_tab[f, h] = face_y(lambda r, n: w_ref[r : r + n, lanes(h)], j)
            w_own[5 - f, h] = w_tab[f, h]
        for f, k in ((4, 7), (5, 0)):
            v_tab[f, h] = zs[0, h, pl.ds(k, 64, stride=8), :]
            w_tab[f, h] = zs[1, h, pl.ds(k, 64, stride=8), :]
            w_own[9 - f, h] = w_tab[f, h]
    for f in range(6):
        for h in range(2):
            ln, cd = lane[f][h], code[f][h]
            w_far = jnp.where(cd == 3, 0.0, w_own[f, h])
            v_far = 0.0
            if f in (2, 3):
                got = sides[f - 2]
                v_far = jnp.where(cd == 3, pick_remote(got, ln, 0), 0.0)
                w_far = jnp.where(cd == 3, pick_remote(got, ln, 1), w_own[f, h])
            w_face = pick(w_tab[f, 0], w_tab[f, 1], ln, cd, w_far)
            if f < 2:
                xface_ref[f, h] = w_face
            else:
                face[f - 2, h] = w_face
                vface[f - 2, h] = pick(v_tab[f, 0], v_tab[f, 1], ln, cd, v_far)
    for h in range(2):
        for i in range(8):
            rows = slice(64 * i, 64 * i + 64)
            small = slice(8 * i, 8 * i + 8)
            w = w_ref[rows, lanes(h)]
            wy_dn, wy_up = ends(w, face[0, h, small], face[1, h, small])
            wz_dn, wz_up = zturns(w, face[2, h, small], face[3, h, small])
            aux_ref[1, h, rows] = w + wy_dn
            aux_ref[2, h, rows] = w + wy_up
            aux_ref[3, h, rows] = w + wz_dn
            aux_ref[4, h, rows] = w + wz_up
            aux_ref[5, h, rows] = 0.5 * dens_ref[rows, lanes(h)] * w
            if i < 7:
                aux_ref[0, h, rows] = w + w_ref[64 * i + 64 : 64 * i + 128, lanes(h)]
            if i in (0, 7):
                continue
            below, above = slice(64 * i - 64, 64 * i), slice(64 * i + 64, 64 * i + 128)
            vy_dn, vy_up = ends(vy_ref[ rows, lanes(h)], vface[0, h, small], vface[1, h, small])
            vz_dn, vz_up = zturns(vxz_ref[1, rows, lanes(h)], vface[2, h, small], vface[3, h, small])
            vx = vxz_ref[0, above, lanes(h)] - vxz_ref[0, below, lanes(h)]
            psrc_ref[h, rows] = -0.5 * (vx + (vy_up - vy_dn) + (vz_up - vz_dn))
            wx = w_ref[above, lanes(h)] + w_ref[below, lanes(h)]
            pdia_ref[h, rows] = 3.0 * w + 0.5 * (wx + (wy_up + wy_dn) + (wz_up + wz_dn))


def z_faces(q_ref, lane, code, zface, layers=()):
    for i in layers:
        for f, k in ((4, 7), (5, 0)):
            tabs = [q_ref[h, pl.ds(64 * i + k, 8, stride=8), :] for h in range(2)]
            for h in range(2):
                zface[f - 4, h, 8 * i : 8 * i + 8] = pick(
                    tabs[0], tabs[1], lane[f][h], code[f][h], 0.0)
    if layers:
        return
    for f, k in ((4, 7), (5, 0)):
        tabs = [q_ref[h, pl.ds(k, 64, stride=8), :] for h in range(2)]
        for h in range(2):
            zface[f - 4, h] = pick(tabs[0], tabs[1], lane[f][h], code[f][h], 0.0)


def x_terms(q_ref, aux_ref, xsum_ref, xface, h, i):
    if i == 0:
        dn, c_dn = xface[0, h], xsum_ref[0, h]
    else:
        below = slice(64 * i - 64, 64 * i)
        dn, c_dn = q_ref[h, below], aux_ref[0, h, below]
    if i == 7:
        up, c_up = xface[1, h], xsum_ref[1, h]
    else:
        up, c_up = q_ref[h, 64 * i + 64 : 64 * i + 128], aux_ref[0, h, 64 * i : 64 * i + 64]
    return dn, up, c_dn * dn + c_up * up


def products(q_ref, aux_ref, xsum_ref, rdia_ref, xface, yface, zface, out_ref, layers=range(8)):
    for h in range(2):
        for i in layers:
            rows = slice(64 * i, 64 * i + 64)
            small = slice(8 * i, 8 * i + 8)
            q = q_ref[h, rows]
            total = x_terms(q_ref, aux_ref, xsum_ref, xface, h, i)[2]
            dn, up = ends(q, yface[0, h, small], yface[1, h, small])
            total = total + (aux_ref[1, h, rows] * dn + aux_ref[2, h, rows] * up)
            dn, up = zturns(q, zface[0, h, small], zface[1, h, small])
            total = total + (aux_ref[3, h, rows] * dn + aux_ref[4, h, rows] * up)
            out_ref[h, rows] = (0.5 * rdia_ref[h, rows]) * total


def first_kernel(
    vxz_ref, w_ref, psrc_ref, pdia_ref, esrc_ref, edia_ref, aux_ref, xface_ref,
    first_ref, second_ref, idx_ref, cidx_ref, after_ref,
    dia_ref, z0_ref, rdia_ref, xsum_ref, xq_ref, xhr_ref, send_ref,
):
    lane, code = tables(idx_ref)
    sides = both_sides(first_ref, second_ref, odd_on("dev"))
    for h in range(2):
        for i in range(1, 7):
            rows = slice(64 * i, 64 * i + 64)
            rdia = 1.0 / dia_ref[h, rows]
            rdia_ref[h, rows] = rdia
            z0_ref[h, rows] = psrc_ref[h, rows] * rdia
        for f, start, sign in ((0, 0, 0.5), (1, 448, -0.5)):
            rows = slice(start, start + 64)
            got = sides[f]
            ln, cd = lane[f][h], code[f][h]
            far = cd == 3
            v_m = jnp.where(far, pick_remote(got[0], ln, 0), 0.0)
            w_m = jnp.where(far, pick_remote(got[0], ln, 1), 0.0)
            src_m = jnp.where(far, pick_remote(got[1], ln, 0), 0.0)
            dia_m = jnp.where(far, pick_remote(got[1], ln, 1), 1.0)
            w = w_ref[rows, lanes(h)]
            dia = edia_ref[f, h] + 0.5 * w_m
            rdia = 1.0 / dia
            dia_ref[h, rows] = dia
            rdia_ref[h, rows] = rdia
            z0_ref[h, rows] = (esrc_ref[f, h] + sign * v_m) * rdia
            rdia_m = 1.0 / (dia_m + 0.5 * w)
            z0_m = (src_m - sign * vxz_ref[0, rows, lanes(h)]) * rdia_m
            xhr_ref[f, h] = rdia_m
            xq_ref[f, h] = jnp.where(far, z0_m, 0.0)
            xsum_ref[f, h] = w + jnp.where(far, w_m, xface_ref[f, h])
    for f, start in ((0, 448), (1, 0)):
        tabs = [z0_ref[h, start : start + 64] for h in range(2)]
        for h in range(2):
            xq_ref[f, h] = pick(tabs[0], tabs[1], lane[f][h], code[f][h], xq_ref[f, h])
    z1f = {}
    for n, f, j, there, inner in ((0, 2, 0, 7, 1), (1, 3, 7, 0, 6)):
        tabs = [face_y(lambda r, m: z0_ref[h, r : r + m], there) for h in range(2)]
        at = slice(8 * j, 8 * j + 8)
        for h in range(2):
            q = face_y(lambda r, m: z0_ref[h, r : r + m], j)
            c = face_y(lambda r, m: aux_ref[0, h, r : r + m], j)[:56]
            c_dn = jnp.concatenate([xsum_ref[0, h, at], c], axis=0)
            c_up = jnp.concatenate([c, xsum_ref[1, h, at]], axis=0)
            dn, up = ends(q, xq_ref[0, h, at], xq_ref[1, h, at])
            total = c_dn * dn + c_up * up
            near = pick(tabs[0], tabs[1], lane[f][h], code[f][h], 0.0)
            next_q = face_y(lambda r, m: z0_ref[h, r : r + m], inner)
            c_near = face_y(lambda r, m: aux_ref[1 + n, h, r : r + m], j)
            c_next = face_y(lambda r, m: aux_ref[2 - n, h, r : r + m], j)
            total = total + (c_near * near + c_next * next_q)
            zf = []
            for g, k in ((4, 7), (5, 0)):
                rows = [z0_ref[e, pl.ds(8 * j + k, 8, stride=64), :] for e in range(2)]
                zf.append(pick(rows[0], rows[1], lane[g][h], code[g][h], 0.0))
            dn, up = zturns(q, zf[0], zf[1])
            c_dn = face_y(lambda r, m: aux_ref[3, h, r : r + m], j)
            c_up = face_y(lambda r, m: aux_ref[4, h, r : r + m], j)
            total = total + (c_dn * dn + c_up * up)
            z1f[n, h] = (0.5 * face_y(lambda r, m: rdia_ref[h, r : r + m], j)) * total
    for n, j in ((0, 0), (1, 7)):
        cl, cc = cidx_ref[2 + n : 3 + n, :], cidx_ref[6 + n : 7 + n, :]
        z0f = [face_y(lambda r, m: z0_ref[h, r : r + m], j) for h in range(2)]
        rdf = [face_y(lambda r, m: rdia_ref[h, r : r + m], j) for h in range(2)]
        slot = slot_of(n, odd_on("grp"))
        kf = [face_y(lambda r, m: aux_ref[5, h, r : r + m], j) for h in range(2)]
        send_ref[slot, 0:64] = packed_pair(z0f, [z1f[n, 0], z1f[n, 1]], cl, cc)
        send_ref[slot, 64:96] = packed_fold(rdf, cl, cc)
        send_ref[slot, 96:128] = packed_fold(kf, cl, cc)


def first_rest_kernel(
    z0_ref, aux_ref, xsum_ref, rdia_ref, xq_ref, idx_ref, pz1_ref, yface, zface,
):
    lane, code = tables(idx_ref)
    for f, j in ((2, 7), (3, 0)):
        tabs = [face_y(lambda r, n: z0_ref[h, r : r + n], j) for h in range(2)]
        for h in range(2):
            yface[f - 2, h] = pick(tabs[0], tabs[1], lane[f][h], code[f][h], 0.0)
    z_faces(z0_ref, lane, code, zface)
    products(z0_ref, aux_ref, xsum_ref, rdia_ref, xq_ref, yface, zface, pz1_ref)


def second_kernel(
    vxz_ref, dens_ref, z0_ref, pz1_ref, rdia_ref, aux_ref, xsum_ref,
    first_ref, second_ref, idx_ref, cidx_ref,
    z1_ref, yq0_ref, yq1_ref, ky_ref, send_ref, pz2_ref, xface, zface,
):
    lane, code = tables(idx_ref)
    sides = both_sides(first_ref, second_ref, odd_on("grp"))
    for h in range(2):
        for f, j in ((2, 0), (3, 7)):
            got = sides[f - 2]
            ln, cd = lane[f][h], code[f][h]
            far = cd == 3
            z0_m = jnp.where(far, pick_remote(got[0:64], ln, 0), 0.0)
            z1_m = pick_remote(got[0:64], ln, 1)
            rd_m = pick_fold(got[64:96], ln)
            ky_ref[f - 2, h] = pick_fold(got[96:128], ln)
            yq0_ref[f - 2, h] = z0_m
            w_sum = 0.5 * face_y(lambda r, n: aux_ref[f - 1, h, r : r + n], j)
            z0_l = face_y(lambda r, n: z0_ref[h, r : r + n], j)
            rd_l = face_y(lambda r, n: rdia_ref[h, r : r + n], j)
            yq1_ref[f - 2, h] = jnp.where(far, z1_m + rd_m * w_sum * z0_l, 0.0)
            extra = rd_l * w_sum * z0_m
            for i in range(8):
                rows = slice(64 * i + 8 * j, 64 * i + 8 * j + 8)
                z1_ref[h, rows] = z1_ref[h, rows] + extra[8 * i : 8 * i + 8]
    for f, start in ((0, 448), (1, 0)):
        tabs = [z1_ref[h, start : start + 64] for h in range(2)]
        for h in range(2):
            xface[f, h] = pick(tabs[0], tabs[1], lane[f][h], code[f][h], 0.0)
    for f, j in ((2, 7), (3, 0)):
        for q_ref, out in ((z0_ref, yq0_ref), (z1_ref, yq1_ref)):
            tabs = [face_y(lambda r, n: q_ref[h, r : r + n], j) for h in range(2)]
            for h in range(2):
                out[f - 2, h] = pick(tabs[0], tabs[1], lane[f][h], code[f][h], out[f - 2, h])
    layers = (0, 1, 6, 7)
    z_faces(z1_ref, lane, code, zface, layers)
    products(z1_ref, aux_ref, xsum_ref, rdia_ref, xface, yq1_ref, zface, pz2_ref, layers)
    for n, start, inner in ((0, 0, 64), (1, 448, 384)):
        cl, cc = cidx_ref[n : n + 1, :], cidx_ref[4 + n : 5 + n, :]
        rows, next_rows = slice(start, start + 64), slice(inner, inner + 64)
        z1f = [z1_ref[h, rows] for h in range(2)]
        z2f = [pz2_ref[h, rows] for h in range(2)]
        kf, sums = [], []
        for h in range(2):
            k = aux_ref[5, h, rows]
            parts = [k * q[h, next_rows] for q in (z0_ref, z1_ref, pz2_ref)]
            parts.append(dens_ref[rows, lanes(h)] * vxz_ref[0, rows, lanes(h)])
            summed = [over_j(p) for p in parts]
            kf.append(k)
            sums.append(jnp.concatenate(summed, axis=0))
        slot = slot_of(n, odd_on("dev"))
        send_ref[slot, 0:64] = packed_pair(z1f, z2f, cl, cc)
        send_ref[slot, 64:96] = packed_fold(kf, cl, cc)
        send_ref[slot, 96:112] = packed_fold(sums, cl, cc)


def second_rest_kernel(
    z1_ref, aux_ref, xsum_ref, rdia_ref, yq1_ref, idx_ref, pz2_ref, xface, zface,
):
    lane, code = tables(idx_ref)
    for f, start in ((0, 448), (1, 0)):
        tabs = [z1_ref[h, start : start + 64] for h in range(2)]
        for h in range(2):
            xface[f, h] = pick(tabs[0], tabs[1], lane[f][h], code[f][h], 0.0)
    z_faces(z1_ref, lane, code, zface)
    products(z1_ref, aux_ref, xsum_ref, rdia_ref, xface, yq1_ref, zface, pz2_ref)


def third_kernel(
    vy_ref, dens_ref, z0_ref, z1_ref, pz2_ref, rdia_ref, aux_ref, xsum_ref, xhr_ref,
    first_ref, second_ref, idx_ref, cidx_ref, after_ref,
    z2_ref, xq1_ref, xq2_ref, xcol_ref, send_ref,
):
    lane, code = tables(idx_ref)
    sides = both_sides(first_ref, second_ref, odd_on("dev"))
    for h in range(2):
        for f, start in ((0, 0), (1, 448)):
            rows = slice(start, start + 64)
            got = sides[f]
            ln, cd = lane[f][h], code[f][h]
            far = cd == 3
            z1_m = jnp.where(far, pick_remote(got[0:64], ln, 0), 0.0)
            z2_m = pick_remote(got[0:64], ln, 1)
            k_m = pick_fold(got[64:96], ln)
            sums = pick_fold(got[96:112], ln)
            w_sum = 0.5 * xsum_ref[f, h]
            xq1_ref[f, h] = z1_m
            xq2_ref[f, h] = jnp.where(far, z2_m + xhr_ref[f, h] * w_sum * z1_ref[h, rows], 0.0)
            z2_l = z2_ref[h, rows] + rdia_ref[h, rows] * w_sum * z1_m
            z2_ref[h, rows] = z2_l
            sign = 1.0 if f == 0 else -1.0
            for c, q in enumerate((z0_ref[h, rows], z1_ref[h, rows], z2_l)):
                mine = over_j(k_m * q)
                xcol_ref[f, h, 8 * c + 8 : 8 * c + 16] = sign * (sums[8 * c : 8 * c + 8] - mine)
            xcol_ref[f, h, 0:8] = sums[24:32]
    for f, start in ((0, 448), (1, 0)):
        for q_ref, out in ((z1_ref, xq1_ref), (z2_ref, xq2_ref)):
            tabs = [q_ref[h, start : start + 64] for h in range(2)]
            for h in range(2):
                out[f, h] = pick(tabs[0], tabs[1], lane[f][h], code[f][h], out[f, h])
    for n, j, inner in ((0, 0, 1), (1, 7, 6)):
        cl, cc = cidx_ref[2 + n : 3 + n, :], cidx_ref[6 + n : 7 + n, :]
        kf, vf = [], []
        for h in range(2):
            dens = face_y(lambda r, m: dens_ref[r : r + m, lanes(h)], j)
            kf.append(face_y(lambda r, m: aux_ref[5, h, r : r + m], j))
            vf.append(dens * face_y(lambda r, m: vy_ref[ r : r + m, lanes(h)], j))
        z2f = [face_y(lambda r, m: z2_ref[h, r : r + m], j) for h in range(2)]
        inners = [
            [kf[h] * face_y(lambda r, m: q[h, r : r + m], inner) for h in range(2)]
            for q in (z0_ref, z1_ref, z2_ref)
        ]
        slot = slot_of(n, odd_on("grp"))
        send_ref[slot, 0:64] = packed_pair(z2f, inners[2], cl, cc)
        send_ref[slot, 64:128] = packed_pair(inners[0], inners[1], cl, cc)
        send_ref[slot, 128:160] = packed_fold(vf, cl, cc)


def over_j(a):
    return jnp.sum(a.reshape(8, 8, HALF), axis=0)


def column_first_kernel(
    vxz_ref, vy_ref, dens_ref, z0_ref, z1_ref, dia_ref, aux_ref, xq0_ref, yq0_ref, yq1_ref, idx_ref,
    col_ref, xs_ref, mom_ref,
    zface, zsum, fy,
):
    lane, code = tables(idx_ref)
    basis = (z0_ref, z1_ref)
    for c in range(2):
        z_faces(basis[c], lane, code, zface.at[c])
    for h in range(2):
        mu = [jnp.zeros((8, HALF), f32) for _ in range(3)]
        for i in range(8):
            rows = slice(64 * i, 64 * i + 64)
            small = slice(8 * i, 8 * i + 8)
            dens = dens_ref[rows, lanes(h)]
            kk = aux_ref[5, h, rows]
            xs_ref[0, h, small] = over_j(dens * vxz_ref[0, rows, lanes(h)])
            zsum[0, h, small] = over_j(dens * vxz_ref[1, rows, lanes(h)])
            col_ref[0, h, small] = over_j(dens)
            q = [basis[c][h, rows] for c in range(2)]
            dn = xq0_ref[0, h] if i == 0 else z0_ref[h, 64 * i - 64 : 64 * i]
            up = xq0_ref[1, h] if i == 7 else z0_ref[h, 64 * i + 64 : 64 * i + 128]
            xs_ref[1, h, small] = over_j(kk * (dn - up))
            for c in range(2):
                zdn, zup = zturns(q[c], zface[c, 0, h, small], zface[c, 1, h, small])
                zsum[c + 1, h, small] = over_j(kk * (zdn - zup))
            dia = dia_ref[h, rows]
            d0, d1 = dia * q[0], dia * q[1]
            mu[0] = mu[0] + over_j(d0 * q[0])
            mu[1] = mu[1] + over_j(d0 * q[1])
            mu[2] = mu[2] + over_j(d1 * q[1])
        for n in range(3):
            mom_ref[h, n] = mu[n]
    scale = RAY * 0.5 * ADVECT
    yq = (yq0_ref, yq1_ref)
    for h in range(2):
        for n, j, inner in ((0, 0, 1), (1, 7, 6)):
            dens = face_y(lambda r, m: dens_ref[r : r + m, lanes(h)], j)
            kk = face_y(lambda r, m: aux_ref[5, h, r : r + m], j)
            fy[n, 0, h] = dens * face_y(lambda r, m: vy_ref[r : r + m, lanes(h)], j)
            for c in range(2):
                near = face_y(lambda r, m: basis[c][h, r : r + m], inner)
                out = yq[c][n, h]
                fy[n, c + 1, h] = kk * ((out - near) if n == 0 else (near - out))
    for c in range(3):
        for h in range(2):
            change = z_change(zsum, c, h, lane, code) + (fy[1, c, h] - fy[0, c, h])
            for n in range(2):
                value = pick(fy[1 - n, c, 0], fy[1 - n, c, 1], lane[2 + n][h], code[2 + n][h], 0.0)
                change = change + value if n == 1 else change - value
            if c == 0:
                col_ref[c, h] = RAY * col_ref[c, h] - scale * change
            else:
                col_ref[c, h] = -scale * change


def z_change(zsum, c, h, lane, code):
    zf = []
    for f, k in ((4, 7), (5, 0)):
        tabs = [zsum[c, g, pl.ds(k, 8, stride=8), :] for g in range(2)]
        zf.append(pick(tabs[0], tabs[1], lane[f][h], code[f][h], 0.0))
    down, up = turns(zsum[c, h].reshape(8, 8, HALF), zf[0], zf[1])
    return (up - down).reshape(64, HALF)


def column_kernel(
    z1_ref, z2_ref, dia_ref, aux_ref, xsum_ref, xq1_ref, xq2_ref, xcol_ref, part_ref, xs_ref, idx_ref,
    col_ref, mom_ref, ynear_ref,
    zface, zsum, xsum,
):
    lane, code = tables(idx_ref)
    for f, j in ((2, 7), (3, 0)):
        tabs = [face_y(lambda r, n: z2_ref[h, r : r + n], j) for h in range(2)]
        for h in range(2):
            ynear_ref[f - 2, h] = pick(tabs[0], tabs[1], lane[f][h], code[f][h], 0.0)
    z_faces(z2_ref, lane, code, zface)
    for h in range(2):
        mu = [jnp.zeros((8, HALF), f32) for _ in range(3)]
        for i in range(8):
            rows = slice(64 * i, 64 * i + 64)
            small = slice(8 * i, 8 * i + 8)
            kk = aux_ref[5, h, rows]
            dn = xq1_ref[0, h] if i == 0 else z1_ref[h, 64 * i - 64 : 64 * i]
            up = xq1_ref[1, h] if i == 7 else z1_ref[h, 64 * i + 64 : 64 * i + 128]
            xsum[0, h, small] = over_j(kk * (dn - up))
            q = z2_ref[h, rows]
            dn, up, total = x_terms(z2_ref, aux_ref, xsum_ref, xq2_ref, h, i)
            xsum[1, h, small] = over_j(kk * (dn - up))
            dn, up = zturns(q, zface[0, h, small], zface[1, h, small])
            zsum[0, h, small] = over_j(kk * (dn - up))
            total = total + (aux_ref[3, h, rows] * dn + aux_ref[4, h, rows] * up)
            dn, up = ends(q, ynear_ref[0, h, small], ynear_ref[1, h, small])
            total = total + (aux_ref[1, h, rows] * dn + aux_ref[2, h, rows] * up)
            d2 = dia_ref[h, rows] * q
            mu[0] = mu[0] + over_j(d2 * z1_ref[h, rows])
            mu[1] = mu[1] + over_j(d2 * q)
            mu[2] = mu[2] + over_j(0.5 * total * q)
        for n in range(3):
            mom_ref[h, n] = mu[n]
    scale = RAY * 0.5 * ADVECT
    for c in range(4):
        for h in range(2):
            sums = [xs_ref[c, g] if c < 2 else xsum[c - 2, g] for g in range(2)]
            faces = []
            for f, start in ((0, 56), (1, 0)):
                far = jnp.where(code[f][h] == 3, xcol_ref[f, h, 8 * c : 8 * c + 8], 0.0)
                faces.append(pick(sums[0][start : start + 8], sums[1][start : start + 8],
                                  lane[f][h], code[f][h], far))
            down, up = ends(sums[h], faces[0], faces[1])
            if c < 3:
                col_ref[c, h] = part_ref[c, h] - scale * (up - down)
            else:
                col_ref[c, h] = -scale * ((up - down) + z_change(zsum, 0, h, lane, code))


def y_kernel(
    tiles, z0_ref, z1_ref, z2_ref, aux_ref, ky_ref,
    col_ref, mom1_ref, mom_ref, ynear_ref, first_ref, second_ref, idx_ref, ids_ref,
    yq2_ref, send_ref, out_ref, fy,
):
    lane, code = tables(idx_ref)
    basis = (z0_ref, z1_ref, z2_ref)
    sides = both_sides(first_ref, second_ref, odd_on("grp"))
    extra = jnp.zeros((64, HALF), f32)
    for h in range(2):
        for n, j, inner in ((0, 0, 1), (1, 7, 6)):
            ln, cd = lane[2 + n][h], code[2 + n][h]
            far = jnp.where(cd == 3, pick_remote(sides[n][0:64], ln, 0), 0.0)
            out = ynear_ref[n, h] + far
            yq2_ref[n, h] = out
            z2 = face_y(lambda r, m: z2_ref[h, r : r + m], j)
            w_sum = 0.5 * face_y(lambda r, m: aux_ref[1 + n, h, r : r + m], j)
            extra = extra + w_sum * (far * z2)
            kk = face_y(lambda r, m: aux_ref[5, h, r : r + m], j)
            near = face_y(lambda r, m: z2_ref[h, r : r + m], inner)
            fy[n, h] = kk * ((out - near) if n == 0 else (near - out))
    scale = RAY * 0.5 * ADVECT
    for h in range(2):
        change = [None, None, None, fy[1, h] - fy[0, h]]
        for n, j in ((0, 0), (1, 7)):
            got = sides[n]
            ln, cd = lane[2 + n][h], code[2 + n][h]
            far = cd == 3
            k_m = ky_ref[n, h]
            for c in range(4):
                if c == 0:
                    other = pick_fold(got[128:160], ln)
                else:
                    at, second = ((64, 0), (64, 1), (0, 1))[c - 1]
                    inner = pick_remote(got[at : at + 64], ln, second)
                    mine = k_m * face_y(lambda r, m: basis[c - 1][h, r : r + m], j)
                    other = (mine - inner) if n == 1 else (inner - mine)
                value = jnp.where(far, other, 0.0)
                if c == 3:
                    value = pick(fy[1 - n, 0], fy[1 - n, 1], ln, cd, value)
                value = value if n == 1 else -value
                change[c] = value if change[c] is None else change[c] + value
        for c in range(4):
            out_ref[c, h] = col_ref[c, h] - scale * change[c]
    parts = [m[0, n] + m[1, n] for m in (mom1_ref, mom_ref) for n in range(3)]
    parts[5] = parts[5] + over_j(extra)
    which = iota((1, HALF), 1)
    row = jnp.zeros((1, HALF), f32)
    for n, m in enumerate(parts):
        total = jnp.sum(jnp.sum(m, axis=0, keepdims=True), axis=1, keepdims=True)
        row = jnp.where(which == n, total, row)
    g_count = send_ref.shape[0] // tiles
    for t in range(tiles):
        names = pltpu.roll(ids_ref[t : t + 1, :], SLOTS, 1)
        line = jnp.where(which < SLOTS, row, names)
        for g in range(g_count):
            send_ref[t * g_count + g] = line


def coefficients(mu):
    def dot(a, b):
        total = None
        for i, x in enumerate(a):
            for j, y in enumerate(b):
                if x is None or y is None:
                    continue
                term = x * y * mu[i + j]
                total = term if total is None else total + term
        return total

    one = jnp.ones_like(mu[0])
    residual = [one]
    direction = [one]
    energy = mu[0]
    pressure = [None, None, None]
    for iteration in range(3):
        image = [direction[0]]
        for n in range(1, len(direction)):
            image.append(direction[n] - direction[n - 1])
        image.append(-direction[-1])
        step = energy / dot(direction, image)
        for n, d in enumerate(direction):
            pressure[n] = step * d if pressure[n] is None else pressure[n] + step * d
        if iteration < 2:
            old = residual + [None]
            residual = []
            for n, im in enumerate(image):
                residual.append(-step * im if old[n] is None else old[n] - step * im)
            fresh = dot(residual, residual)
            beta = fresh / energy
            energy = fresh
            longer = direction + [None]
            direction = [
                r if d is None else r + beta * d for r, d in zip(residual, longer)
            ]
    return pressure


def pack_kernel(tiles, cap, fold, got_ref, col_ref, tidx_ref, send_ref, coef_ref):
    sources = got_ref.shape[0]
    total = got_ref[0]
    for s in range(1, sources):
        total = total + got_ref[s]
    coef = coefficients([jnp.broadcast_to(total[:, n : n + 1], (1, HALF)) for n in range(6)])
    coef_ref[...] = jnp.concatenate(coef + [jnp.zeros((5, HALF), f32)], axis=0)
    full = []
    for h in range(2):
        value = col_ref[0, h]
        for n in range(3):
            value = value + coef[n] * col_ref[n + 1, h]
        full.append(value)
    g_count = sources // tiles
    height = 64 // g_count
    left = iota((1, HALF), 1) < cap
    for t in range(tiles):
        ln = tidx_ref[t : t + 1, :]
        cd = tidx_ref[tiles + t : tiles + t + 1, :]
        value = pick(full[0], full[1], ln, cd, 0.0)
        for g in range(g_count):
            part = value[g * height : g * height + height]
            if fold == 2:
                part = jnp.where(left, part[0:8], part[8:16])
            send_ref[t * g_count + g] = part


def final_kernel(
    fold, got_ref, names_ref, coef_ref, vxz_ref, vy_ref, w_ref, z0_ref, z1_ref, z2_ref,
    xq0_ref, xq1_ref, xq2_ref, yq0_ref, yq1_ref, yq2_ref, idx_ref,
    vout_any, image_ref, vout, p, sems,
):
    coef = [coef_ref[n : n + 1, :] for n in range(3)]
    lane, code = tables(idx_ref)

    def pressure(i):
        rows = slice(64 * i, 64 * i + 64)
        for h in range(2):
            p[h, rows] = (
                coef[0] * z0_ref[h, rows] + coef[1] * z1_ref[h, rows] + coef[2] * z2_ref[h, rows])

    def blend(refs, n, h, at):
        return coef[0] * refs[0][n, h, at] + coef[1] * refs[1][n, h, at] + coef[2] * refs[2][n, h, at]

    sources, height = got_ref.shape[0], 8 * fold
    left = iota((1, HALF), 1) < HALF // 2
    blocks_id = iota((BLOCKS, 2 * HALF), 0).astype(f32).astype(bf16)
    one, zero = jnp.ones((), bf16), jnp.zeros((), bf16)

    def chunk_image(chunk):
        pieces, names = [], []
        for s in range(chunk, chunk + 2 * fold, fold):
            value = got_ref[s]
            after_ids = names_ref[s + 1] if fold == 2 else -1.0
            names.append(jnp.where(left, pltpu.roll(names_ref[s], HALF // 2, 1), after_ids))
            if fold == 2:
                after = got_ref[s + 1]
                value = jnp.concatenate(
                    [jnp.where(left, value, pltpu.roll(after, HALF // 2, 1)),
                     jnp.where(left, pltpu.roll(value, HALF // 2, 1), after)], axis=0)
            high = value.astype(bf16)
            rest = value - high.astype(f32)
            middle = rest.astype(bf16)
            low = (rest - middle.astype(f32)).astype(bf16)
            pieces.append(jnp.concatenate([high, middle, low], axis=0))
        ids = jnp.broadcast_to(jnp.concatenate(names, axis=1), (16, 2 * HALF)).astype(bf16)
        ids = jnp.concatenate([ids] * (BLOCKS // 16), axis=0)
        hot = jnp.where(blocks_id == ids, one, zero)
        product = lax.dot_general(
            jnp.concatenate(pieces, axis=1), hot, (((1,), (1,)), ((), ())),
            preferred_element_type=f32)
        return product[0:height] + (
            product[height : 2 * height] + product[2 * height : 3 * height])

    optical = jnp.zeros((height, BLOCKS), f32)
    chunks = list(range(0, sources, 2 * fold))
    turn = -(-len(chunks) // 8)
    xq, yq = (xq0_ref, xq1_ref, xq2_ref), (yq0_ref, yq1_ref, yq2_ref)
    copies = []
    pressure(0)
    for i in range(8):
        if i < 7:
            pressure(i + 1)
        rows = slice(64 * i, 64 * i + 64)
        small = slice(8 * i, 8 * i + 8)
        tabs = [[p[h, pl.ds(64 * i + k, 8, stride=8), :] for h in range(2)] for k in (7, 0)]
        for h in range(2):
            w = 0.5 * w_ref[rows, lanes(h)]
            mine = p[h, rows]
            dn = blend(xq, 0, h, slice(0, 64)) if i == 0 else p[h, 64 * i - 64 : 64 * i]
            up = blend(xq, 1, h, slice(0, 64)) if i == 7 else p[h, 64 * i + 64 : 64 * i + 128]
            vout[0, rows, lanes(h)] = vxz_ref[0, rows, lanes(h)] - w * (up - dn)
            dn, up = ends(mine, blend(yq, 0, h, small), blend(yq, 1, h, small))
            vout[1, rows, lanes(h)] = vy_ref[rows, lanes(h)] - w * (up - dn)
            zf = [pick(tabs[n][0], tabs[n][1], lane[4 + n][h], code[4 + n][h], 0.0) for n in range(2)]
            dn, up = zturns(mine, zf[0], zf[1])
            vout[2, rows, lanes(h)] = vxz_ref[1, rows, lanes(h)] - w * (up - dn)
        copies.append(pltpu.make_async_copy(vout.at[:, rows], vout_any.at[:, rows], sems.at[i]))
        copies[i].start()
        for chunk in chunks[i * turn : (i + 1) * turn]:
            optical = optical + chunk_image(chunk)

    shade = 1.0 - jnp.exp(-optical)
    for m in range(height):
        image_ref[0:1, m * BLOCKS : (m + 1) * BLOCKS] = shade[m : m + 1, :]
    for c in copies:
        c.wait()


def call(kernel, outs, scratch, args, any_args=0, limit=10, final=False, alias=None):
    spaces = [pltpu.HBM if n < any_args else pltpu.VMEM for n in range(len(args))]
    out_specs = [pl.BlockSpec(memory_space=pltpu.VMEM) for _ in outs]
    if final:
        out_specs[0] = pl.BlockSpec(memory_space=pltpu.HBM)
    return pl.pallas_call(
        kernel,
        out_shape=[jax.ShapeDtypeStruct(s, d) if final else pltpu.VMEM(s, d) for s, d in outs],
        in_specs=[pl.BlockSpec(memory_space=space) for space in spaces],
        out_specs=out_specs,
        scratch_shapes=scratch,
        input_output_aliases=alias or {},
        compiler_params=pltpu.CompilerParams(vmem_limit_bytes=limit * 1024 * 1024),
    )(*[pltpu.with_memory_space_constraint(a, space) for a, space in zip(args, spaces)])


def swap(packed, axis):
    count = lax.axis_size(axis)
    results = []
    for start in range(2):
        pairs = [(i, i + 1) for i in range(start, count - 1, 2)]
        results.append(lax.ppermute(packed[start], axis, pairs + [(b, a) for a, b in pairs]))
    return results


def shards(
    velocity, density, inverse_density, neighbours, leaf_layer, leaf_tile, leaf_block, samples
):
    count = density.shape[1]
    tiles = samples.shape[0]
    grp_size, dev_size = lax.axis_size("grp"), lax.axis_size("dev")
    cap = 2 * count // tiles
    height = 64 // grp_size
    fold = min(height // 8, HALF // cap)
    sources = grp_size * dev_size
    everyone = ("dev", "grp")

    field = ((2, 512, HALF), f32)
    sides = ((2, 2, 64, HALF), f32)

    def vm(*shape):
        return pltpu.VMEM(shape, f32)

    vy, inv, nb, send = call(
        functools.partial(load_kernel, dev_size),
        [((512, count), f32), ((512, count), f32), ((6, count), i32), ((2, 64, HALF), f32)],
        [pltpu.SemaphoreType.DMA((3,))],
        (velocity, inverse_density, neighbours),
        any_args=3,
    )
    first, second = swap(send, "grp")
    vxz, dens, idx, cidx, small, limits = call(
        functools.partial(index_kernel, dev_size),
        [((2, 512, count), f32), ((512, count), f32), ((16, count), i32), ((8, HALF), i32),
         ((8, count), i32), ((1, tiles), i32)],
        [pltpu.SemaphoreType.DMA((7,))],
        (velocity, density, leaf_layer.reshape(1, count), leaf_tile.reshape(1, count),
         leaf_block.reshape(1, count), samples.reshape(1, tiles), nb),
        any_args=6,
    )
    esrc, edia, send = call(
        edge_kernel,
        [sides, sides, ((2, 2, 64, HALF), f32)],
        [vm(2, 2, HALF, HALF)],
        (vxz, vy, inv, first, second, idx, cidx),
    )
    got_first, got_second = swap(send, "dev")
    psrc, pdia, aux, xface = call(
        inner_kernel,
        [field, field, ((6, 2, 512, HALF), f32), sides],
        [vm(2, 2, 512, HALF), vm(4, 2, 64, HALF), vm(4, 2, 64, HALF)],
        (vxz, vy, inv, dens, first, second, idx, cidx),
    )
    tidx, ids = call(
        functools.partial(tile_kernel, cap, fold),
        [((2 * tiles, HALF), i32), ((tiles, HALF), f32)],
        [],
        (small, limits, esrc),
    )
    dia, z0, rdia, xsum, xq0, xhr, send = call(
        first_kernel,
        [field, field, field, sides, sides, sides, ((2, 128, HALF), f32)],
        [],
        (vxz, inv, psrc, pdia, esrc, edia, aux, xface, got_first, got_second, idx, cidx, ids),
        alias={3: 0},
    )
    first, second = swap(send, "grp")
    (pz1,) = call(
        first_rest_kernel,
        [field],
        [vm(2, 2, 64, HALF), vm(2, 2, 64, HALF)],
        (z0, aux, xsum, rdia, xq0, idx),
    )
    z1, yq0, yq1, ky, send = call(
        second_kernel,
        [field, sides, sides, sides, ((2, 112, HALF), f32)],
        [vm(2, 512, HALF), vm(2, 2, 64, HALF), vm(2, 2, 64, HALF)],
        (vxz, dens, z0, pz1, rdia, aux, xsum, first, second, idx, cidx),
        alias={3: 0},
    )
    first, second = swap(send, "dev")
    (pz2,) = call(
        second_rest_kernel,
        [field],
        [vm(2, 2, 64, HALF), vm(2, 2, 64, HALF)],
        (z1, aux, xsum, rdia, yq1, idx),
    )
    col1, xs, mom1 = call(
        column_first_kernel,
        [((3, 2, 64, HALF), f32), ((2, 2, 64, HALF), f32), ((2, 3, 8, HALF), f32)],
        [vm(2, 2, 2, 64, HALF), vm(3, 2, 64, HALF), vm(2, 3, 2, 64, HALF)],
        (vxz, vy, dens, z0, z1, dia, aux, xq0, yq0, yq1, idx),
    )
    z2, xq1, xq2, xcol, send = call(
        third_kernel,
        [field, sides, sides, ((2, 2, 32, HALF), f32), ((2, 160, HALF), f32)],
        [],
        (vy, dens, z0, z1, pz2, rdia, aux, xsum, xhr, first, second, idx, cidx, mom1),
        alias={4: 0},
    )
    first, second = swap(send, "grp")
    col, mom, ynear = call(
        column_kernel,
        [((4, 2, 64, HALF), f32), ((2, 3, 8, HALF), f32), sides],
        [vm(2, 2, 64, HALF), vm(1, 2, 64, HALF), vm(2, 2, 64, HALF)],
        (z1, z2, dia, aux, xsum, xq1, xq2, xcol, col1, xs, idx),
    )
    yq2, send, col = call(
        functools.partial(y_kernel, tiles),
        [sides, ((sources, 1, HALF), f32), ((4, 2, 64, HALF), f32)],
        [vm(2, 2, 64, HALF)],
        (z0, z1, z2, aux, ky, col, mom1, mom, ynear, first, second, idx, ids),
    )
    moments = lax.all_to_all(send, everyone, 0, 0, tiled=True)
    send, coef = call(
        functools.partial(pack_kernel, tiles, cap, fold),
        [((sources, 8, HALF), f32), ((8, HALF), f32)],
        [],
        (moments, col, tidx),
    )
    got = lax.all_to_all(send, everyone, 0, 0, tiled=True)
    vout, image = call(
        functools.partial(final_kernel, fold),
        [((3, 512, count), f32), ((1, height * BLOCKS), f32)],
        [vm(3, 512, count), vm(2, 512, HALF), pltpu.SemaphoreType.DMA((8,))],
        (got, moments, coef, vxz, vy, inv, z0, z1, z2, xq0, xq1, xq2, yq0, yq1, yq2, idx),
        final=True,
    )
    return vout, image


def solution(mesh):
    return jax.shard_map(
        shards,
        mesh=mesh,
        in_specs=(
            P(None, None, ("grp", "dev")),
            P(None, ("grp", "dev")),
            P(None, ("grp", "dev")),
            P(None, ("grp", "dev")),
            P(("grp", "dev")),
            P(("grp", "dev"), None),
            P(("grp", "dev")),
            P(),
        ),
        out_specs=(P(None, None, ("grp", "dev")), P("dev", "grp")),
        check_vma=False,
    )
```

```python
import functools

import jax
import jax.numpy as jnp
from jax import lax
from jax.experimental import pallas as pl
from jax.experimental.pallas import tpu as pltpu
from jax.sharding import PartitionSpec as P

BLOCKS = 256
HALF = 128
SLOTS = 64
ADVECT = 0.2
RAY = 0.03

f32 = jnp.float32
bf16 = jnp.bfloat16
i32 = jnp.int32


def iota(shape, axis):
    return lax.broadcasted_iota(i32, shape, axis)


def take(table, lane):
    index = jnp.broadcast_to(lane, table.shape)
    return jnp.take_along_axis(table, index, axis=1, mode="promise_in_bounds")


def pick(low, high, lane, code, other):
    near = jnp.where(code == 1, take(low, lane), take(high, lane))
    return jnp.where((code == 1) | (code == 2), near, other)


def pick_remote(packed, lane, second):
    return take(packed, lane + second * SLOTS)


def packed_pair(first, second, lane, code):
    ga = jnp.where(code == 2, take(first[1], lane), take(first[0], lane))
    gb = jnp.where(code == 2, take(second[1], lane), take(second[0], lane))
    left = iota((1, HALF), 1) < SLOTS
    return jnp.where(left, ga, gb)


def packed_fold(parts, lane, code):
    half = parts[0].shape[0] // 2
    return packed_pair([p[:half] for p in parts], [p[half:] for p in parts], lane, code)


def pick_fold(packed, lane):
    return jnp.concatenate([take(packed, lane), take(packed, lane + SLOTS)], axis=0)


def ends(slab, low, high):
    down = jnp.concatenate([low, slab[:-8]], axis=0)
    up = jnp.concatenate([slab[8:], high], axis=0)
    return down, up


def turns(slab, low, high):
    n = slab.shape[0]
    row = iota((1, 8, 1), 1)
    down = jnp.where(row == 0, low.reshape(n, 1, HALF), pltpu.roll(slab, 1, 1))
    up = jnp.where(row == 7, high.reshape(n, 1, HALF), pltpu.roll(slab, 7, 1))
    return down, up


def zturns(slab, low, high):
    down, up = turns(slab.reshape(8, 8, HALF), low, high)
    return down.reshape(64, HALF), up.reshape(64, HALF)


def face_y(read, j):
    return jnp.concatenate([read(64 * i + 8 * j, 8) for i in range(8)], axis=0)


def odd_on(axis):
    return lax.axis_index(axis) & 1


def slot_of(n, odd):
    return (n + 1 + odd) & 1


def both_sides(first_ref, second_ref, odd):
    first, second = first_ref[...], second_ref[...]
    is_odd = jnp.broadcast_to(odd, first.shape) == 1
    return jnp.where(is_odd, first, second), jnp.where(is_odd, second, first)


def lanes(h):
    return slice(h * HALF, (h + 1) * HALF)


def link_lists(nb, dirs, dev_size):
    count = nb.shape[1]
    me = lax.axis_index("grp") * dev_size + lax.axis_index("dev")
    base = nb - me * count
    present = nb >= 0
    local = present & (base >= 0) & (base < count)
    remote = present & jnp.logical_not(local)
    slot = nb & (count - 1)
    code = jnp.where(local, jnp.where(slot < HALF, 1, 2), jnp.where(remote, 3, 0))
    rem = remote[0:4].astype(f32)
    key = jnp.where(remote[0:4], slot[0:4], 2 * count).astype(f32)
    cols = jnp.concatenate([rem, key], axis=0).T
    tri = (iota((count, count), 1) <= iota((count, count), 0)).astype(bf16)
    upto = jnp.dot(tri, cols.astype(bf16), preferred_element_type=f32)
    target = (iota((1, HALF), 1) & (SLOTS - 1)).astype(f32)
    lists = []
    for f in dirs:
        listed = (upto[:, f : f + 1] <= target).astype(f32)
        lists.append(jnp.sum(listed, axis=0, keepdims=True).astype(i32))
    listing = jnp.concatenate(lists, axis=0)
    clane = listing & (HALF - 1)
    ccode = jnp.where(listing < HALF, 1, jnp.where(listing < count, 2, 0))
    return code, slot, remote, key, cols, clane, ccode


def load_kernel(
    dev_size, v_any, w_any, nb_any, vy_ref, w_ref, nb_ref, send_ref, sems,
):
    copies = [
        pltpu.make_async_copy(nb_any, nb_ref, sems.at[0]),
        pltpu.make_async_copy(v_any.at[1], vy_ref, sems.at[1]),
        pltpu.make_async_copy(w_any, w_ref, sems.at[2]),
    ]
    for c in copies:
        c.start()
    copies[0].wait()
    clane, ccode = link_lists(nb_ref[...], (2, 3), dev_size)[-2:]
    copies[1].wait()
    copies[2].wait()
    for n, j in ((0, 0), (1, 7)):
        send_ref[slot_of(n, odd_on("grp"))] = packed_pair(
            [face_y(lambda r, m: vy_ref[r : r + m, lanes(h)], j) for h in range(2)],
            [face_y(lambda r, m: w_ref[r : r + m, lanes(h)], j) for h in range(2)],
            clane[n : n + 1], ccode[n : n + 1])


def index_kernel(
    dev_size, v_any, dens_any, layer_any, tile_any, block_any, samples_any, nb_ref,
    vxz_ref, dens_ref, idx_ref, cidx_ref, small_ref, samples_ref, sems,
):
    copies = [
        pltpu.make_async_copy(layer_any, small_ref.at[0:1], sems.at[3]),
        pltpu.make_async_copy(tile_any, small_ref.at[1:2], sems.at[4]),
        pltpu.make_async_copy(block_any, small_ref.at[2:3], sems.at[5]),
        pltpu.make_async_copy(samples_any, samples_ref, sems.at[6]),
        pltpu.make_async_copy(v_any.at[0], vxz_ref.at[0], sems.at[0]),
        pltpu.make_async_copy(v_any.at[2], vxz_ref.at[1], sems.at[1]),
        pltpu.make_async_copy(dens_any, dens_ref, sems.at[2]),
    ]
    for c in copies:
        c.start()
    count = nb_ref.shape[1]
    code, slot, remote, key, cols, clane, ccode = link_lists(nb_ref[...], range(4), dev_size)
    lane = slot & (HALF - 1)
    ranks = []
    for f in range(4):
        below = (cols[:, 4 + f : 5 + f] < key[f : f + 1, :]).astype(f32)
        ranks.append(jnp.sum(below, axis=0, keepdims=True).astype(i32))
    rank = jnp.concatenate(ranks, axis=0)
    lane4 = jnp.where(remote[0:4], rank & (SLOTS - 1), lane[0:4])
    zero2 = jnp.zeros((2, count), i32)
    idx_ref[0:8, :] = jnp.concatenate([lane4, lane[4:6], zero2], axis=0)
    idx_ref[8:16, :] = jnp.concatenate([code, zero2], axis=0)
    cidx_ref[...] = jnp.concatenate([clane, ccode], axis=0)
    for c in copies:
        c.wait()


def tile_kernel(cap, reps, small, samples_ref, after_ref, tidx_ref, ids_ref):
    count = small.shape[1]
    tiles = samples_ref.shape[1]
    rows = jnp.concatenate([small[0:1], small[1:2], small[2:3], jnp.zeros((5, count), i32)], axis=0)
    rows = rows.astype(f32)
    cols = rows.T
    tile = cols[:, 1:2]
    hot = tile == iota((count, tiles), 1).astype(f32)
    limit = jnp.sum(jnp.where(hot, samples_ref[...].astype(f32), 0.0), axis=1, keepdims=True)
    marched = cols[:, 0:1] < limit
    hot = hot & marched
    tri = (iota((count, count), 1) <= iota((count, count), 0)).astype(bf16)
    upto = jnp.dot(tri, hot.astype(bf16), preferred_element_type=f32)
    rank = jnp.sum(jnp.where(hot, upto, 0.0), axis=1, keepdims=True) - 1.0
    place = jnp.where(marched, tile * cap + rank, -1.0)
    place = jnp.broadcast_to(place, (count, HALF))
    lane_id = iota((1, HALF), 1)
    used = lane_id < cap * reps
    slot = (lane_id & (cap - 1)).astype(f32)
    listed = jnp.concatenate(
        [(place == jnp.where(used, slot + float(t * cap), -2.0)).astype(bf16)
         for t in range(tiles)], axis=1)
    leaf = iota((1, count), 1).astype(f32)
    table = jnp.concatenate([leaf, rows[2:3], jnp.ones((1, count), f32),
                             jnp.zeros((13, count), f32)], axis=0).astype(bf16)
    found = jnp.dot(table, listed, preferred_element_type=f32)
    for t in range(tiles):
        at = slice(t * HALF, (t + 1) * HALF)
        there = found[2:3, at] > 0.5
        listing = found[0:1, at].astype(i32)
        tidx_ref[t : t + 1, :] = listing & (HALF - 1)
        tidx_ref[tiles + t : tiles + t + 1, :] = jnp.where(
            there, jnp.where(listing < HALF, 1, 2), 0)
        ids_ref[t : t + 1, :] = jnp.where(there, found[1:2, at], -1.0)


def tables(idx_ref):
    lane = [[idx_ref[f : f + 1, lanes(h)] for h in range(2)] for f in range(6)]
    code = [[idx_ref[8 + f : 9 + f, lanes(h)] for h in range(2)] for f in range(6)]
    return lane, code


def edge_kernel(
    vxz_ref, vy_ref, w_ref, first_ref, second_ref, idx_ref, cidx_ref,
    src_ref, dia_ref, send_ref, zs,
):
    lane, code = tables(idx_ref)
    sides = both_sides(first_ref, second_ref, odd_on("grp"))
    for h in range(2):
        for n, start in ((0, 0), (1, 448)):
            rows = slice(start, start + 64)
            zs[0, h, 64 * n : 64 * n + 64] = vxz_ref[1, rows, lanes(h)]
            zs[1, h, 64 * n : 64 * n + 64] = w_ref[rows, lanes(h)]
    for n, start, inner, far_side in ((0, 0, 64, 448), (1, 448, 384, 0)):
        rows = slice(start, start + 64)
        small = slice(start // 8, start // 8 + 8)

        def tabs(read):
            return [read(h) for h in range(2)]

        for h in range(2):
            def face(f, v_tab, w_tab, w_own):
                ln, cd = lane[f][h], code[f][h]
                v_far, w_far = 0.0, jnp.where(cd == 3, 0.0, w_own)
                if f in (2, 3):
                    got = sides[f - 2][small]
                    v_far = jnp.where(cd == 3, pick_remote(got, ln, 0), 0.0)
                    w_far = jnp.where(cd == 3, pick_remote(got, ln, 1), w_own)
                return (pick(v_tab[0], v_tab[1], ln, cd, v_far),
                        pick(w_tab[0], w_tab[1], ln, cd, w_far))

            w = w_ref[rows, lanes(h)]
            far = slice(far_side, far_side + 64)
            next_rows = slice(inner, inner + 64)
            vx, wx = face(n, tabs(lambda g: vxz_ref[0, far, lanes(g)]),
                          tabs(lambda g: w_ref[far, lanes(g)]), w)
            sign = 1.0 if n == 0 else -1.0
            src = sign * (vxz_ref[0, next_rows, lanes(h)] - vx)
            dia = wx + w_ref[next_rows, lanes(h)]
            faces = []
            for f, j in ((2, 7), (3, 0)):
                at = slice(start + 8 * j, start + 8 * j + 8)
                mine = start + 56 - 8 * j
                faces.append(face(f, tabs(lambda g: vy_ref[ at, lanes(g)]),
                                  tabs(lambda g: w_ref[at, lanes(g)]),
                                  w_ref[mine : mine + 8, lanes(h)]))
            v_dn, v_up = ends(vy_ref[ rows, lanes(h)], faces[0][0], faces[1][0])
            w_dn, w_up = ends(w, faces[0][1], faces[1][1])
            src = src + (v_up - v_dn)
            dia = dia + (w_up + w_dn)
            faces = []
            for f, k in ((4, 7), (5, 0)):
                faces.append(face(f, tabs(lambda g: zs[0, g, pl.ds(64 * n + k, 8, stride=8), :]),
                                  tabs(lambda g: zs[1, g, pl.ds(64 * n + k, 8, stride=8), :]),
                                  zs[1, h, pl.ds(64 * n + 7 - k, 8, stride=8), :]))
            v_dn, v_up = zturns(vxz_ref[1, rows, lanes(h)], faces[0][0], faces[1][0])
            w_dn, w_up = zturns(w, faces[0][1], faces[1][1])
            src_ref[n, h] = -0.5 * (src + (v_up - v_dn))
            dia_ref[n, h] = 3.0 * w + 0.5 * (dia + (w_up + w_dn))
        cl, cc = cidx_ref[n : n + 1, :], cidx_ref[4 + n : 5 + n, :]
        slot = slot_of(n, odd_on("dev"))
        send_ref[slot, 0] = packed_pair(
            [vxz_ref[0, rows, lanes(h)] for h in range(2)],
            [w_ref[rows, lanes(h)] for h in range(2)], cl, cc)
        send_ref[slot, 1] = packed_pair(
            [src_ref[n, h] for h in range(2)], [dia_ref[n, h] for h in range(2)], cl, cc)


def inner_kernel(
    vxz_ref, vy_ref, w_ref, dens_ref, first_ref, second_ref, idx_ref, cidx_ref,
    psrc_ref, pdia_ref, aux_ref, xface_ref, zs, vface, face,
):
    lane, code = tables(idx_ref)
    sides = both_sides(first_ref, second_ref, odd_on("grp"))
    for h in range(2):
        zs[0, h] = vxz_ref[1, :, lanes(h)]
        zs[1, h] = w_ref[:, lanes(h)]
    v_tab, w_tab, w_own = {}, {}, {}
    for h in range(2):
        for f, start in ((0, 448), (1, 0)):
            w_tab[f, h] = w_ref[start : start + 64, lanes(h)]
            w_own[1 - f, h] = w_tab[f, h]
        for f, j in ((2, 7), (3, 0)):
            v_tab[f, h] = face_y(lambda r, n: vy_ref[ r : r + n, lanes(h)], j)
            w_tab[f, h] = face_y(lambda r, n: w_ref[r : r + n, lanes(h)], j)
            w_own[5 - f, h] = w_tab[f, h]
        for f, k in ((4, 7), (5, 0)):
            v_tab[f, h] = zs[0, h, pl.ds(k, 64, stride=8), :]
            w_tab[f, h] = zs[1, h, pl.ds(k, 64, stride=8), :]
            w_own[9 - f, h] = w_tab[f, h]
    for f in range(6):
        for h in range(2):
            ln, cd = lane[f][h], code[f][h]
            w_far = jnp.where(cd == 3, 0.0, w_own[f, h])
            v_far = 0.0
            if f in (2, 3):
                got = sides[f - 2]
                v_far = jnp.where(cd == 3, pick_remote(got, ln, 0), 0.0)
                w_far = jnp.where(cd == 3, pick_remote(got, ln, 1), w_own[f, h])
            w_face = pick(w_tab[f, 0], w_tab[f, 1], ln, cd, w_far)
            if f < 2:
                xface_ref[f, h] = w_face
            else:
                face[f - 2, h] = w_face
                vface[f - 2, h] = pick(v_tab[f, 0], v_tab[f, 1], ln, cd, v_far)
    for h in range(2):
        for i in range(8):
            rows = slice(64 * i, 64 * i + 64)
            small = slice(8 * i, 8 * i + 8)
            w = w_ref[rows, lanes(h)]
            wy_dn, wy_up = ends(w, face[0, h, small], face[1, h, small])
            wz_dn, wz_up = zturns(w, face[2, h, small], face[3, h, small])
            aux_ref[1, h, rows] = w + wy_dn
            aux_ref[2, h, rows] = w + wy_up
            aux_ref[3, h, rows] = w + wz_dn
            aux_ref[4, h, rows] = w + wz_up
            aux_ref[5, h, rows] = 0.5 * dens_ref[rows, lanes(h)] * w
            if i < 7:
                aux_ref[0, h, rows] = w + w_ref[64 * i + 64 : 64 * i + 128, lanes(h)]
            if i in (0, 7):
                continue
            below, above = slice(64 * i - 64, 64 * i), slice(64 * i + 64, 64 * i + 128)
            vy_dn, vy_up = ends(vy_ref[ rows, lanes(h)], vface[0, h, small], vface[1, h, small])
            vz_dn, vz_up = zturns(vxz_ref[1, rows, lanes(h)], vface[2, h, small], vface[3, h, small])
            vx = vxz_ref[0, above, lanes(h)] - vxz_ref[0, below, lanes(h)]
            psrc_ref[h, rows] = -0.5 * (vx + (vy_up - vy_dn) + (vz_up - vz_dn))
            wx = w_ref[above, lanes(h)] + w_ref[below, lanes(h)]
            pdia_ref[h, rows] = 3.0 * w + 0.5 * (wx + (wy_up + wy_dn) + (wz_up + wz_dn))


def z_faces(q_ref, lane, code, zface, layers=()):
    for i in layers:
        for f, k in ((4, 7), (5, 0)):
            tabs = [q_ref[h, pl.ds(64 * i + k, 8, stride=8), :] for h in range(2)]
            for h in range(2):
                zface[f - 4, h, 8 * i : 8 * i + 8] = pick(
                    tabs[0], tabs[1], lane[f][h], code[f][h], 0.0)
    if layers:
        return
    for f, k in ((4, 7), (5, 0)):
        tabs = [q_ref[h, pl.ds(k, 64, stride=8), :] for h in range(2)]
        for h in range(2):
            zface[f - 4, h] = pick(tabs[0], tabs[1], lane[f][h], code[f][h], 0.0)


def x_terms(q_ref, aux_ref, xsum_ref, xface, h, i):
    if i == 0:
        dn, c_dn = xface[0, h], xsum_ref[0, h]
    else:
        below = slice(64 * i - 64, 64 * i)
        dn, c_dn = q_ref[h, below], aux_ref[0, h, below]
    if i == 7:
        up, c_up = xface[1, h], xsum_ref[1, h]
    else:
        up, c_up = q_ref[h, 64 * i + 64 : 64 * i + 128], aux_ref[0, h, 64 * i : 64 * i + 64]
    return dn, up, c_dn * dn + c_up * up


def products(q_ref, aux_ref, xsum_ref, rdia_ref, xface, yface, zface, out_ref, layers=range(8)):
    for h in range(2):
        for i in layers:
            rows = slice(64 * i, 64 * i + 64)
            small = slice(8 * i, 8 * i + 8)
            q = q_ref[h, rows]
            total = x_terms(q_ref, aux_ref, xsum_ref, xface, h, i)[2]
            dn, up = ends(q, yface[0, h, small], yface[1, h, small])
            total = total + (aux_ref[1, h, rows] * dn + aux_ref[2, h, rows] * up)
            dn, up = zturns(q, zface[0, h, small], zface[1, h, small])
            total = total + (aux_ref[3, h, rows] * dn + aux_ref[4, h, rows] * up)
            out_ref[h, rows] = (0.5 * rdia_ref[h, rows]) * total


def first_kernel(
    vxz_ref, w_ref, psrc_ref, pdia_ref, esrc_ref, edia_ref, aux_ref, xface_ref,
    first_ref, second_ref, idx_ref, cidx_ref, after_ref,
    dia_ref, z0_ref, rdia_ref, xsum_ref, xq_ref, xhr_ref, send_ref,
):
    lane, code = tables(idx_ref)
    sides = both_sides(first_ref, second_ref, odd_on("dev"))
    for h in range(2):
        for i in range(1, 7):
            rows = slice(64 * i, 64 * i + 64)
            rdia = 1.0 / dia_ref[h, rows]
            rdia_ref[h, rows] = rdia
            z0_ref[h, rows] = psrc_ref[h, rows] * rdia
        for f, start, sign in ((0, 0, 0.5), (1, 448, -0.5)):
            rows = slice(start, start + 64)
            got = sides[f]
            ln, cd = lane[f][h], code[f][h]
            far = cd == 3
            v_m = jnp.where(far, pick_remote(got[0], ln, 0), 0.0)
            w_m = jnp.where(far, pick_remote(got[0], ln, 1), 0.0)
            src_m = jnp.where(far, pick_remote(got[1], ln, 0), 0.0)
            dia_m = jnp.where(far, pick_remote(got[1], ln, 1), 1.0)
            w = w_ref[rows, lanes(h)]
            dia = edia_ref[f, h] + 0.5 * w_m
            rdia = 1.0 / dia
            dia_ref[h, rows] = dia
            rdia_ref[h, rows] = rdia
            z0_ref[h, rows] = (esrc_ref[f, h] + sign * v_m) * rdia
            rdia_m = 1.0 / (dia_m + 0.5 * w)
            z0_m = (src_m - sign * vxz_ref[0, rows, lanes(h)]) * rdia_m
            xhr_ref[f, h] = rdia_m
            xq_ref[f, h] = jnp.where(far, z0_m, 0.0)
            xsum_ref[f, h] = w + jnp.where(far, w_m, xface_ref[f, h])
    for f, start in ((0, 448), (1, 0)):
        tabs = [z0_ref[h, start : start + 64] for h in range(2)]
        for h in range(2):
            xq_ref[f, h] = pick(tabs[0], tabs[1], lane[f][h], code[f][h], xq_ref[f, h])
    z1f = {}
    for n, f, j, there, inner in ((0, 2, 0, 7, 1), (1, 3, 7, 0, 6)):
        tabs = [face_y(lambda r, m: z0_ref[h, r : r + m], there) for h in range(2)]
        at = slice(8 * j, 8 * j + 8)
        for h in range(2):
            q = face_y(lambda r, m: z0_ref[h, r : r + m], j)
            c = face_y(lambda r, m: aux_ref[0, h, r : r + m], j)[:56]
            c_dn = jnp.concatenate([xsum_ref[0, h, at], c], axis=0)
            c_up = jnp.concatenate([c, xsum_ref[1, h, at]], axis=0)
            dn, up = ends(q, xq_ref[0, h, at], xq_ref[1, h, at])
            total = c_dn * dn + c_up * up
            near = pick(tabs[0], tabs[1], lane[f][h], code[f][h], 0.0)
            next_q = face_y(lambda r, m: z0_ref[h, r : r + m], inner)
            c_near = face_y(lambda r, m: aux_ref[1 + n, h, r : r + m], j)
            c_next = face_y(lambda r, m: aux_ref[2 - n, h, r : r + m], j)
            total = total + (c_near * near + c_next * next_q)
            zf = []
            for g, k in ((4, 7), (5, 0)):
                rows = [z0_ref[e, pl.ds(8 * j + k, 8, stride=64), :] for e in range(2)]
                zf.append(pick(rows[0], rows[1], lane[g][h], code[g][h], 0.0))
            dn, up = zturns(q, zf[0], zf[1])
            c_dn = face_y(lambda r, m: aux_ref[3, h, r : r + m], j)
            c_up = face_y(lambda r, m: aux_ref[4, h, r : r + m], j)
            total = total + (c_dn * dn + c_up * up)
            z1f[n, h] = (0.5 * face_y(lambda r, m: rdia_ref[h, r : r + m], j)) * total
    for n, j in ((0, 0), (1, 7)):
        cl, cc = cidx_ref[2 + n : 3 + n, :], cidx_ref[6 + n : 7 + n, :]
        z0f = [face_y(lambda r, m: z0_ref[h, r : r + m], j) for h in range(2)]
        rdf = [face_y(lambda r, m: rdia_ref[h, r : r + m], j) for h in range(2)]
        slot = slot_of(n, odd_on("grp"))
        kf = [face_y(lambda r, m: aux_ref[5, h, r : r + m], j) for h in range(2)]
        send_ref[slot, 0:64] = packed_pair(z0f, [z1f[n, 0], z1f[n, 1]], cl, cc)
        send_ref[slot, 64:96] = packed_fold(rdf, cl, cc)
        send_ref[slot, 96:128] = packed_fold(kf, cl, cc)


def first_rest_kernel(
    z0_ref, aux_ref, xsum_ref, rdia_ref, xq_ref, idx_ref, pz1_ref, yface, zface,
):
    lane, code = tables(idx_ref)
    for f, j in ((2, 7), (3, 0)):
        tabs = [face_y(lambda r, n: z0_ref[h, r : r + n], j) for h in range(2)]
        for h in range(2):
            yface[f - 2, h] = pick(tabs[0], tabs[1], lane[f][h], code[f][h], 0.0)
    z_faces(z0_ref, lane, code, zface)
    products(z0_ref, aux_ref, xsum_ref, rdia_ref, xq_ref, yface, zface, pz1_ref)


def second_kernel(
    vxz_ref, dens_ref, z0_ref, pz1_ref, rdia_ref, aux_ref, xsum_ref,
    first_ref, second_ref, idx_ref, cidx_ref,
    z1_ref, yq0_ref, yq1_ref, ky_ref, send_ref, pz2_ref, xface, zface,
):
    lane, code = tables(idx_ref)
    sides = both_sides(first_ref, second_ref, odd_on("grp"))
    for h in range(2):
        for f, j in ((2, 0), (3, 7)):
            got = sides[f - 2]
            ln, cd = lane[f][h], code[f][h]
            far = cd == 3
            z0_m = jnp.where(far, pick_remote(got[0:64], ln, 0), 0.0)
            z1_m = pick_remote(got[0:64], ln, 1)
            rd_m = pick_fold(got[64:96], ln)
            ky_ref[f - 2, h] = pick_fold(got[96:128], ln)
            yq0_ref[f - 2, h] = z0_m
            w_sum = 0.5 * face_y(lambda r, n: aux_ref[f - 1, h, r : r + n], j)
            z0_l = face_y(lambda r, n: z0_ref[h, r : r + n], j)
            rd_l = face_y(lambda r, n: rdia_ref[h, r : r + n], j)
            yq1_ref[f - 2, h] = jnp.where(far, z1_m + rd_m * w_sum * z0_l, 0.0)
            extra = rd_l * w_sum * z0_m
            for i in range(8):
                rows = slice(64 * i + 8 * j, 64 * i + 8 * j + 8)
                z1_ref[h, rows] = z1_ref[h, rows] + extra[8 * i : 8 * i + 8]
    for f, start in ((0, 448), (1, 0)):
        tabs = [z1_ref[h, start : start + 64] for h in range(2)]
        for h in range(2):
            xface[f, h] = pick(tabs[0], tabs[1], lane[f][h], code[f][h], 0.0)
    for f, j in ((2, 7), (3, 0)):
        for q_ref, out in ((z0_ref, yq0_ref), (z1_ref, yq1_ref)):
            tabs = [face_y(lambda r, n: q_ref[h, r : r + n], j) for h in range(2)]
            for h in range(2):
                out[f - 2, h] = pick(tabs[0], tabs[1], lane[f][h], code[f][h], out[f - 2, h])
    layers = (0, 1, 6, 7)
    z_faces(z1_ref, lane, code, zface, layers)
    products(z1_ref, aux_ref, xsum_ref, rdia_ref, xface, yq1_ref, zface, pz2_ref, layers)
    for n, start, inner in ((0, 0, 64), (1, 448, 384)):
        cl, cc = cidx_ref[n : n + 1, :], cidx_ref[4 + n : 5 + n, :]
        rows, next_rows = slice(start, start + 64), slice(inner, inner + 64)
        z1f = [z1_ref[h, rows] for h in range(2)]
        z2f = [pz2_ref[h, rows] for h in range(2)]
        kf, sums = [], []
        for h in range(2):
            k = aux_ref[5, h, rows]
            parts = [k * q[h, next_rows] for q in (z0_ref, z1_ref, pz2_ref)]
            parts.append(dens_ref[rows, lanes(h)] * vxz_ref[0, rows, lanes(h)])
            summed = [over_j(p) for p in parts]
            kf.append(k)
            sums.append(jnp.concatenate(summed, axis=0))
        slot = slot_of(n, odd_on("dev"))
        send_ref[slot, 0:64] = packed_pair(z1f, z2f, cl, cc)
        send_ref[slot, 64:96] = packed_fold(kf, cl, cc)
        send_ref[slot, 96:112] = packed_fold(sums, cl, cc)


def second_rest_kernel(
    z1_ref, aux_ref, xsum_ref, rdia_ref, yq1_ref, idx_ref, pz2_ref, xface, zface,
):
    lane, code = tables(idx_ref)
    for f, start in ((0, 448), (1, 0)):
        tabs = [z1_ref[h, start : start + 64] for h in range(2)]
        for h in range(2):
            xface[f, h] = pick(tabs[0], tabs[1], lane[f][h], code[f][h], 0.0)
    z_faces(z1_ref, lane, code, zface)
    products(z1_ref, aux_ref, xsum_ref, rdia_ref, xface, yq1_ref, zface, pz2_ref)


def third_kernel(
    vy_ref, dens_ref, z0_ref, z1_ref, pz2_ref, rdia_ref, aux_ref, xsum_ref, xhr_ref,
    first_ref, second_ref, idx_ref, cidx_ref, after_ref,
    z2_ref, xq1_ref, xq2_ref, xcol_ref, send_ref,
):
    lane, code = tables(idx_ref)
    sides = both_sides(first_ref, second_ref, odd_on("dev"))
    for h in range(2):
        for f, start in ((0, 0), (1, 448)):
            rows = slice(start, start + 64)
            got = sides[f]
            ln, cd = lane[f][h], code[f][h]
            far = cd == 3
            z1_m = jnp.where(far, pick_remote(got[0:64], ln, 0), 0.0)
            z2_m = pick_remote(got[0:64], ln, 1)
            k_m = pick_fold(got[64:96], ln)
            sums = pick_fold(got[96:112], ln)
            w_sum = 0.5 * xsum_ref[f, h]
            xq1_ref[f, h] = z1_m
            xq2_ref[f, h] = jnp.where(far, z2_m + xhr_ref[f, h] * w_sum * z1_ref[h, rows], 0.0)
            z2_l = z2_ref[h, rows] + rdia_ref[h, rows] * w_sum * z1_m
            z2_ref[h, rows] = z2_l
            sign = 1.0 if f == 0 else -1.0
            for c, q in enumerate((z0_ref[h, rows], z1_ref[h, rows], z2_l)):
                mine = over_j(k_m * q)
                xcol_ref[f, h, 8 * c + 8 : 8 * c + 16] = sign * (sums[8 * c : 8 * c + 8] - mine)
            xcol_ref[f, h, 0:8] = sums[24:32]
    for f, start in ((0, 448), (1, 0)):
        for q_ref, out in ((z1_ref, xq1_ref), (z2_ref, xq2_ref)):
            tabs = [q_ref[h, start : start + 64] for h in range(2)]
            for h in range(2):
                out[f, h] = pick(tabs[0], tabs[1], lane[f][h], code[f][h], out[f, h])
    for n, j, inner in ((0, 0, 1), (1, 7, 6)):
        cl, cc = cidx_ref[2 + n : 3 + n, :], cidx_ref[6 + n : 7 + n, :]
        kf, vf = [], []
        for h in range(2):
            dens = face_y(lambda r, m: dens_ref[r : r + m, lanes(h)], j)
            kf.append(face_y(lambda r, m: aux_ref[5, h, r : r + m], j))
            vf.append(dens * face_y(lambda r, m: vy_ref[ r : r + m, lanes(h)], j))
        z2f = [face_y(lambda r, m: z2_ref[h, r : r + m], j) for h in range(2)]
        inners = [
            [kf[h] * face_y(lambda r, m: q[h, r : r + m], inner) for h in range(2)]
            for q in (z0_ref, z1_ref, z2_ref)
        ]
        slot = slot_of(n, odd_on("grp"))
        send_ref[slot, 0:64] = packed_pair(z2f, inners[2], cl, cc)
        send_ref[slot, 64:128] = packed_pair(inners[0], inners[1], cl, cc)
        send_ref[slot, 128:160] = packed_fold(vf, cl, cc)


def over_j(a):
    return jnp.sum(a.reshape(8, 8, HALF), axis=0)


def column_first_kernel(
    vxz_ref, vy_ref, dens_ref, z0_ref, z1_ref, dia_ref, aux_ref, xq0_ref, yq0_ref, yq1_ref, idx_ref,
    col_ref, xs_ref, mom_ref,
    zface, zsum, fy,
):
    lane, code = tables(idx_ref)
    basis = (z0_ref, z1_ref)
    for c in range(2):
        z_faces(basis[c], lane, code, zface.at[c])
    for h in range(2):
        mu = [jnp.zeros((8, HALF), f32) for _ in range(3)]
        for i in range(8):
            rows = slice(64 * i, 64 * i + 64)
            small = slice(8 * i, 8 * i + 8)
            dens = dens_ref[rows, lanes(h)]
            kk = aux_ref[5, h, rows]
            xs_ref[0, h, small] = over_j(dens * vxz_ref[0, rows, lanes(h)])
            zsum[0, h, small] = over_j(dens * vxz_ref[1, rows, lanes(h)])
            col_ref[0, h, small] = over_j(dens)
            q = [basis[c][h, rows] for c in range(2)]
            dn = xq0_ref[0, h] if i == 0 else z0_ref[h, 64 * i - 64 : 64 * i]
            up = xq0_ref[1, h] if i == 7 else z0_ref[h, 64 * i + 64 : 64 * i + 128]
            xs_ref[1, h, small] = over_j(kk * (dn - up))
            for c in range(2):
                zdn, zup = zturns(q[c], zface[c, 0, h, small], zface[c, 1, h, small])
                zsum[c + 1, h, small] = over_j(kk * (zdn - zup))
            dia = dia_ref[h, rows]
            d0, d1 = dia * q[0], dia * q[1]
            mu[0] = mu[0] + over_j(d0 * q[0])
            mu[1] = mu[1] + over_j(d0 * q[1])
            mu[2] = mu[2] + over_j(d1 * q[1])
        for n in range(3):
            mom_ref[h, n] = mu[n]
    scale = RAY * 0.5 * ADVECT
    yq = (yq0_ref, yq1_ref)
    for h in range(2):
        for n, j, inner in ((0, 0, 1), (1, 7, 6)):
            dens = face_y(lambda r, m: dens_ref[r : r + m, lanes(h)], j)
            kk = face_y(lambda r, m: aux_ref[5, h, r : r + m], j)
            fy[n, 0, h] = dens * face_y(lambda r, m: vy_ref[r : r + m, lanes(h)], j)
            for c in range(2):
                near = face_y(lambda r, m: basis[c][h, r : r + m], inner)
                out = yq[c][n, h]
                fy[n, c + 1, h] = kk * ((out - near) if n == 0 else (near - out))
    for c in range(3):
        for h in range(2):
            change = z_change(zsum, c, h, lane, code) + (fy[1, c, h] - fy[0, c, h])
            for n in range(2):
                value = pick(fy[1 - n, c, 0], fy[1 - n, c, 1], lane[2 + n][h], code[2 + n][h], 0.0)
                change = change + value if n == 1 else change - value
            if c == 0:
                col_ref[c, h] = RAY * col_ref[c, h] - scale * change
            else:
                col_ref[c, h] = -scale * change


def z_change(zsum, c, h, lane, code):
    zf = []
    for f, k in ((4, 7), (5, 0)):
        tabs = [zsum[c, g, pl.ds(k, 8, stride=8), :] for g in range(2)]
        zf.append(pick(tabs[0], tabs[1], lane[f][h], code[f][h], 0.0))
    down, up = turns(zsum[c, h].reshape(8, 8, HALF), zf[0], zf[1])
    return (up - down).reshape(64, HALF)


def column_kernel(
    z1_ref, z2_ref, dia_ref, aux_ref, xsum_ref, xq1_ref, xq2_ref, xcol_ref, part_ref, xs_ref, idx_ref,
    col_ref, mom_ref, ynear_ref,
    zface, zsum, xsum,
):
    lane, code = tables(idx_ref)
    for f, j in ((2, 7), (3, 0)):
        tabs = [face_y(lambda r, n: z2_ref[h, r : r + n], j) for h in range(2)]
        for h in range(2):
            ynear_ref[f - 2, h] = pick(tabs[0], tabs[1], lane[f][h], code[f][h], 0.0)
    z_faces(z2_ref, lane, code, zface)
    for h in range(2):
        mu = [jnp.zeros((8, HALF), f32) for _ in range(3)]
        for i in range(8):
            rows = slice(64 * i, 64 * i + 64)
            small = slice(8 * i, 8 * i + 8)
            kk = aux_ref[5, h, rows]
            dn = xq1_ref[0, h] if i == 0 else z1_ref[h, 64 * i - 64 : 64 * i]
            up = xq1_ref[1, h] if i == 7 else z1_ref[h, 64 * i + 64 : 64 * i + 128]
            xsum[0, h, small] = over_j(kk * (dn - up))
            q = z2_ref[h, rows]
            dn, up, total = x_terms(z2_ref, aux_ref, xsum_ref, xq2_ref, h, i)
            xsum[1, h, small] = over_j(kk * (dn - up))
            dn, up = zturns(q, zface[0, h, small], zface[1, h, small])
            zsum[0, h, small] = over_j(kk * (dn - up))
            total = total + (aux_ref[3, h, rows] * dn + aux_ref[4, h, rows] * up)
            dn, up = ends(q, ynear_ref[0, h, small], ynear_ref[1, h, small])
            total = total + (aux_ref[1, h, rows] * dn + aux_ref[2, h, rows] * up)
            d2 = dia_ref[h, rows] * q
            mu[0] = mu[0] + over_j(d2 * z1_ref[h, rows])
            mu[1] = mu[1] + over_j(d2 * q)
            mu[2] = mu[2] + over_j(0.5 * total * q)
        for n in range(3):
            mom_ref[h, n] = mu[n]
    scale = RAY * 0.5 * ADVECT
    for c in range(4):
        for h in range(2):
            sums = [xs_ref[c, g] if c < 2 else xsum[c - 2, g] for g in range(2)]
            faces = []
            for f, start in ((0, 56), (1, 0)):
                far = jnp.where(code[f][h] == 3, xcol_ref[f, h, 8 * c : 8 * c + 8], 0.0)
                faces.append(pick(sums[0][start : start + 8], sums[1][start : start + 8],
                                  lane[f][h], code[f][h], far))
            down, up = ends(sums[h], faces[0], faces[1])
            if c < 3:
                col_ref[c, h] = part_ref[c, h] - scale * (up - down)
            else:
                col_ref[c, h] = -scale * ((up - down) + z_change(zsum, 0, h, lane, code))


def y_kernel(
    tiles, z0_ref, z1_ref, z2_ref, aux_ref, ky_ref,
    col_ref, mom1_ref, mom_ref, ynear_ref, first_ref, second_ref, idx_ref, ids_ref,
    yq2_ref, send_ref, out_ref, fy,
):
    lane, code = tables(idx_ref)
    basis = (z0_ref, z1_ref, z2_ref)
    sides = both_sides(first_ref, second_ref, odd_on("grp"))
    extra = jnp.zeros((64, HALF), f32)
    for h in range(2):
        for n, j, inner in ((0, 0, 1), (1, 7, 6)):
            ln, cd = lane[2 + n][h], code[2 + n][h]
            far = jnp.where(cd == 3, pick_remote(sides[n][0:64], ln, 0), 0.0)
            out = ynear_ref[n, h] + far
            yq2_ref[n, h] = out
            z2 = face_y(lambda r, m: z2_ref[h, r : r + m], j)
            w_sum = 0.5 * face_y(lambda r, m: aux_ref[1 + n, h, r : r + m], j)
            extra = extra + w_sum * (far * z2)
            kk = face_y(lambda r, m: aux_ref[5, h, r : r + m], j)
            near = face_y(lambda r, m: z2_ref[h, r : r + m], inner)
            fy[n, h] = kk * ((out - near) if n == 0 else (near - out))
    scale = RAY * 0.5 * ADVECT
    for h in range(2):
        change = [None, None, None, fy[1, h] - fy[0, h]]
        for n, j in ((0, 0), (1, 7)):
            got = sides[n]
            ln, cd = lane[2 + n][h], code[2 + n][h]
            far = cd == 3
            k_m = ky_ref[n, h]
            for c in range(4):
                if c == 0:
                    other = pick_fold(got[128:160], ln)
                else:
                    at, second = ((64, 0), (64, 1), (0, 1))[c - 1]
                    inner = pick_remote(got[at : at + 64], ln, second)
                    mine = k_m * face_y(lambda r, m: basis[c - 1][h, r : r + m], j)
                    other = (mine - inner) if n == 1 else (inner - mine)
                value = jnp.where(far, other, 0.0)
                if c == 3:
                    value = pick(fy[1 - n, 0], fy[1 - n, 1], ln, cd, value)
                value = value if n == 1 else -value
                change[c] = value if change[c] is None else change[c] + value
        for c in range(4):
            out_ref[c, h] = col_ref[c, h] - scale * change[c]
    parts = [m[0, n] + m[1, n] for m in (mom1_ref, mom_ref) for n in range(3)]
    parts[5] = parts[5] + over_j(extra)
    which = iota((1, HALF), 1)
    row = jnp.zeros((1, HALF), f32)
    for n, m in enumerate(parts):
        total = jnp.sum(jnp.sum(m, axis=0, keepdims=True), axis=1, keepdims=True)
        row = jnp.where(which == n, total, row)
    g_count = send_ref.shape[0] // tiles
    for t in range(tiles):
        names = pltpu.roll(ids_ref[t : t + 1, :], SLOTS, 1)
        line = jnp.where(which < SLOTS, row, names)
        for g in range(g_count):
            send_ref[t * g_count + g] = line


def pairwise(terms):
    while len(terms) > 1:
        odd = terms[len(terms) // 2 * 2 :]
        terms = [a + b for a, b in zip(terms[0::2], terms[1::2])] + odd
    return terms[0]


def coefficients(mu):
    def dot(a, b):
        return pairwise([x * y * mu[i + j] for i, x in enumerate(a) for j, y in enumerate(b)])

    one = jnp.ones_like(mu[0])
    residual = [one]
    direction = [one]
    energy = mu[0]
    pressure = [None, None, None]
    for iteration in range(3):
        image = [direction[0]]
        for n in range(1, len(direction)):
            image.append(direction[n] - direction[n - 1])
        image.append(-direction[-1])
        step = energy / dot(direction, image)
        for n, d in enumerate(direction):
            pressure[n] = step * d if pressure[n] is None else pressure[n] + step * d
        if iteration < 2:
            old = residual + [None]
            residual = []
            for n, im in enumerate(image):
                residual.append(-step * im if old[n] is None else old[n] - step * im)
            fresh = dot(residual, residual)
            beta = fresh / energy
            energy = fresh
            longer = direction + [None]
            direction = [
                r if d is None else r + beta * d for r, d in zip(residual, longer)
            ]
    return pressure


def pack_kernel(tiles, cap, fold, got_ref, col_ref, tidx_ref, send_ref, coef_ref):
    sources = got_ref.shape[0]
    total = pairwise([got_ref[s] for s in range(sources)])
    coef = coefficients([jnp.broadcast_to(total[:, n : n + 1], (1, HALF)) for n in range(6)])
    coef_ref[...] = jnp.concatenate(coef + [jnp.zeros((5, HALF), f32)], axis=0)
    full = []
    for h in range(2):
        value = col_ref[0, h]
        for n in range(3):
            value = value + coef[n] * col_ref[n + 1, h]
        full.append(value)
    g_count = sources // tiles
    height = 64 // g_count
    left = iota((1, HALF), 1) < cap
    for t in range(tiles):
        ln = tidx_ref[t : t + 1, :]
        cd = tidx_ref[tiles + t : tiles + t + 1, :]
        value = pick(full[0], full[1], ln, cd, 0.0)
        for g in range(g_count):
            part = value[g * height : g * height + height]
            if fold == 2:
                part = jnp.where(left, part[0:8], part[8:16])
            send_ref[t * g_count + g] = part


def final_kernel(
    fold, got_ref, names_ref, coef_ref, vxz_ref, vy_ref, w_ref, z0_ref, z1_ref, z2_ref,
    xq0_ref, xq1_ref, xq2_ref, yq0_ref, yq1_ref, yq2_ref, idx_ref,
    vout_any, image_ref, vout, p, sems,
):
    coef = [coef_ref[n : n + 1, :] for n in range(3)]
    lane, code = tables(idx_ref)

    def pressure(i):
        rows = slice(64 * i, 64 * i + 64)
        for h in range(2):
            p[h, rows] = (
                coef[0] * z0_ref[h, rows] + coef[1] * z1_ref[h, rows] + coef[2] * z2_ref[h, rows])

    def blend(refs, n, h, at):
        return coef[0] * refs[0][n, h, at] + coef[1] * refs[1][n, h, at] + coef[2] * refs[2][n, h, at]

    sources, height = got_ref.shape[0], 8 * fold
    left = iota((1, HALF), 1) < HALF // 2
    blocks_id = iota((BLOCKS, 2 * HALF), 0).astype(f32).astype(bf16)
    one, zero = jnp.ones((), bf16), jnp.zeros((), bf16)

    def chunk_image(chunk):
        pieces, names = [], []
        for s in range(chunk, chunk + 2 * fold, fold):
            value = got_ref[s]
            after_ids = names_ref[s + 1] if fold == 2 else -1.0
            names.append(jnp.where(left, pltpu.roll(names_ref[s], HALF // 2, 1), after_ids))
            if fold == 2:
                after = got_ref[s + 1]
                value = jnp.concatenate(
                    [jnp.where(left, value, pltpu.roll(after, HALF // 2, 1)),
                     jnp.where(left, pltpu.roll(value, HALF // 2, 1), after)], axis=0)
            high = value.astype(bf16)
            rest = value - high.astype(f32)
            middle = rest.astype(bf16)
            low = (rest - middle.astype(f32)).astype(bf16)
            pieces.append(jnp.concatenate([high, middle, low], axis=0))
        ids = jnp.broadcast_to(jnp.concatenate(names, axis=1), (16, 2 * HALF)).astype(bf16)
        ids = jnp.concatenate([ids] * (BLOCKS // 16), axis=0)
        hot = jnp.where(blocks_id == ids, one, zero)
        product = lax.dot_general(
            jnp.concatenate(pieces, axis=1), hot, (((1,), (1,)), ((), ())),
            preferred_element_type=f32)
        return product[0:height] + (
            product[height : 2 * height] + product[2 * height : 3 * height])

    optical = jnp.zeros((height, BLOCKS), f32)
    chunks = list(range(0, sources, 2 * fold))
    turn = -(-len(chunks) // 16)
    xq, yq = (xq0_ref, xq1_ref, xq2_ref), (yq0_ref, yq1_ref, yq2_ref)
    copies = []
    pressure(0)
    for i in range(8):
        if i < 7:
            pressure(i + 1)
        rows = slice(64 * i, 64 * i + 64)
        small = slice(8 * i, 8 * i + 8)
        tabs = [[p[h, pl.ds(64 * i + k, 8, stride=8), :] for h in range(2)] for k in (7, 0)]
        for h in range(2):
            w = 0.5 * w_ref[rows, lanes(h)]
            mine = p[h, rows]
            dn = blend(xq, 0, h, slice(0, 64)) if i == 0 else p[h, 64 * i - 64 : 64 * i]
            up = blend(xq, 1, h, slice(0, 64)) if i == 7 else p[h, 64 * i + 64 : 64 * i + 128]
            vout[0, rows, lanes(h)] = vxz_ref[0, rows, lanes(h)] - w * (up - dn)
            dn, up = ends(mine, blend(yq, 0, h, small), blend(yq, 1, h, small))
            vout[1, rows, lanes(h)] = vy_ref[rows, lanes(h)] - w * (up - dn)
            zf = [pick(tabs[n][0], tabs[n][1], lane[4 + n][h], code[4 + n][h], 0.0) for n in range(2)]
            dn, up = zturns(mine, zf[0], zf[1])
            vout[2, rows, lanes(h)] = vxz_ref[1, rows, lanes(h)] - w * (up - dn)
        copies.append(pltpu.make_async_copy(vout.at[:, rows], vout_any.at[:, rows], sems.at[i]))
        copies[i].start()
        if len(chunks) > 8 or i % 2 == 0:
            for chunk in chunks[:turn]:
                optical = optical + chunk_image(chunk)
            chunks = chunks[turn:]

    for chunk in chunks:
        optical = optical + chunk_image(chunk)

    shade = 1.0 - jnp.exp(-optical)
    for m in range(height):
        image_ref[0:1, m * BLOCKS : (m + 1) * BLOCKS] = shade[m : m + 1, :]
    for c in copies:
        c.wait()


def call(kernel, outs, scratch, args, any_args=0, limit=10, final=False, alias=None):
    spaces = [pltpu.HBM if n < any_args else pltpu.VMEM for n in range(len(args))]
    out_specs = [pl.BlockSpec(memory_space=pltpu.VMEM) for _ in outs]
    if final:
        out_specs[0] = pl.BlockSpec(memory_space=pltpu.HBM)
    return pl.pallas_call(
        kernel,
        out_shape=[jax.ShapeDtypeStruct(s, d) if final else pltpu.VMEM(s, d) for s, d in outs],
        in_specs=[pl.BlockSpec(memory_space=space) for space in spaces],
        out_specs=out_specs,
        scratch_shapes=scratch,
        input_output_aliases=alias or {},
        compiler_params=pltpu.CompilerParams(vmem_limit_bytes=limit * 1024 * 1024),
    )(*[pltpu.with_memory_space_constraint(a, space) for a, space in zip(args, spaces)])


def swap(packed, axis):
    count = lax.axis_size(axis)
    results = []
    for start in range(2):
        pairs = [(i, i + 1) for i in range(start, count - 1, 2)]
        results.append(lax.ppermute(packed[start], axis, pairs + [(b, a) for a, b in pairs]))
    return results


def shards(
    velocity, density, inverse_density, neighbours, leaf_layer, leaf_tile, leaf_block, samples
):
    count = density.shape[1]
    tiles = samples.shape[0]
    grp_size, dev_size = lax.axis_size("grp"), lax.axis_size("dev")
    cap = 2 * count // tiles
    height = 64 // grp_size
    fold = min(height // 8, HALF // cap)
    sources = grp_size * dev_size
    everyone = ("dev", "grp")

    field = ((2, 512, HALF), f32)
    sides = ((2, 2, 64, HALF), f32)

    def vm(*shape):
        return pltpu.VMEM(shape, f32)

    vy, inv, nb, send = call(
        functools.partial(load_kernel, dev_size),
        [((512, count), f32), ((512, count), f32), ((6, count), i32), ((2, 64, HALF), f32)],
        [pltpu.SemaphoreType.DMA((3,))],
        (velocity, inverse_density, neighbours),
        any_args=3,
    )
    first, second = swap(send, "grp")
    vxz, dens, idx, cidx, small, limits = call(
        functools.partial(index_kernel, dev_size),
        [((2, 512, count), f32), ((512, count), f32), ((16, count), i32), ((8, HALF), i32),
         ((8, count), i32), ((1, tiles), i32)],
        [pltpu.SemaphoreType.DMA((7,))],
        (velocity, density, leaf_layer.reshape(1, count), leaf_tile.reshape(1, count),
         leaf_block.reshape(1, count), samples.reshape(1, tiles), nb),
        any_args=6,
    )
    esrc, edia, send = call(
        edge_kernel,
        [sides, sides, ((2, 2, 64, HALF), f32)],
        [vm(2, 2, HALF, HALF)],
        (vxz, vy, inv, first, second, idx, cidx),
    )
    got_first, got_second = swap(send, "dev")
    psrc, pdia, aux, xface = call(
        inner_kernel,
        [field, field, ((6, 2, 512, HALF), f32), sides],
        [vm(2, 2, 512, HALF), vm(4, 2, 64, HALF), vm(4, 2, 64, HALF)],
        (vxz, vy, inv, dens, first, second, idx, cidx),
    )
    tidx, ids = call(
        functools.partial(tile_kernel, cap, fold),
        [((2 * tiles, HALF), i32), ((tiles, HALF), f32)],
        [],
        (small, limits, esrc),
    )
    dia, z0, rdia, xsum, xq0, xhr, send = call(
        first_kernel,
        [field, field, field, sides, sides, sides, ((2, 128, HALF), f32)],
        [],
        (vxz, inv, psrc, pdia, esrc, edia, aux, xface, got_first, got_second, idx, cidx, ids),
        alias={3: 0},
    )
    first, second = swap(send, "grp")
    (pz1,) = call(
        first_rest_kernel,
        [field],
        [vm(2, 2, 64, HALF), vm(2, 2, 64, HALF)],
        (z0, aux, xsum, rdia, xq0, idx),
    )
    z1, yq0, yq1, ky, send = call(
        second_kernel,
        [field, sides, sides, sides, ((2, 112, HALF), f32)],
        [vm(2, 512, HALF), vm(2, 2, 64, HALF), vm(2, 2, 64, HALF)],
        (vxz, dens, z0, pz1, rdia, aux, xsum, first, second, idx, cidx),
        alias={3: 0},
    )
    first, second = swap(send, "dev")
    (pz2,) = call(
        second_rest_kernel,
        [field],
        [vm(2, 2, 64, HALF), vm(2, 2, 64, HALF)],
        (z1, aux, xsum, rdia, yq1, idx),
    )
    col1, xs, mom1 = call(
        column_first_kernel,
        [((3, 2, 64, HALF), f32), ((2, 2, 64, HALF), f32), ((2, 3, 8, HALF), f32)],
        [vm(2, 2, 2, 64, HALF), vm(3, 2, 64, HALF), vm(2, 3, 2, 64, HALF)],
        (vxz, vy, dens, z0, z1, dia, aux, xq0, yq0, yq1, idx),
    )
    z2, xq1, xq2, xcol, send = call(
        third_kernel,
        [field, sides, sides, ((2, 2, 32, HALF), f32), ((2, 160, HALF), f32)],
        [],
        (vy, dens, z0, z1, pz2, rdia, aux, xsum, xhr, first, second, idx, cidx, mom1),
        alias={4: 0},
    )
    first, second = swap(send, "grp")
    col, mom, ynear = call(
        column_kernel,
        [((4, 2, 64, HALF), f32), ((2, 3, 8, HALF), f32), sides],
        [vm(2, 2, 64, HALF), vm(1, 2, 64, HALF), vm(2, 2, 64, HALF)],
        (z1, z2, dia, aux, xsum, xq1, xq2, xcol, col1, xs, idx),
    )
    yq2, send, col = call(
        functools.partial(y_kernel, tiles),
        [sides, ((sources, 1, HALF), f32), ((4, 2, 64, HALF), f32)],
        [vm(2, 2, 64, HALF)],
        (z0, z1, z2, aux, ky, col, mom1, mom, ynear, first, second, idx, ids),
    )
    moments = lax.all_to_all(send, everyone, 0, 0, tiled=True)
    send, coef = call(
        functools.partial(pack_kernel, tiles, cap, fold),
        [((sources, 8, HALF), f32), ((8, HALF), f32)],
        [],
        (moments, col, tidx),
    )
    got = lax.all_to_all(send, everyone, 0, 0, tiled=True)
    vout, image = call(
        functools.partial(final_kernel, fold),
        [((3, 512, count), f32), ((1, height * BLOCKS), f32)],
        [vm(3, 512, count), vm(2, 512, HALF), pltpu.SemaphoreType.DMA((8,))],
        (got, moments, coef, vxz, vy, inv, z0, z1, z2, xq0, xq1, xq2, yq0, yq1, yq2, idx),
        final=True,
    )
    return vout, image


def solution(mesh):
    return jax.shard_map(
        shards,
        mesh=mesh,
        in_specs=(
            P(None, None, ("grp", "dev")),
            P(None, ("grp", "dev")),
            P(None, ("grp", "dev")),
            P(None, ("grp", "dev")),
            P(("grp", "dev")),
            P(("grp", "dev"), None),
            P(("grp", "dev")),
            P(),
        ),
        out_specs=(P(None, None, ("grp", "dev")), P("dev", "grp")),
        check_vma=False,
    )
```

```python
import functools

import jax
import jax.numpy as jnp
from jax import lax
from jax.experimental import pallas as pl
from jax.experimental.pallas import tpu as pltpu
from jax.sharding import PartitionSpec as P

BLOCKS = 256
HALF = 128
SLOTS = 64
ADVECT = 0.2
RAY = 0.03

f32 = jnp.float32
bf16 = jnp.bfloat16
i32 = jnp.int32


def iota(shape, axis):
    return lax.broadcasted_iota(i32, shape, axis)


def take(table, lane):
    index = jnp.broadcast_to(lane, table.shape)
    return jnp.take_along_axis(table, index, axis=1, mode="promise_in_bounds")


def pick(low, high, lane, code, other):
    near = jnp.where(code == 1, take(low, lane), take(high, lane))
    return jnp.where((code == 1) | (code == 2), near, other)


def pick_remote(packed, lane, second):
    return take(packed, lane + second * SLOTS)


def packed_pair(first, second, lane, code):
    ga = jnp.where(code == 2, take(first[1], lane), take(first[0], lane))
    gb = jnp.where(code == 2, take(second[1], lane), take(second[0], lane))
    left = iota((1, HALF), 1) < SLOTS
    return jnp.where(left, ga, gb)


def packed_fold(parts, lane, code):
    half = parts[0].shape[0] // 2
    return packed_pair([p[:half] for p in parts], [p[half:] for p in parts], lane, code)


def pick_fold(packed, lane):
    return jnp.concatenate([take(packed, lane), take(packed, lane + SLOTS)], axis=0)


def ends(slab, low, high):
    down = jnp.concatenate([low, slab[:-8]], axis=0)
    up = jnp.concatenate([slab[8:], high], axis=0)
    return down, up


def turns(slab, low, high):
    n = slab.shape[0]
    row = iota((1, 8, 1), 1)
    down = jnp.where(row == 0, low.reshape(n, 1, HALF), pltpu.roll(slab, 1, 1))
    up = jnp.where(row == 7, high.reshape(n, 1, HALF), pltpu.roll(slab, 7, 1))
    return down, up


def zturns(slab, low, high):
    down, up = turns(slab.reshape(8, 8, HALF), low, high)
    return down.reshape(64, HALF), up.reshape(64, HALF)


def face_y(read, j):
    return jnp.concatenate([read(64 * i + 8 * j, 8) for i in range(8)], axis=0)


def odd_on(axis):
    return lax.axis_index(axis) & 1


def slot_of(n, odd):
    return (n + 1 + odd) & 1


def both_sides(first_ref, second_ref, odd):
    first, second = first_ref[...], second_ref[...]
    is_odd = jnp.broadcast_to(odd, first.shape) == 1
    return jnp.where(is_odd, first, second), jnp.where(is_odd, second, first)


def lanes(h):
    return slice(h * HALF, (h + 1) * HALF)


def link_lists(nb, dirs, dev_size):
    count = nb.shape[1]
    me = lax.axis_index("grp") * dev_size + lax.axis_index("dev")
    base = nb - me * count
    present = nb >= 0
    local = present & (base >= 0) & (base < count)
    remote = present & jnp.logical_not(local)
    slot = nb & (count - 1)
    code = jnp.where(local, jnp.where(slot < HALF, 1, 2), jnp.where(remote, 3, 0))
    rem = remote[0:4].astype(f32)
    key = jnp.where(remote[0:4], slot[0:4], 2 * count).astype(f32)
    cols = jnp.concatenate([rem, key], axis=0).T
    tri = (iota((count, count), 1) <= iota((count, count), 0)).astype(bf16)
    upto = jnp.dot(tri, cols.astype(bf16), preferred_element_type=f32)
    target = (iota((1, HALF), 1) & (SLOTS - 1)).astype(f32)
    lists = []
    for f in dirs:
        listed = (upto[:, f : f + 1] <= target).astype(f32)
        lists.append(jnp.sum(listed, axis=0, keepdims=True).astype(i32))
    listing = jnp.concatenate(lists, axis=0)
    clane = listing & (HALF - 1)
    ccode = jnp.where(listing < HALF, 1, jnp.where(listing < count, 2, 0))
    return code, slot, remote, key, cols, clane, ccode


def load_kernel(
    dev_size, v_any, w_any, nb_any, vy_ref, w_ref, nb_ref, send_ref, sems,
):
    copies = [
        pltpu.make_async_copy(nb_any, nb_ref, sems.at[0]),
    ]
    for n in range(4):
        part = slice(128 * n, 128 * n + 128)
        copies.append(pltpu.make_async_copy(v_any.at[1, part], vy_ref.at[part], sems.at[1 + n]))
        copies.append(pltpu.make_async_copy(w_any.at[part], w_ref.at[part], sems.at[5 + n]))
    for c in copies:
        c.start()
    copies[0].wait()
    clane, ccode = link_lists(nb_ref[...], (2, 3), dev_size)[-2:]
    for c in copies[1:]:
        c.wait()
    for n, j in ((0, 0), (1, 7)):
        send_ref[slot_of(n, odd_on("grp"))] = packed_pair(
            [face_y(lambda r, m: vy_ref[r : r + m, lanes(h)], j) for h in range(2)],
            [face_y(lambda r, m: w_ref[r : r + m, lanes(h)], j) for h in range(2)],
            clane[n : n + 1], ccode[n : n + 1])


def index_kernel(
    dev_size, v_any, dens_any, layer_any, tile_any, block_any, samples_any, nb_ref,
    vxz_ref, dens_ref, idx_ref, cidx_ref, small_ref, samples_ref, sems,
):
    copies = [
        pltpu.make_async_copy(layer_any, small_ref.at[0:1], sems.at[3]),
        pltpu.make_async_copy(tile_any, small_ref.at[1:2], sems.at[4]),
        pltpu.make_async_copy(block_any, small_ref.at[2:3], sems.at[5]),
        pltpu.make_async_copy(samples_any, samples_ref, sems.at[6]),
        pltpu.make_async_copy(v_any.at[0], vxz_ref.at[0], sems.at[0]),
        pltpu.make_async_copy(v_any.at[2], vxz_ref.at[1], sems.at[1]),
        pltpu.make_async_copy(dens_any, dens_ref, sems.at[2]),
    ]
    for c in copies:
        c.start()
    count = nb_ref.shape[1]
    code, slot, remote, key, cols, clane, ccode = link_lists(nb_ref[...], range(4), dev_size)
    lane = slot & (HALF - 1)
    ranks = []
    for f in range(4):
        below = (cols[:, 4 + f : 5 + f] < key[f : f + 1, :]).astype(f32)
        ranks.append(jnp.sum(below, axis=0, keepdims=True).astype(i32))
    rank = jnp.concatenate(ranks, axis=0)
    lane4 = jnp.where(remote[0:4], rank & (SLOTS - 1), lane[0:4])
    zero2 = jnp.zeros((2, count), i32)
    idx_ref[0:8, :] = jnp.concatenate([lane4, lane[4:6], zero2], axis=0)
    idx_ref[8:16, :] = jnp.concatenate([code, zero2], axis=0)
    cidx_ref[...] = jnp.concatenate([clane, ccode], axis=0)
    for c in copies:
        c.wait()


def tile_kernel(cap, reps, small, samples_ref, after_ref, tidx_ref, ids_ref):
    count = small.shape[1]
    tiles = samples_ref.shape[1]
    rows = jnp.concatenate([small[0:1], small[1:2], small[2:3], jnp.zeros((5, count), i32)], axis=0)
    rows = rows.astype(f32)
    cols = rows.T
    tile = cols[:, 1:2]
    hot = tile == iota((count, tiles), 1).astype(f32)
    limit = jnp.sum(jnp.where(hot, samples_ref[...].astype(f32), 0.0), axis=1, keepdims=True)
    marched = cols[:, 0:1] < limit
    hot = hot & marched
    tri = (iota((count, count), 1) <= iota((count, count), 0)).astype(bf16)
    upto = jnp.dot(tri, hot.astype(bf16), preferred_element_type=f32)
    rank = jnp.sum(jnp.where(hot, upto, 0.0), axis=1, keepdims=True) - 1.0
    place = jnp.where(marched, tile * cap + rank, -1.0)
    place = jnp.broadcast_to(place, (count, HALF))
    lane_id = iota((1, HALF), 1)
    used = lane_id < cap * reps
    slot = (lane_id & (cap - 1)).astype(f32)
    listed = jnp.concatenate(
        [(place == jnp.where(used, slot + float(t * cap), -2.0)).astype(bf16)
         for t in range(tiles)], axis=1)
    leaf = iota((1, count), 1).astype(f32)
    table = jnp.concatenate([leaf, rows[2:3], jnp.ones((1, count), f32),
                             jnp.zeros((13, count), f32)], axis=0).astype(bf16)
    found = jnp.dot(table, listed, preferred_element_type=f32)
    for t in range(tiles):
        at = slice(t * HALF, (t + 1) * HALF)
        there = found[2:3, at] > 0.5
        listing = found[0:1, at].astype(i32)
        tidx_ref[t : t + 1, :] = listing & (HALF - 1)
        tidx_ref[tiles + t : tiles + t + 1, :] = jnp.where(
            there, jnp.where(listing < HALF, 1, 2), 0)
        ids_ref[t : t + 1, :] = jnp.where(there, found[1:2, at], -1.0)


def tables(idx_ref):
    lane = [[idx_ref[f : f + 1, lanes(h)] for h in range(2)] for f in range(6)]
    code = [[idx_ref[8 + f : 9 + f, lanes(h)] for h in range(2)] for f in range(6)]
    return lane, code


def edge_kernel(
    vxz_ref, vy_ref, w_ref, first_ref, second_ref, idx_ref, cidx_ref,
    src_ref, dia_ref, send_ref, zs,
):
    lane, code = tables(idx_ref)
    sides = both_sides(first_ref, second_ref, odd_on("grp"))
    for h in range(2):
        for n, start in ((0, 0), (1, 448)):
            rows = slice(start, start + 64)
            zs[0, h, 64 * n : 64 * n + 64] = vxz_ref[1, rows, lanes(h)]
            zs[1, h, 64 * n : 64 * n + 64] = w_ref[rows, lanes(h)]
    for n, start, inner, far_side in ((0, 0, 64, 448), (1, 448, 384, 0)):
        rows = slice(start, start + 64)
        small = slice(start // 8, start // 8 + 8)

        def tabs(read):
            return [read(h) for h in range(2)]

        for h in range(2):
            def face(f, v_tab, w_tab, w_own):
                ln, cd = lane[f][h], code[f][h]
                v_far, w_far = 0.0, jnp.where(cd == 3, 0.0, w_own)
                if f in (2, 3):
                    got = sides[f - 2][small]
                    v_far = jnp.where(cd == 3, pick_remote(got, ln, 0), 0.0)
                    w_far = jnp.where(cd == 3, pick_remote(got, ln, 1), w_own)
                return (pick(v_tab[0], v_tab[1], ln, cd, v_far),
                        pick(w_tab[0], w_tab[1], ln, cd, w_far))

            w = w_ref[rows, lanes(h)]
            far = slice(far_side, far_side + 64)
            next_rows = slice(inner, inner + 64)
            vx, wx = face(n, tabs(lambda g: vxz_ref[0, far, lanes(g)]),
                          tabs(lambda g: w_ref[far, lanes(g)]), w)
            sign = 1.0 if n == 0 else -1.0
            src = sign * (vxz_ref[0, next_rows, lanes(h)] - vx)
            dia = wx + w_ref[next_rows, lanes(h)]
            faces = []
            for f, j in ((2, 7), (3, 0)):
                at = slice(start + 8 * j, start + 8 * j + 8)
                mine = start + 56 - 8 * j
                faces.append(face(f, tabs(lambda g: vy_ref[ at, lanes(g)]),
                                  tabs(lambda g: w_ref[at, lanes(g)]),
                                  w_ref[mine : mine + 8, lanes(h)]))
            v_dn, v_up = ends(vy_ref[ rows, lanes(h)], faces[0][0], faces[1][0])
            w_dn, w_up = ends(w, faces[0][1], faces[1][1])
            src = src + (v_up - v_dn)
            dia = dia + (w_up + w_dn)
            faces = []
            for f, k in ((4, 7), (5, 0)):
                faces.append(face(f, tabs(lambda g: zs[0, g, pl.ds(64 * n + k, 8, stride=8), :]),
                                  tabs(lambda g: zs[1, g, pl.ds(64 * n + k, 8, stride=8), :]),
                                  zs[1, h, pl.ds(64 * n + 7 - k, 8, stride=8), :]))
            v_dn, v_up = zturns(vxz_ref[1, rows, lanes(h)], faces[0][0], faces[1][0])
            w_dn, w_up = zturns(w, faces[0][1], faces[1][1])
            src_ref[n, h] = -0.5 * (src + (v_up - v_dn))
            dia_ref[n, h] = 3.0 * w + 0.5 * (dia + (w_up + w_dn))
        cl, cc = cidx_ref[n : n + 1, :], cidx_ref[4 + n : 5 + n, :]
        slot = slot_of(n, odd_on("dev"))
        send_ref[slot, 0] = packed_pair(
            [vxz_ref[0, rows, lanes(h)] for h in range(2)],
            [w_ref[rows, lanes(h)] for h in range(2)], cl, cc)
        send_ref[slot, 1] = packed_pair(
            [src_ref[n, h] for h in range(2)], [dia_ref[n, h] for h in range(2)], cl, cc)


def inner_kernel(
    vxz_ref, vy_ref, w_ref, dens_ref, first_ref, second_ref, idx_ref, cidx_ref,
    psrc_ref, pdia_ref, aux_ref, xface_ref, zs, vface, face,
):
    lane, code = tables(idx_ref)
    sides = both_sides(first_ref, second_ref, odd_on("grp"))
    for h in range(2):
        zs[0, h] = vxz_ref[1, :, lanes(h)]
        zs[1, h] = w_ref[:, lanes(h)]
    v_tab, w_tab, w_own = {}, {}, {}
    for h in range(2):
        for f, start in ((0, 448), (1, 0)):
            w_tab[f, h] = w_ref[start : start + 64, lanes(h)]
            w_own[1 - f, h] = w_tab[f, h]
        for f, j in ((2, 7), (3, 0)):
            v_tab[f, h] = face_y(lambda r, n: vy_ref[ r : r + n, lanes(h)], j)
            w_tab[f, h] = face_y(lambda r, n: w_ref[r : r + n, lanes(h)], j)
            w_own[5 - f, h] = w_tab[f, h]
        for f, k in ((4, 7), (5, 0)):
            v_tab[f, h] = zs[0, h, pl.ds(k, 64, stride=8), :]
            w_tab[f, h] = zs[1, h, pl.ds(k, 64, stride=8), :]
            w_own[9 - f, h] = w_tab[f, h]
    for f in range(6):
        for h in range(2):
            ln, cd = lane[f][h], code[f][h]
            w_far = jnp.where(cd == 3, 0.0, w_own[f, h])
            v_far = 0.0
            if f in (2, 3):
                got = sides[f - 2]
                v_far = jnp.where(cd == 3, pick_remote(got, ln, 0), 0.0)
                w_far = jnp.where(cd == 3, pick_remote(got, ln, 1), w_own[f, h])
            w_face = pick(w_tab[f, 0], w_tab[f, 1], ln, cd, w_far)
            if f < 2:
                xface_ref[f, h] = w_face
            else:
                face[f - 2, h] = w_face
                vface[f - 2, h] = pick(v_tab[f, 0], v_tab[f, 1], ln, cd, v_far)
    for h in range(2):
        for i in range(8):
            rows = slice(64 * i, 64 * i + 64)
            small = slice(8 * i, 8 * i + 8)
            w = w_ref[rows, lanes(h)]
            wy_dn, wy_up = ends(w, face[0, h, small], face[1, h, small])
            wz_dn, wz_up = zturns(w, face[2, h, small], face[3, h, small])
            aux_ref[1, h, rows] = w + wy_dn
            aux_ref[2, h, rows] = w + wy_up
            aux_ref[3, h, rows] = w + wz_dn
            aux_ref[4, h, rows] = w + wz_up
            aux_ref[5, h, rows] = 0.5 * dens_ref[rows, lanes(h)] * w
            if i < 7:
                aux_ref[0, h, rows] = w + w_ref[64 * i + 64 : 64 * i + 128, lanes(h)]
            if i in (0, 7):
                continue
            below, above = slice(64 * i - 64, 64 * i), slice(64 * i + 64, 64 * i + 128)
            vy_dn, vy_up = ends(vy_ref[ rows, lanes(h)], vface[0, h, small], vface[1, h, small])
            vz_dn, vz_up = zturns(vxz_ref[1, rows, lanes(h)], vface[2, h, small], vface[3, h, small])
            vx = vxz_ref[0, above, lanes(h)] - vxz_ref[0, below, lanes(h)]
            psrc_ref[h, rows] = -0.5 * (vx + (vy_up - vy_dn) + (vz_up - vz_dn))
            wx = w_ref[above, lanes(h)] + w_ref[below, lanes(h)]
            pdia_ref[h, rows] = 3.0 * w + 0.5 * (wx + (wy_up + wy_dn) + (wz_up + wz_dn))


def z_faces(q_ref, lane, code, zface, layers=()):
    for i in layers:
        for f, k in ((4, 7), (5, 0)):
            tabs = [q_ref[h, pl.ds(64 * i + k, 8, stride=8), :] for h in range(2)]
            for h in range(2):
                zface[f - 4, h, 8 * i : 8 * i + 8] = pick(
                    tabs[0], tabs[1], lane[f][h], code[f][h], 0.0)
    if layers:
        return
    for f, k in ((4, 7), (5, 0)):
        tabs = [q_ref[h, pl.ds(k, 64, stride=8), :] for h in range(2)]
        for h in range(2):
            zface[f - 4, h] = pick(tabs[0], tabs[1], lane[f][h], code[f][h], 0.0)


def x_terms(q_ref, aux_ref, xsum_ref, xface, h, i):
    if i == 0:
        dn, c_dn = xface[0, h], xsum_ref[0, h]
    else:
        below = slice(64 * i - 64, 64 * i)
        dn, c_dn = q_ref[h, below], aux_ref[0, h, below]
    if i == 7:
        up, c_up = xface[1, h], xsum_ref[1, h]
    else:
        up, c_up = q_ref[h, 64 * i + 64 : 64 * i + 128], aux_ref[0, h, 64 * i : 64 * i + 64]
    return dn, up, c_dn * dn + c_up * up


def products(q_ref, aux_ref, xsum_ref, rdia_ref, xface, yface, zface, out_ref, layers=range(8)):
    for h in range(2):
        for i in layers:
            rows = slice(64 * i, 64 * i + 64)
            small = slice(8 * i, 8 * i + 8)
            q = q_ref[h, rows]
            total = x_terms(q_ref, aux_ref, xsum_ref, xface, h, i)[2]
            dn, up = ends(q, yface[0, h, small], yface[1, h, small])
            total = total + (aux_ref[1, h, rows] * dn + aux_ref[2, h, rows] * up)
            dn, up = zturns(q, zface[0, h, small], zface[1, h, small])
            total = total + (aux_ref[3, h, rows] * dn + aux_ref[4, h, rows] * up)
            out_ref[h, rows] = (0.5 * rdia_ref[h, rows]) * total


def first_kernel(
    vxz_ref, w_ref, psrc_ref, pdia_ref, esrc_ref, edia_ref, aux_ref, xface_ref,
    first_ref, second_ref, idx_ref, cidx_ref, after_ref,
    dia_ref, z0_ref, rdia_ref, xsum_ref, xq_ref, xhr_ref, send_ref,
):
    lane, code = tables(idx_ref)
    sides = both_sides(first_ref, second_ref, odd_on("dev"))
    for h in range(2):
        for i in range(1, 7):
            rows = slice(64 * i, 64 * i + 64)
            rdia = 1.0 / dia_ref[h, rows]
            rdia_ref[h, rows] = rdia
            z0_ref[h, rows] = psrc_ref[h, rows] * rdia
        for f, start, sign in ((0, 0, 0.5), (1, 448, -0.5)):
            rows = slice(start, start + 64)
            got = sides[f]
            ln, cd = lane[f][h], code[f][h]
            far = cd == 3
            v_m = jnp.where(far, pick_remote(got[0], ln, 0), 0.0)
            w_m = jnp.where(far, pick_remote(got[0], ln, 1), 0.0)
            src_m = jnp.where(far, pick_remote(got[1], ln, 0), 0.0)
            dia_m = jnp.where(far, pick_remote(got[1], ln, 1), 1.0)
            w = w_ref[rows, lanes(h)]
            dia = edia_ref[f, h] + 0.5 * w_m
            rdia = 1.0 / dia
            dia_ref[h, rows] = dia
            rdia_ref[h, rows] = rdia
            z0_ref[h, rows] = (esrc_ref[f, h] + sign * v_m) * rdia
            rdia_m = 1.0 / (dia_m + 0.5 * w)
            z0_m = (src_m - sign * vxz_ref[0, rows, lanes(h)]) * rdia_m
            xhr_ref[f, h] = rdia_m
            xq_ref[f, h] = jnp.where(far, z0_m, 0.0)
            xsum_ref[f, h] = w + jnp.where(far, w_m, xface_ref[f, h])
    for f, start in ((0, 448), (1, 0)):
        tabs = [z0_ref[h, start : start + 64] for h in range(2)]
        for h in range(2):
            xq_ref[f, h] = pick(tabs[0], tabs[1], lane[f][h], code[f][h], xq_ref[f, h])
    z1f = {}
    for n, f, j, there, inner in ((0, 2, 0, 7, 1), (1, 3, 7, 0, 6)):
        tabs = [face_y(lambda r, m: z0_ref[h, r : r + m], there) for h in range(2)]
        at = slice(8 * j, 8 * j + 8)
        for h in range(2):
            q = face_y(lambda r, m: z0_ref[h, r : r + m], j)
            c = face_y(lambda r, m: aux_ref[0, h, r : r + m], j)[:56]
            c_dn = jnp.concatenate([xsum_ref[0, h, at], c], axis=0)
            c_up = jnp.concatenate([c, xsum_ref[1, h, at]], axis=0)
            dn, up = ends(q, xq_ref[0, h, at], xq_ref[1, h, at])
            total = c_dn * dn + c_up * up
            near = pick(tabs[0], tabs[1], lane[f][h], code[f][h], 0.0)
            next_q = face_y(lambda r, m: z0_ref[h, r : r + m], inner)
            c_near = face_y(lambda r, m: aux_ref[1 + n, h, r : r + m], j)
            c_next = face_y(lambda r, m: aux_ref[2 - n, h, r : r + m], j)
            total = total + (c_near * near + c_next * next_q)
            zf = []
            for g, k in ((4, 7), (5, 0)):
                rows = [z0_ref[e, pl.ds(8 * j + k, 8, stride=64), :] for e in range(2)]
                zf.append(pick(rows[0], rows[1], lane[g][h], code[g][h], 0.0))
            dn, up = zturns(q, zf[0], zf[1])
            c_dn = face_y(lambda r, m: aux_ref[3, h, r : r + m], j)
            c_up = face_y(lambda r, m: aux_ref[4, h, r : r + m], j)
            total = total + (c_dn * dn + c_up * up)
            z1f[n, h] = (0.5 * face_y(lambda r, m: rdia_ref[h, r : r + m], j)) * total
    for n, j in ((0, 0), (1, 7)):
        cl, cc = cidx_ref[2 + n : 3 + n, :], cidx_ref[6 + n : 7 + n, :]
        z0f = [face_y(lambda r, m: z0_ref[h, r : r + m], j) for h in range(2)]
        rdf = [face_y(lambda r, m: rdia_ref[h, r : r + m], j) for h in range(2)]
        slot = slot_of(n, odd_on("grp"))
        kf = [face_y(lambda r, m: aux_ref[5, h, r : r + m], j) for h in range(2)]
        send_ref[slot, 0:64] = packed_pair(z0f, [z1f[n, 0], z1f[n, 1]], cl, cc)
        send_ref[slot, 64:96] = packed_fold(rdf, cl, cc)
        send_ref[slot, 96:128] = packed_fold(kf, cl, cc)


def first_rest_kernel(
    z0_ref, aux_ref, xsum_ref, rdia_ref, xq_ref, idx_ref, pz1_ref, yface, zface,
):
    lane, code = tables(idx_ref)
    for f, j in ((2, 7), (3, 0)):
        tabs = [face_y(lambda r, n: z0_ref[h, r : r + n], j) for h in range(2)]
        for h in range(2):
            yface[f - 2, h] = pick(tabs[0], tabs[1], lane[f][h], code[f][h], 0.0)
    z_faces(z0_ref, lane, code, zface)
    products(z0_ref, aux_ref, xsum_ref, rdia_ref, xq_ref, yface, zface, pz1_ref)


def second_kernel(
    vxz_ref, dens_ref, z0_ref, pz1_ref, rdia_ref, aux_ref, xsum_ref,
    first_ref, second_ref, idx_ref, cidx_ref,
    z1_ref, yq0_ref, yq1_ref, ky_ref, send_ref, pz2_ref, xface, zface,
):
    lane, code = tables(idx_ref)
    sides = both_sides(first_ref, second_ref, odd_on("grp"))
    for h in range(2):
        for f, j in ((2, 0), (3, 7)):
            got = sides[f - 2]
            ln, cd = lane[f][h], code[f][h]
            far = cd == 3
            z0_m = jnp.where(far, pick_remote(got[0:64], ln, 0), 0.0)
            z1_m = pick_remote(got[0:64], ln, 1)
            rd_m = pick_fold(got[64:96], ln)
            ky_ref[f - 2, h] = pick_fold(got[96:128], ln)
            yq0_ref[f - 2, h] = z0_m
            w_sum = 0.5 * face_y(lambda r, n: aux_ref[f - 1, h, r : r + n], j)
            z0_l = face_y(lambda r, n: z0_ref[h, r : r + n], j)
            rd_l = face_y(lambda r, n: rdia_ref[h, r : r + n], j)
            yq1_ref[f - 2, h] = jnp.where(far, z1_m + rd_m * w_sum * z0_l, 0.0)
            extra = rd_l * w_sum * z0_m
            for i in range(8):
                rows = slice(64 * i + 8 * j, 64 * i + 8 * j + 8)
                z1_ref[h, rows] = z1_ref[h, rows] + extra[8 * i : 8 * i + 8]
    for f, start in ((0, 448), (1, 0)):
        tabs = [z1_ref[h, start : start + 64] for h in range(2)]
        for h in range(2):
            xface[f, h] = pick(tabs[0], tabs[1], lane[f][h], code[f][h], 0.0)
    for f, j in ((2, 7), (3, 0)):
        for q_ref, out in ((z0_ref, yq0_ref), (z1_ref, yq1_ref)):
            tabs = [face_y(lambda r, n: q_ref[h, r : r + n], j) for h in range(2)]
            for h in range(2):
                out[f - 2, h] = pick(tabs[0], tabs[1], lane[f][h], code[f][h], out[f - 2, h])
    layers = (0, 1, 6, 7)
    z_faces(z1_ref, lane, code, zface, layers)
    products(z1_ref, aux_ref, xsum_ref, rdia_ref, xface, yq1_ref, zface, pz2_ref, layers)
    for n, start, inner in ((0, 0, 64), (1, 448, 384)):
        cl, cc = cidx_ref[n : n + 1, :], cidx_ref[4 + n : 5 + n, :]
        rows, next_rows = slice(start, start + 64), slice(inner, inner + 64)
        z1f = [z1_ref[h, rows] for h in range(2)]
        z2f = [pz2_ref[h, rows] for h in range(2)]
        kf, sums = [], []
        for h in range(2):
            k = aux_ref[5, h, rows]
            parts = [k * q[h, next_rows] for q in (z0_ref, z1_ref, pz2_ref)]
            parts.append(dens_ref[rows, lanes(h)] * vxz_ref[0, rows, lanes(h)])
            summed = [over_j(p) for p in parts]
            kf.append(k)
            sums.append(jnp.concatenate(summed, axis=0))
        slot = slot_of(n, odd_on("dev"))
        send_ref[slot, 0:64] = packed_pair(z1f, z2f, cl, cc)
        send_ref[slot, 64:96] = packed_fold(kf, cl, cc)
        send_ref[slot, 96:112] = packed_fold(sums, cl, cc)


def second_rest_kernel(
    z1_ref, aux_ref, xsum_ref, rdia_ref, yq1_ref, idx_ref, pz2_ref, xface, zface,
):
    lane, code = tables(idx_ref)
    for f, start in ((0, 448), (1, 0)):
        tabs = [z1_ref[h, start : start + 64] for h in range(2)]
        for h in range(2):
            xface[f, h] = pick(tabs[0], tabs[1], lane[f][h], code[f][h], 0.0)
    z_faces(z1_ref, lane, code, zface)
    products(z1_ref, aux_ref, xsum_ref, rdia_ref, xface, yq1_ref, zface, pz2_ref)


def third_kernel(
    vy_ref, dens_ref, z0_ref, z1_ref, pz2_ref, rdia_ref, aux_ref, xsum_ref, xhr_ref,
    first_ref, second_ref, idx_ref, cidx_ref, after_ref,
    z2_ref, xq1_ref, xq2_ref, xcol_ref, send_ref,
):
    lane, code = tables(idx_ref)
    sides = both_sides(first_ref, second_ref, odd_on("dev"))
    for h in range(2):
        for f, start in ((0, 0), (1, 448)):
            rows = slice(start, start + 64)
            got = sides[f]
            ln, cd = lane[f][h], code[f][h]
            far = cd == 3
            z1_m = jnp.where(far, pick_remote(got[0:64], ln, 0), 0.0)
            z2_m = pick_remote(got[0:64], ln, 1)
            k_m = pick_fold(got[64:96], ln)
            sums = pick_fold(got[96:112], ln)
            w_sum = 0.5 * xsum_ref[f, h]
            xq1_ref[f, h] = z1_m
            xq2_ref[f, h] = jnp.where(far, z2_m + xhr_ref[f, h] * w_sum * z1_ref[h, rows], 0.0)
            z2_l = z2_ref[h, rows] + rdia_ref[h, rows] * w_sum * z1_m
            z2_ref[h, rows] = z2_l
            sign = 1.0 if f == 0 else -1.0
            for c, q in enumerate((z0_ref[h, rows], z1_ref[h, rows], z2_l)):
                mine = over_j(k_m * q)
                xcol_ref[f, h, 8 * c + 8 : 8 * c + 16] = sign * (sums[8 * c : 8 * c + 8] - mine)
            xcol_ref[f, h, 0:8] = sums[24:32]
    for f, start in ((0, 448), (1, 0)):
        for q_ref, out in ((z1_ref, xq1_ref), (z2_ref, xq2_ref)):
            tabs = [q_ref[h, start : start + 64] for h in range(2)]
            for h in range(2):
                out[f, h] = pick(tabs[0], tabs[1], lane[f][h], code[f][h], out[f, h])
    for n, j, inner in ((0, 0, 1), (1, 7, 6)):
        cl, cc = cidx_ref[2 + n : 3 + n, :], cidx_ref[6 + n : 7 + n, :]
        kf, vf = [], []
        for h in range(2):
            dens = face_y(lambda r, m: dens_ref[r : r + m, lanes(h)], j)
            kf.append(face_y(lambda r, m: aux_ref[5, h, r : r + m], j))
            vf.append(dens * face_y(lambda r, m: vy_ref[ r : r + m, lanes(h)], j))
        z2f = [face_y(lambda r, m: z2_ref[h, r : r + m], j) for h in range(2)]
        inners = [
            [kf[h] * face_y(lambda r, m: q[h, r : r + m], inner) for h in range(2)]
            for q in (z0_ref, z1_ref, z2_ref)
        ]
        slot = slot_of(n, odd_on("grp"))
        send_ref[slot, 0:64] = packed_pair(z2f, inners[2], cl, cc)
        send_ref[slot, 64:128] = packed_pair(inners[0], inners[1], cl, cc)
        send_ref[slot, 128:160] = packed_fold(vf, cl, cc)


def over_j(a):
    return jnp.sum(a.reshape(8, 8, HALF), axis=0)


def column_first_kernel(
    vxz_ref, vy_ref, dens_ref, z0_ref, z1_ref, dia_ref, aux_ref, xq0_ref, yq0_ref, yq1_ref, idx_ref,
    col_ref, xs_ref, mom_ref,
    zface, zsum, fy,
):
    lane, code = tables(idx_ref)
    basis = (z0_ref, z1_ref)
    for c in range(2):
        z_faces(basis[c], lane, code, zface.at[c])
    for h in range(2):
        mu = [jnp.zeros((8, HALF), f32) for _ in range(3)]
        for i in range(8):
            rows = slice(64 * i, 64 * i + 64)
            small = slice(8 * i, 8 * i + 8)
            dens = dens_ref[rows, lanes(h)]
            kk = aux_ref[5, h, rows]
            xs_ref[0, h, small] = over_j(dens * vxz_ref[0, rows, lanes(h)])
            zsum[0, h, small] = over_j(dens * vxz_ref[1, rows, lanes(h)])
            col_ref[0, h, small] = over_j(dens)
            q = [basis[c][h, rows] for c in range(2)]
            dn = xq0_ref[0, h] if i == 0 else z0_ref[h, 64 * i - 64 : 64 * i]
            up = xq0_ref[1, h] if i == 7 else z0_ref[h, 64 * i + 64 : 64 * i + 128]
            xs_ref[1, h, small] = over_j(kk * (dn - up))
            for c in range(2):
                zdn, zup = zturns(q[c], zface[c, 0, h, small], zface[c, 1, h, small])
                zsum[c + 1, h, small] = over_j(kk * (zdn - zup))
            dia = dia_ref[h, rows]
            d0, d1 = dia * q[0], dia * q[1]
            mu[0] = mu[0] + over_j(d0 * q[0])
            mu[1] = mu[1] + over_j(d0 * q[1])
            mu[2] = mu[2] + over_j(d1 * q[1])
        for n in range(3):
            mom_ref[h, n] = mu[n]
    scale = RAY * 0.5 * ADVECT
    yq = (yq0_ref, yq1_ref)
    for h in range(2):
        for n, j, inner in ((0, 0, 1), (1, 7, 6)):
            dens = face_y(lambda r, m: dens_ref[r : r + m, lanes(h)], j)
            kk = face_y(lambda r, m: aux_ref[5, h, r : r + m], j)
            fy[n, 0, h] = dens * face_y(lambda r, m: vy_ref[r : r + m, lanes(h)], j)
            for c in range(2):
                near = face_y(lambda r, m: basis[c][h, r : r + m], inner)
                out = yq[c][n, h]
                fy[n, c + 1, h] = kk * ((out - near) if n == 0 else (near - out))
    for c in range(3):
        for h in range(2):
            change = z_change(zsum, c, h, lane, code) + (fy[1, c, h] - fy[0, c, h])
            for n in range(2):
                value = pick(fy[1 - n, c, 0], fy[1 - n, c, 1], lane[2 + n][h], code[2 + n][h], 0.0)
                change = change + value if n == 1 else change - value
            if c == 0:
                col_ref[c, h] = RAY * col_ref[c, h] - scale * change
            else:
                col_ref[c, h] = -scale * change


def z_change(zsum, c, h, lane, code):
    zf = []
    for f, k in ((4, 7), (5, 0)):
        tabs = [zsum[c, g, pl.ds(k, 8, stride=8), :] for g in range(2)]
        zf.append(pick(tabs[0], tabs[1], lane[f][h], code[f][h], 0.0))
    down, up = turns(zsum[c, h].reshape(8, 8, HALF), zf[0], zf[1])
    return (up - down).reshape(64, HALF)


def column_kernel(
    z1_ref, z2_ref, dia_ref, aux_ref, xsum_ref, xq1_ref, xq2_ref, xcol_ref, part_ref, xs_ref, idx_ref,
    col_ref, mom_ref, ynear_ref,
    zface, zsum, xsum,
):
    lane, code = tables(idx_ref)
    for f, j in ((2, 7), (3, 0)):
        tabs = [face_y(lambda r, n: z2_ref[h, r : r + n], j) for h in range(2)]
        for h in range(2):
            ynear_ref[f - 2, h] = pick(tabs[0], tabs[1], lane[f][h], code[f][h], 0.0)
    z_faces(z2_ref, lane, code, zface)
    for h in range(2):
        mu = [jnp.zeros((8, HALF), f32) for _ in range(3)]
        for i in range(8):
            rows = slice(64 * i, 64 * i + 64)
            small = slice(8 * i, 8 * i + 8)
            kk = aux_ref[5, h, rows]
            dn = xq1_ref[0, h] if i == 0 else z1_ref[h, 64 * i - 64 : 64 * i]
            up = xq1_ref[1, h] if i == 7 else z1_ref[h, 64 * i + 64 : 64 * i + 128]
            xsum[0, h, small] = over_j(kk * (dn - up))
            q = z2_ref[h, rows]
            dn, up, total = x_terms(z2_ref, aux_ref, xsum_ref, xq2_ref, h, i)
            xsum[1, h, small] = over_j(kk * (dn - up))
            dn, up = zturns(q, zface[0, h, small], zface[1, h, small])
            zsum[0, h, small] = over_j(kk * (dn - up))
            total = total + (aux_ref[3, h, rows] * dn + aux_ref[4, h, rows] * up)
            dn, up = ends(q, ynear_ref[0, h, small], ynear_ref[1, h, small])
            total = total + (aux_ref[1, h, rows] * dn + aux_ref[2, h, rows] * up)
            d2 = dia_ref[h, rows] * q
            mu[0] = mu[0] + over_j(d2 * z1_ref[h, rows])
            mu[1] = mu[1] + over_j(d2 * q)
            mu[2] = mu[2] + over_j(0.5 * total * q)
        for n in range(3):
            mom_ref[h, n] = mu[n]
    scale = RAY * 0.5 * ADVECT
    for c in range(4):
        for h in range(2):
            sums = [xs_ref[c, g] if c < 2 else xsum[c - 2, g] for g in range(2)]
            faces = []
            for f, start in ((0, 56), (1, 0)):
                far = jnp.where(code[f][h] == 3, xcol_ref[f, h, 8 * c : 8 * c + 8], 0.0)
                faces.append(pick(sums[0][start : start + 8], sums[1][start : start + 8],
                                  lane[f][h], code[f][h], far))
            down, up = ends(sums[h], faces[0], faces[1])
            if c < 3:
                col_ref[c, h] = part_ref[c, h] - scale * (up - down)
            else:
                col_ref[c, h] = -scale * ((up - down) + z_change(zsum, 0, h, lane, code))


def y_kernel(
    tiles, z0_ref, z1_ref, z2_ref, aux_ref, ky_ref,
    col_ref, mom1_ref, mom_ref, ynear_ref, first_ref, second_ref, idx_ref, ids_ref,
    yq2_ref, send_ref, out_ref, fy,
):
    lane, code = tables(idx_ref)
    basis = (z0_ref, z1_ref, z2_ref)
    sides = both_sides(first_ref, second_ref, odd_on("grp"))
    extra = jnp.zeros((64, HALF), f32)
    for h in range(2):
        for n, j, inner in ((0, 0, 1), (1, 7, 6)):
            ln, cd = lane[2 + n][h], code[2 + n][h]
            far = jnp.where(cd == 3, pick_remote(sides[n][0:64], ln, 0), 0.0)
            out = ynear_ref[n, h] + far
            yq2_ref[n, h] = out
            z2 = face_y(lambda r, m: z2_ref[h, r : r + m], j)
            w_sum = 0.5 * face_y(lambda r, m: aux_ref[1 + n, h, r : r + m], j)
            extra = extra + w_sum * (far * z2)
            kk = face_y(lambda r, m: aux_ref[5, h, r : r + m], j)
            near = face_y(lambda r, m: z2_ref[h, r : r + m], inner)
            fy[n, h] = kk * ((out - near) if n == 0 else (near - out))
    scale = RAY * 0.5 * ADVECT
    for h in range(2):
        change = [None, None, None, fy[1, h] - fy[0, h]]
        for n, j in ((0, 0), (1, 7)):
            got = sides[n]
            ln, cd = lane[2 + n][h], code[2 + n][h]
            far = cd == 3
            k_m = ky_ref[n, h]
            for c in range(4):
                if c == 0:
                    other = pick_fold(got[128:160], ln)
                else:
                    at, second = ((64, 0), (64, 1), (0, 1))[c - 1]
                    inner = pick_remote(got[at : at + 64], ln, second)
                    mine = k_m * face_y(lambda r, m: basis[c - 1][h, r : r + m], j)
                    other = (mine - inner) if n == 1 else (inner - mine)
                value = jnp.where(far, other, 0.0)
                if c == 3:
                    value = pick(fy[1 - n, 0], fy[1 - n, 1], ln, cd, value)
                value = value if n == 1 else -value
                change[c] = value if change[c] is None else change[c] + value
        for c in range(4):
            out_ref[c, h] = col_ref[c, h] - scale * change[c]
    parts = [m[0, n] + m[1, n] for m in (mom1_ref, mom_ref) for n in range(3)]
    parts[5] = parts[5] + over_j(extra)
    which = iota((1, HALF), 1)
    row = jnp.zeros((1, HALF), f32)
    for n, m in enumerate(parts):
        total = jnp.sum(jnp.sum(m, axis=0, keepdims=True), axis=1, keepdims=True)
        row = jnp.where(which == n, total, row)
    g_count = send_ref.shape[0] // tiles
    for t in range(tiles):
        names = pltpu.roll(ids_ref[t : t + 1, :], SLOTS, 1)
        line = jnp.where(which < SLOTS, row, names)
        for g in range(g_count):
            send_ref[g * tiles + t] = line


def pairwise(terms):
    while len(terms) > 1:
        odd = terms[len(terms) // 2 * 2 :]
        terms = [a + b for a, b in zip(terms[0::2], terms[1::2])] + odd
    return terms[0]


def coefficients(mu):
    def dot(a, b):
        return pairwise([x * y * mu[i + j] for i, x in enumerate(a) for j, y in enumerate(b)])

    one = jnp.ones_like(mu[0])
    residual = [one]
    direction = [one]
    energy = mu[0]
    pressure = [None, None, None]
    for iteration in range(3):
        image = [direction[0]]
        for n in range(1, len(direction)):
            image.append(direction[n] - direction[n - 1])
        image.append(-direction[-1])
        step = energy / dot(direction, image)
        for n, d in enumerate(direction):
            pressure[n] = step * d if pressure[n] is None else pressure[n] + step * d
        if iteration < 2:
            old = residual + [None]
            residual = []
            for n, im in enumerate(image):
                residual.append(-step * im if old[n] is None else old[n] - step * im)
            fresh = dot(residual, residual)
            beta = fresh / energy
            energy = fresh
            longer = direction + [None]
            direction = [
                r if d is None else r + beta * d for r, d in zip(residual, longer)
            ]
    return pressure


def pack_kernel(tiles, cap, fold, got_ref, col_ref, tidx_ref, send_ref, coef_ref):
    sources = got_ref.shape[0]
    total = pairwise([got_ref[s] for s in range(sources)])
    coef = coefficients([jnp.broadcast_to(total[:, n : n + 1], (1, HALF)) for n in range(6)])
    coef_ref[...] = jnp.concatenate(coef + [jnp.zeros((5, HALF), f32)], axis=0)
    full = []
    for h in range(2):
        value = col_ref[0, h]
        for n in range(3):
            value = value + coef[n] * col_ref[n + 1, h]
        full.append(value)
    g_count = sources // tiles
    height = 64 // g_count
    left = iota((1, HALF), 1) < cap
    for t in range(tiles):
        ln = tidx_ref[t : t + 1, :]
        cd = tidx_ref[tiles + t : tiles + t + 1, :]
        value = pick(full[0], full[1], ln, cd, 0.0)
        for g in range(g_count):
            part = value[g * height : g * height + height]
            if fold == 2:
                part = jnp.where(left, part[0:8], part[8:16])
            send_ref[g * tiles + t] = part


def final_kernel(
    fold, got_ref, names_ref, coef_ref, vxz_ref, vy_ref, w_ref, z0_ref, z1_ref, z2_ref,
    xq0_ref, xq1_ref, xq2_ref, yq0_ref, yq1_ref, yq2_ref, idx_ref,
    vout_any, image_ref, vout, p, sems,
):
    coef = [coef_ref[n : n + 1, :] for n in range(3)]
    lane, code = tables(idx_ref)

    def pressure(i):
        rows = slice(64 * i, 64 * i + 64)
        for h in range(2):
            p[h, rows] = (
                coef[0] * z0_ref[h, rows] + coef[1] * z1_ref[h, rows] + coef[2] * z2_ref[h, rows])

    def blend(refs, n, h, at):
        return coef[0] * refs[0][n, h, at] + coef[1] * refs[1][n, h, at] + coef[2] * refs[2][n, h, at]

    sources, height = got_ref.shape[0], 8 * fold
    left = iota((1, HALF), 1) < HALF // 2
    blocks_id = iota((BLOCKS, 2 * HALF), 0).astype(f32).astype(bf16)
    one, zero = jnp.ones((), bf16), jnp.zeros((), bf16)

    def chunk_image(chunk):
        pieces, names = [], []
        for s in range(chunk, chunk + 2 * fold, fold):
            value = got_ref[s]
            after_ids = names_ref[s + 1] if fold == 2 else -1.0
            names.append(jnp.where(left, pltpu.roll(names_ref[s], HALF // 2, 1), after_ids))
            if fold == 2:
                after = got_ref[s + 1]
                value = jnp.concatenate(
                    [jnp.where(left, value, pltpu.roll(after, HALF // 2, 1)),
                     jnp.where(left, pltpu.roll(value, HALF // 2, 1), after)], axis=0)
            high = value.astype(bf16)
            rest = value - high.astype(f32)
            middle = rest.astype(bf16)
            low = (rest - middle.astype(f32)).astype(bf16)
            pieces.append(jnp.concatenate([high, middle, low], axis=0))
        ids = jnp.broadcast_to(jnp.concatenate(names, axis=1), (16, 2 * HALF)).astype(bf16)
        ids = jnp.concatenate([ids] * (BLOCKS // 16), axis=0)
        hot = jnp.where(blocks_id == ids, one, zero)
        product = lax.dot_general(
            jnp.concatenate(pieces, axis=1), hot, (((1,), (1,)), ((), ())),
            preferred_element_type=f32)
        return product[0:height] + (
            product[height : 2 * height] + product[2 * height : 3 * height])

    optical = jnp.zeros((height, BLOCKS), f32)
    chunks = list(range(0, sources, 2 * fold))
    turn = -(-len(chunks) // 16)
    xq, yq = (xq0_ref, xq1_ref, xq2_ref), (yq0_ref, yq1_ref, yq2_ref)
    copies = []
    pressure(0)
    for i in range(8):
        if i < 7:
            pressure(i + 1)
        rows = slice(64 * i, 64 * i + 64)
        small = slice(8 * i, 8 * i + 8)
        tabs = [[p[h, pl.ds(64 * i + k, 8, stride=8), :] for h in range(2)] for k in (7, 0)]
        for h in range(2):
            w = 0.5 * w_ref[rows, lanes(h)]
            mine = p[h, rows]
            dn = blend(xq, 0, h, slice(0, 64)) if i == 0 else p[h, 64 * i - 64 : 64 * i]
            up = blend(xq, 1, h, slice(0, 64)) if i == 7 else p[h, 64 * i + 64 : 64 * i + 128]
            vout[0, rows, lanes(h)] = vxz_ref[0, rows, lanes(h)] - w * (up - dn)
            dn, up = ends(mine, blend(yq, 0, h, small), blend(yq, 1, h, small))
            vout[1, rows, lanes(h)] = vy_ref[rows, lanes(h)] - w * (up - dn)
            zf = [pick(tabs[n][0], tabs[n][1], lane[4 + n][h], code[4 + n][h], 0.0) for n in range(2)]
            dn, up = zturns(mine, zf[0], zf[1])
            vout[2, rows, lanes(h)] = vxz_ref[1, rows, lanes(h)] - w * (up - dn)
        copies.append(pltpu.make_async_copy(vout.at[:, rows], vout_any.at[:, rows], sems.at[i]))
        copies[i].start()
        if len(chunks) > 8 or i % 2 == 0:
            for chunk in chunks[:turn]:
                optical = optical + chunk_image(chunk)
            chunks = chunks[turn:]

    for chunk in chunks:
        optical = optical + chunk_image(chunk)

    shade = 1.0 - jnp.exp(-optical)
    for m in range(height):
        image_ref[0:1, m * BLOCKS : (m + 1) * BLOCKS] = shade[m : m + 1, :]
    for c in copies:
        c.wait()


def call(kernel, outs, scratch, args, any_args=0, limit=10, final=False, alias=None):
    spaces = [pltpu.HBM if n < any_args else pltpu.VMEM for n in range(len(args))]
    out_specs = [pl.BlockSpec(memory_space=pltpu.VMEM) for _ in outs]
    if final:
        out_specs[0] = pl.BlockSpec(memory_space=pltpu.HBM)
    return pl.pallas_call(
        kernel,
        out_shape=[jax.ShapeDtypeStruct(s, d) if final else pltpu.VMEM(s, d) for s, d in outs],
        in_specs=[pl.BlockSpec(memory_space=space) for space in spaces],
        out_specs=out_specs,
        scratch_shapes=scratch,
        input_output_aliases=alias or {},
        compiler_params=pltpu.CompilerParams(vmem_limit_bytes=limit * 1024 * 1024),
    )(*[pltpu.with_memory_space_constraint(a, space) for a, space in zip(args, spaces)])


def swap(packed, axis):
    count = lax.axis_size(axis)
    results = []
    for start in range(2):
        pairs = [(i, i + 1) for i in range(start, count - 1, 2)]
        results.append(lax.ppermute(packed[start], axis, pairs + [(b, a) for a, b in pairs]))
    return results


def shards(
    velocity, density, inverse_density, neighbours, leaf_layer, leaf_tile, leaf_block, samples
):
    count = density.shape[1]
    tiles = samples.shape[0]
    grp_size, dev_size = lax.axis_size("grp"), lax.axis_size("dev")
    cap = 2 * count // tiles
    height = 64 // grp_size
    fold = min(height // 8, HALF // cap)
    sources = grp_size * dev_size
    everyone = ("grp", "dev")

    field = ((2, 512, HALF), f32)
    sides = ((2, 2, 64, HALF), f32)

    def vm(*shape):
        return pltpu.VMEM(shape, f32)

    vy, inv, nb, send = call(
        functools.partial(load_kernel, dev_size),
        [((512, count), f32), ((512, count), f32), ((6, count), i32), ((2, 64, HALF), f32)],
        [pltpu.SemaphoreType.DMA((9,))],
        (velocity, inverse_density, neighbours),
        any_args=3,
    )
    first, second = swap(send, "grp")
    vxz, dens, idx, cidx, small, limits = call(
        functools.partial(index_kernel, dev_size),
        [((2, 512, count), f32), ((512, count), f32), ((16, count), i32), ((8, HALF), i32),
         ((8, count), i32), ((1, tiles), i32)],
        [pltpu.SemaphoreType.DMA((7,))],
        (velocity, density, leaf_layer.reshape(1, count), leaf_tile.reshape(1, count),
         leaf_block.reshape(1, count), samples.reshape(1, tiles), nb),
        any_args=6,
    )
    esrc, edia, send = call(
        edge_kernel,
        [sides, sides, ((2, 2, 64, HALF), f32)],
        [vm(2, 2, HALF, HALF)],
        (vxz, vy, inv, first, second, idx, cidx),
    )
    got_first, got_second = swap(send, "dev")
    psrc, pdia, aux, xface = call(
        inner_kernel,
        [field, field, ((6, 2, 512, HALF), f32), sides],
        [vm(2, 2, 512, HALF), vm(4, 2, 64, HALF), vm(4, 2, 64, HALF)],
        (vxz, vy, inv, dens, first, second, idx, cidx),
    )
    tidx, ids = call(
        functools.partial(tile_kernel, cap, fold),
        [((2 * tiles, HALF), i32), ((tiles, HALF), f32)],
        [],
        (small, limits, esrc),
    )
    dia, z0, rdia, xsum, xq0, xhr, send = call(
        first_kernel,
        [field, field, field, sides, sides, sides, ((2, 128, HALF), f32)],
        [],
        (vxz, inv, psrc, pdia, esrc, edia, aux, xface, got_first, got_second, idx, cidx, ids),
        alias={3: 0},
    )
    first, second = swap(send, "grp")
    (pz1,) = call(
        first_rest_kernel,
        [field],
        [vm(2, 2, 64, HALF), vm(2, 2, 64, HALF)],
        (z0, aux, xsum, rdia, xq0, idx),
    )
    z1, yq0, yq1, ky, send = call(
        second_kernel,
        [field, sides, sides, sides, ((2, 112, HALF), f32)],
        [vm(2, 512, HALF), vm(2, 2, 64, HALF), vm(2, 2, 64, HALF)],
        (vxz, dens, z0, pz1, rdia, aux, xsum, first, second, idx, cidx),
        alias={3: 0},
    )
    first, second = swap(send, "dev")
    (pz2,) = call(
        second_rest_kernel,
        [field],
        [vm(2, 2, 64, HALF), vm(2, 2, 64, HALF)],
        (z1, aux, xsum, rdia, yq1, idx),
    )
    col1, xs, mom1 = call(
        column_first_kernel,
        [((3, 2, 64, HALF), f32), ((2, 2, 64, HALF), f32), ((2, 3, 8, HALF), f32)],
        [vm(2, 2, 2, 64, HALF), vm(3, 2, 64, HALF), vm(2, 3, 2, 64, HALF)],
        (vxz, vy, dens, z0, z1, dia, aux, xq0, yq0, yq1, idx),
    )
    z2, xq1, xq2, xcol, send = call(
        third_kernel,
        [field, sides, sides, ((2, 2, 32, HALF), f32), ((2, 160, HALF), f32)],
        [],
        (vy, dens, z0, z1, pz2, rdia, aux, xsum, xhr, first, second, idx, cidx, mom1),
        alias={4: 0},
    )
    first, second = swap(send, "grp")
    col, mom, ynear = call(
        column_kernel,
        [((4, 2, 64, HALF), f32), ((2, 3, 8, HALF), f32), sides],
        [vm(2, 2, 64, HALF), vm(1, 2, 64, HALF), vm(2, 2, 64, HALF)],
        (z1, z2, dia, aux, xsum, xq1, xq2, xcol, col1, xs, idx),
    )
    yq2, send, col = call(
        functools.partial(y_kernel, tiles),
        [sides, ((sources, 1, HALF), f32), ((4, 2, 64, HALF), f32)],
        [vm(2, 2, 64, HALF)],
        (z0, z1, z2, aux, ky, col, mom1, mom, ynear, first, second, idx, ids),
    )
    moments = lax.all_to_all(send, everyone, 0, 0, tiled=True)
    send, coef = call(
        functools.partial(pack_kernel, tiles, cap, fold),
        [((sources, 8, HALF), f32), ((8, HALF), f32)],
        [],
        (moments, col, tidx),
    )
    got = lax.all_to_all(send, everyone, 0, 0, tiled=True)
    vout, image = call(
        functools.partial(final_kernel, fold),
        [((3, 512, count), f32), ((1, height * BLOCKS), f32)],
        [vm(3, 512, count), vm(2, 512, HALF), pltpu.SemaphoreType.DMA((8,))],
        (got, moments, coef, vxz, vy, inv, z0, z1, z2, xq0, xq1, xq2, yq0, yq1, yq2, idx),
        final=True,
    )
    return vout, image


def solution(mesh):
    return jax.shard_map(
        shards,
        mesh=mesh,
        in_specs=(
            P(None, None, ("grp", "dev")),
            P(None, ("grp", "dev")),
            P(None, ("grp", "dev")),
            P(None, ("grp", "dev")),
            P(("grp", "dev")),
            P(("grp", "dev"), None),
            P(("grp", "dev")),
            P(),
        ),
        out_specs=(P(None, None, ("grp", "dev")), P("dev", "grp")),
        check_vma=False,
    )
```
